128 devices in a mesh: gx: 16 (over z, y_hi, core), gy: 8 (over x, y_lo).
Axes of the slice: x: 4, y: 4 (y_hi: 2, y_lo: 2; y = y_hi * 2 + y_lo), z: 4, core: 2. Of those that a mesh axis runs over, the one named last changes fastest.
Arguments:
- obj_field: float32 [2, 2, 4096, 8192], P(None, None, 'gy', 'gx'), may hold values from -0.8 to 0.8
- probe_modes: float32 [2, 2, 256, 256], P(None, None, 'gx'), may hold values from -6 to 6
- positions: int32 [8, 16, 6, 2], P('gy', 'gx'), may hold values from 0 to 511
- counts: int32 [8, 16], P('gy', 'gx'), may hold values from 1 to 6, as said below
- amplitudes: float32 [8, 16, 6, 256, 256], P('gy', 'gx'), may hold values from 0.6 to 1.8
Outputs:
- obj_grad: float32 [2, 2, 4096, 8192], P(None, None, 'gy', 'gx')
- probe_grad: float32 [2, 2, 256, 256], P(None, None, 'gx')
The draws below stay inside these ranges and needn't reach their ends.
Inputs may be any that keep to these rules, and one draw needn't show every extreme that they name: `counts`: each tile has between 1 and 6 used slots and at least one tile uses all 6.
All inputs are finite; a program needn't handle non-finite values.
Results may differ from the reference program's by a relative error of at most 0.00014.
Values sent between devices are 32-bit elements; how exact they have to be, the bound alone decides.
No kernel may reach another device: no remote copies, remote signals or barrier semaphores. Data moves between devices by JAX's collectives and lax.ppermute only.
A program may use at most 128 MiB of HBM per device.

```python
import math
import jax
import jax.numpy as jnp
from jax import lax

PROBE = 256
MODES = 2
SLICES = 2
BAND = 48
TILE = 512
P_MAX = 6
NROWS = 4096
NCOLS = 8192
N_GX = 16
N_GY = 8


def draw_counts(key, part):
    key = jax.random.fold_in(key, 11)
    first_key, second_key, third_key = jax.random.split(key, 3)
    baseline = jax.random.randint(first_key, (N_GY, N_GX), 1, P_MAX // 2 + 1)
    crowded = jax.random.randint(second_key, (N_GY, N_GX), 0, 8) == 0
    chosen = jax.random.randint(third_key, (), 0, N_GY * N_GX)
    picked = jnp.arange(N_GY * N_GX).reshape(N_GY, N_GX) == chosen
    return jnp.where(crowded | picked, P_MAX, baseline).astype(jnp.int32)


def place_ends(array, key, least, high):
    shape = array.shape
    index_at = [jax.random.randint(jax.random.fold_in(key, axis), (), 0, shape[axis]) for axis in range(len(shape))]
    array = array.at[tuple(index_at)].set(least)
    longest = shape.index(max(shape))
    index_at[longest] = (index_at[longest] + 1) % shape[longest]
    return array.at[tuple(index_at)].set(high)


def steps_of(rng, extent, cuts, smallest, high):
    level = 1.0
    for position, shards_of in cuts:
        heights = jax.random.uniform(jax.random.fold_in(jax.random.fold_in(rng, 6), position), (shards_of,), jnp.float32, smallest / len(cuts), high / len(cuts))
        level = level * jnp.repeat(jnp.exp(heights), extent[position] // shards_of).reshape((-1,) + (1,) * (len(extent) - 1 - position))
    return level


def gaussian(rng, shape, width, most, cuts=(), kind=jnp.bfloat16):
    gain = steps_of(rng, shape, cuts, -0.22, 0.18) if cuts else 1.0
    entries = jax.random.normal(rng, shape, jnp.float32) * width * gain
    return jnp.minimum(jnp.maximum(entries, -most), most).astype(kind)


def setup_inputs(seed: int = 0) -> dict:
    splits = jax.random.split(jax.random.key(seed), 6)
    return {
        "obj_field": jnp.clip(jax.random.uniform(splits[0], (SLICES, 2, NROWS, NCOLS), jnp.float32, -0.8, 0.8) * steps_of(splits[0], (SLICES, 2, NROWS, NCOLS), ((2, 8), (3, 16)), -0.4, 0.0), -0.8, 0.8),
        "probe_modes": gaussian(splits[1], (MODES, 2, PROBE, PROBE), 1.0, 6.0, ((2, 16),), jnp.float32),
        "positions": place_ends(jax.random.randint(splits[2], (N_GY, N_GX, P_MAX, 2), 0, TILE), jax.random.fold_in(splits[2], 1), 0, TILE - 1).astype(jnp.int32),
        "counts": draw_counts(jax.random.fold_in(splits[5], 71), 0),
        "amplitudes": jnp.clip(0.6 + 1.1999999 * jax.random.uniform(splits[4], (N_GY, N_GX, P_MAX, PROBE, PROBE), jnp.float32) ** steps_of(splits[4], (N_GY, N_GX, P_MAX, PROBE, PROBE), ((0, 8), (1, 16)), -0.2, 0.2), 0.6, 1.8),
    }


def tables_for(probe_len, ftype):
    indices = jnp.arange(probe_len, dtype=jnp.int32)
    offsets = (indices[:, None] - indices[None, :]).astype(ftype)
    chirp = math.pi * offsets * offsets / (2.0 * BAND)
    inside = jnp.where(jnp.abs(offsets) <= BAND, 1.0, 0.0).astype(ftype) / math.sqrt(2.0 * BAND + 1.0)
    cycles = (indices[:, None] * indices[None, :] % probe_len).astype(ftype)
    angles = -2.0 * math.pi * cycles / probe_len
    scaling = 1.0 / math.sqrt(probe_len)
    return (jnp.cos(chirp) * inside, jnp.sin(chirp) * inside, jnp.cos(angles) * scaling, jnp.sin(angles) * scaling)

def left_apply(mat_re, mat_im, wave_re, wave_im):
    highest = lax.Precision.HIGHEST
    out_re = jnp.einsum('ab,mbc->mac', mat_re, wave_re, precision=highest) - jnp.einsum('ab,mbc->mac', mat_im, wave_im, precision=highest)
    out_im = jnp.einsum('ab,mbc->mac', mat_re, wave_im, precision=highest) + jnp.einsum('ab,mbc->mac', mat_im, wave_re, precision=highest)
    return (out_re, out_im)

def right_apply(mat_re, mat_im, wave_re, wave_im):
    highest = lax.Precision.HIGHEST
    out_re = jnp.einsum('mab,bc->mac', wave_re, mat_re, precision=highest) - jnp.einsum('mab,bc->mac', wave_im, mat_im, precision=highest)
    out_im = jnp.einsum('mab,bc->mac', wave_im, mat_re, precision=highest) + jnp.einsum('mab,bc->mac', wave_re, mat_im, precision=highest)
    return (out_re, out_im)

def position_loss(window, mode_set, amplitude, weight, tables):
    prop_re, prop_im, four_re, four_im = tables
    wave_re = mode_set[:, 0] * window[0, 0] - mode_set[:, 1] * window[0, 1]
    wave_im = mode_set[:, 0] * window[0, 1] + mode_set[:, 1] * window[0, 0]
    for slice_index in range(1, window.shape[0]):
        wave_re, wave_im = left_apply(prop_re, prop_im, wave_re, wave_im)
        wave_re, wave_im = right_apply(prop_re, prop_im, wave_re, wave_im)
        trans_re = window[slice_index, 0]
        trans_im = window[slice_index, 1]
        wave_re, wave_im = (wave_re * trans_re - wave_im * trans_im, wave_re * trans_im + wave_im * trans_re)
    far_re, far_im = left_apply(four_re, four_im, wave_re, wave_im)
    far_re, far_im = right_apply(four_re, four_im, far_re, far_im)
    intensity = lax.optimization_barrier(jnp.sum(far_re * far_re + far_im * far_im, axis=0))
    misfit = jnp.sqrt(intensity + 1.0) - amplitude
    return weight * jnp.sum(misfit * misfit)

def reference(obj_field, probe_modes, positions, counts, amplitudes):
    ftype = obj_field.dtype
    tables = tables_for(PROBE, ftype)
    padded = jnp.pad(obj_field, ((0, 0), (0, 0), (0, PROBE), (0, PROBE)))
    per_row = N_GX * P_MAX
    anchor = jnp.int32(0)

    def visit(number, running):
        grad_pad, grad_probe = running
        number = number.astype(jnp.int32)
        row_dev = number // per_row
        col_dev = number // P_MAX % N_GX
        slot_index = number % P_MAX
        row_at = (row_dev * TILE + positions[row_dev, col_dev, slot_index, 0]).astype(jnp.int32)
        col_at = (col_dev * TILE + positions[row_dev, col_dev, slot_index, 1]).astype(jnp.int32)
        weight = jnp.where(slot_index < counts[row_dev, col_dev], 1.0, 0.0).astype(ftype)
        starts = (anchor, anchor, row_at, col_at)
        window = lax.dynamic_slice(padded, starts, (SLICES, 2, PROBE, PROBE))
        window_grad, modes_grad = jax.grad(position_loss, argnums=(0, 1))(window, probe_modes, amplitudes[row_dev, col_dev, slot_index], weight, tables)
        current = lax.dynamic_slice(grad_pad, starts, (SLICES, 2, PROBE, PROBE))
        grad_pad = lax.dynamic_update_slice(grad_pad, current + window_grad, starts)
        return (grad_pad, grad_probe + modes_grad)
    grad_pad, grad_probe = lax.fori_loop(jnp.int32(0), jnp.int32(N_GY * N_GX * P_MAX), visit, (jnp.zeros_like(padded), jnp.zeros_like(probe_modes)))
    return (grad_pad[:, :, :N_GY * TILE, :N_GX * TILE], grad_probe)
```

```python
import functools
import math

import jax
import jax.numpy as jnp
import numpy as np
from jax import lax
from jax.experimental import pallas as pl
from jax.experimental.pallas import tpu as pltpu
from jax.sharding import PartitionSpec as P

BAND = 48
PROBE = 256
HALF = 128
TILE = 512
SLOTS = 6
F32 = jnp.float32
BF16 = jnp.bfloat16
VMEM_LIMIT = 48 * 1024 * 1024


def split_table(mat):
    hi = mat.astype(BF16)
    lo = (mat - hi.astype(np.float64)).astype(BF16)
    return hi, lo


def left_table(mat):
    hi, lo = split_table(mat)
    return np.concatenate([hi, lo, hi], axis=1)


def right_table(mat):
    hi, lo = split_table(mat)
    return np.concatenate([hi, lo, hi], axis=0)


def make_tables():
    index = np.arange(PROBE)
    offset = (index[:, None] - index[None, :]).astype(np.float64)
    prop = np.where(np.abs(offset) <= BAND, np.exp(1j * np.pi * offset**2 / (2 * BAND)), 0)
    prop = prop / math.sqrt(2 * BAND + 1)
    half = np.arange(HALF)
    four = np.exp(-2j * np.pi * ((half[:, None] * half[None, :]) % HALF) / HALF) / math.sqrt(PROBE)
    twist = np.exp(-2j * np.pi * half / PROBE)

    def from_left(mat):
        return np.block([[mat.real, -mat.imag], [mat.imag, mat.real]])

    def from_right(mat):
        return from_left(mat).T

    order = np.concatenate([np.arange(0, PROBE, 2), np.arange(1, PROBE, 2)])
    perm = np.zeros((PROBE, PROBE))
    perm[np.arange(PROBE), order] = 1
    return {
        "prop_l": left_table(from_left(prop)),
        "prop_r": right_table(from_right(prop)),
        "back_l": left_table(from_left(prop.conj())),
        "back_r": right_table(from_right(prop.conj())),
        "four_l": left_table(from_left(four)),
        "four_r": right_table(from_right(four)),
        "ruof_l": left_table(from_left(four.conj())),
        "ruof_r": right_table(from_right(four.conj())),
        "tw_row": np.stack(
            [
                np.broadcast_to(twist.real[:, None], (HALF, PROBE)),
                np.broadcast_to(twist.imag[:, None], (HALF, PROBE)),
            ]
        ).astype(np.float32),
        "tw_col": np.stack(
            [
                np.broadcast_to(twist.real[None, :], (8, HALF)),
                np.broadcast_to(twist.imag[None, :], (8, HALF)),
            ]
        ).astype(np.float32),
        "perm_l": np.concatenate([perm] * 3, axis=1).astype(BF16),
        "perm_r": np.concatenate([perm.T] * 3, axis=0).astype(BF16),
    }


def parted(x):
    hi = x.astype(BF16)
    return hi, (x - hi.astype(F32)).astype(BF16)


def lmul(table, x):
    hi, lo = parted(x)
    return jnp.dot(table, jnp.concatenate([hi, hi, lo], axis=0), preferred_element_type=F32)


def rmul(x, table):
    hi, lo = parted(x)
    return jnp.dot(jnp.concatenate([hi, hi, lo], axis=1), table, preferred_element_type=F32)


def exact_parts(x):
    hi = x.astype(BF16)
    rest = x - hi.astype(F32)
    mid = rest.astype(BF16)
    return hi, mid, (rest - mid.astype(F32)).astype(BF16)


def both_sides(re, im, table_l, table_r):
    x = jnp.concatenate(
        [jnp.concatenate(re, axis=1), jnp.concatenate(im, axis=1)], axis=0
    )
    y = lmul(table_l, x)
    n = PROBE
    x = jnp.concatenate(
        [jnp.concatenate([y[:n, m * n : (m + 1) * n], y[n:, m * n : (m + 1) * n]], axis=1) for m in (0, 1)],
        axis=0,
    )
    y = rmul(x, table_r)
    return [y[m * n : (m + 1) * n, :n] for m in (0, 1)], [y[m * n : (m + 1) * n, n:] for m in (0, 1)]


def place_of(scalars, slot):
    row = scalars[2 * slot]
    col = scalars[2 * slot + 1]
    row_base = pl.multiple_of(row // 8 * 8, 8)
    col_base = pl.multiple_of(col // 128 * 128, 128)
    return row_base, row - row_base, col_base, col - col_base


def window_of(field, part, place):
    row_base, row_off, col_base, col_off = place
    x = field[part, pl.ds(row_base, PROBE + 8), pl.ds(col_base, PROBE + 128)]
    x = pltpu.roll(x, (PROBE + 128 - col_off) % (PROBE + 128), 1)[:, :PROBE]
    return pltpu.roll(x, (PROBE + 8 - row_off) % (PROBE + 8), 0)[:PROBE]


def add_window(field, part, place, x):
    row_base, row_off, col_base, col_off = place
    x = jnp.concatenate([x, jnp.zeros((8, PROBE), F32)], axis=0)
    x = pltpu.roll(x, row_off, 0)
    x = jnp.concatenate([x, jnp.zeros((PROBE + 8, 128), F32)], axis=1)
    x = pltpu.roll(x, col_off, 1)
    at = (part, pl.ds(row_base, PROBE + 8), pl.ds(col_base, PROBE + 128))
    field[at] = field[at] + x


def fetch_field(layer, core, obj, right, low_a, low_b, diag, side, field, sems):
    n, t = PROBE, TILE
    copies = [
        pltpu.make_async_copy(obj.at[layer], field.at[:, :t, :t], sems.at[0]),
        pltpu.make_async_copy(right, field.at[:, :t, t:], sems.at[1]),
        pltpu.make_async_copy(low_a, field.at[:, t:, :n], sems.at[2]),
        pltpu.make_async_copy(low_b, field.at[:, t:, n:t], sems.at[3]),
    ]
    for copy in copies:
        copy.start()

    @pl.when(core == 0)
    def _():
        copy = pltpu.make_async_copy(side, field.at[:, t:, t:], sems.at[4])
        copy.start()
        copy.wait()

    @pl.when(core != 0)
    def _():
        copy = pltpu.make_async_copy(diag, field.at[:, t:, t:], sems.at[4])
        copy.start()
        copy.wait()

    for copy in copies:
        copy.wait()


def store_field(field, main, right, low_a, low_b, corner, sems):
    n, t = PROBE, TILE
    copies = [
        pltpu.make_async_copy(field.at[:, :t, t:], right, sems.at[0]),
        pltpu.make_async_copy(field.at[:, t:, n:t], low_b, sems.at[1]),
        pltpu.make_async_copy(field.at[:, t:, :n], low_a, sems.at[2]),
        pltpu.make_async_copy(field.at[:, t:, t:], corner, sems.at[3]),
        pltpu.make_async_copy(field.at[:, :t, :t], main, sems.at[4]),
    ]
    for copy in copies:
        copy.start()
    for copy in copies:
        copy.wait()


def amp_kernel(amp, perm_l, perm_r, out):
    hi, mid, lo = exact_parts(amp[0])
    y = jnp.dot(perm_l[...], jnp.concatenate([hi, mid, lo], axis=0), preferred_element_type=F32)
    hi, mid, lo = exact_parts(y)
    out[0] = jnp.dot(jnp.concatenate([hi, mid, lo], axis=1), perm_r[...], preferred_element_type=F32)


def out_kernel(scalars, obj, right, low_a, low_b, diag, side, probe, table_l, table_r, psi, win, field, sems):
    slot = pl.program_id(0)

    @pl.when(slot == 0)
    def _():
        fetch_field(0, scalars[13], obj, right, low_a, low_b, diag, side, field, sems)

    @pl.when(slot < scalars[12])
    def _():
        place = place_of(scalars, slot)
        w_re = window_of(field, 0, place)
        w_im = window_of(field, 1, place)
        win[0, 0] = w_re
        win[0, 1] = w_im
        re = [probe[m, 0] * w_re - probe[m, 1] * w_im for m in (0, 1)]
        im = [probe[m, 0] * w_im + probe[m, 1] * w_re for m in (0, 1)]
        re, im = both_sides(re, im, table_l[...], table_r[...])
        for m in (0, 1):
            psi[0, m, 0] = re[m]
            psi[0, m, 1] = im[m]


def far_kernel(
    scalars, obj, right, low_a, low_b, diag, side, psi, amp, four_l, four_r, ruof_l, ruof_r, tw_row, tw_col,
    g_psi, g_main, g_right, g_low_a, g_low_b, g_corner, field, grad, sems,
):
    slot = pl.program_id(0)
    h, n = HALF, PROBE

    @pl.when(slot == 0)
    def _():
        fetch_field(1, scalars[13], obj, right, low_a, low_b, diag, side, field, sems)
        grad[...] = jnp.zeros_like(grad)

    @pl.when(slot < scalars[12])
    def _():
        place = place_of(scalars, slot)
        w_re = window_of(field, 0, place)
        w_im = window_of(field, 1, place)
        tr, ti = tw_row[0], tw_row[1]
        cr, ci = tw_col[0, 0:1], tw_col[1, 0:1]
        outs = []
        for m in (0, 1):
            p_re, p_im = psi[0, m, 0], psi[0, m, 1]
            re = p_re * w_re - p_im * w_im
            im = p_re * w_im + p_im * w_re
            d_re, d_im = re[:h] - re[h:], im[:h] - im[h:]
            top = jnp.concatenate([re[:h] + re[h:], d_re * tr - d_im * ti], axis=1)
            bottom = jnp.concatenate([im[:h] + im[h:], d_re * ti + d_im * tr], axis=1)
            y = lmul(four_l[...], jnp.concatenate([top, bottom], axis=0))
            re = jnp.concatenate([y[:h, :n], y[:h, n:]], axis=0)
            im = jnp.concatenate([y[h:, :n], y[h:, n:]], axis=0)
            d_re, d_im = re[:, :h] - re[:, h:], im[:, :h] - im[:, h:]
            even = jnp.concatenate([re[:, :h] + re[:, h:], im[:, :h] + im[:, h:]], axis=1)
            odd = jnp.concatenate([d_re * cr - d_im * ci, d_re * ci + d_im * cr], axis=1)
            outs.append(rmul(jnp.concatenate([even, odd], axis=0), four_r[...]))
        sq = outs[0] * outs[0] + outs[1] * outs[1]
        total = sq[:, :h] + sq[:, h:] + 1.0
        both = jnp.concatenate([amp[0, :, :h], amp[0, :, h:]], axis=0)
        slope = 2.0 - 2.0 * both * lax.rsqrt(total)
        slope = jnp.concatenate([slope, slope], axis=1)
        gw_re = gw_im = None
        for m in (0, 1):
            y = rmul(outs[m] * slope, ruof_r[...])
            q_re = y[n:, :h] * cr + y[n:, h:] * ci
            q_im = y[n:, h:] * cr - y[n:, :h] * ci
            re = jnp.concatenate([y[:n, :h] + q_re, y[:n, :h] - q_re], axis=1)
            im = jnp.concatenate([y[:n, h:] + q_im, y[:n, h:] - q_im], axis=1)
            x = jnp.concatenate(
                [
                    jnp.concatenate([re[:h], re[h:]], axis=1),
                    jnp.concatenate([im[:h], im[h:]], axis=1),
                ],
                axis=0,
            )
            y = lmul(ruof_l[...], x)
            q_re = y[:h, n:] * tr + y[h:, n:] * ti
            q_im = y[h:, n:] * tr - y[:h, n:] * ti
            re = jnp.concatenate([y[:h, :n] + q_re, y[:h, :n] - q_re], axis=0)
            im = jnp.concatenate([y[h:, :n] + q_im, y[h:, :n] - q_im], axis=0)
            g_psi[0, m, 0] = w_re * re + w_im * im
            g_psi[0, m, 1] = w_re * im - w_im * re
            p_re, p_im = psi[0, m, 0], psi[0, m, 1]
            a_re = p_re * re + p_im * im
            a_im = p_re * im - p_im * re
            gw_re = a_re if m == 0 else gw_re + a_re
            gw_im = a_im if m == 0 else gw_im + a_im
        add_window(grad, 0, place, gw_re)
        add_window(grad, 1, place, gw_im)

    @pl.when(slot == pl.num_programs(0) - 1)
    def _():
        store_field(grad, g_main, g_right, g_low_a, g_low_b, g_corner, sems)


def home_kernel(
    scalars, win, g_psi, probe, table_l, table_r,
    g_probe, g_main, g_right, g_low_a, g_low_b, g_corner, grad, sems,
):
    slot = pl.program_id(0)

    @pl.when(slot == 0)
    def _():
        grad[...] = jnp.zeros_like(grad)
        g_probe[...] = jnp.zeros_like(g_probe)

    @pl.when(slot < scalars[12])
    def _():
        place = place_of(scalars, slot)
        re = [g_psi[0, m, 0] for m in (0, 1)]
        im = [g_psi[0, m, 1] for m in (0, 1)]
        re, im = both_sides(re, im, table_l[...], table_r[...])
        w_re, w_im = win[0, 0], win[0, 1]
        gw_re = gw_im = None
        for m in (0, 1):
            p_re, p_im = probe[m, 0], probe[m, 1]
            a_re = p_re * re[m] + p_im * im[m]
            a_im = p_re * im[m] - p_im * re[m]
            gw_re = a_re if m == 0 else gw_re + a_re
            gw_im = a_im if m == 0 else gw_im + a_im
            g_probe[m, 0] += w_re * re[m] + w_im * im[m]
            g_probe[m, 1] += w_re * im[m] - w_im * re[m]
        add_window(grad, 0, place, gw_re)
        add_window(grad, 1, place, gw_im)

    @pl.when(slot == pl.num_programs(0) - 1)
    def _():
        store_field(grad, g_main, g_right, g_low_a, g_low_b, g_corner, sems)


def join_kernel(main, right, low_a, low_b, diag, *rest):
    out = rest[-1]
    n, h = PROBE, HALF
    i = pl.program_id(0)

    @pl.when(i < 2)
    def _():
        out[0, :, :, :n] = main[:, :, :n] + right[...] + low_a[...] + diag[...]
        out[0, :, :, n:] = main[:, :, n:] + low_b[...]

    @pl.when(i >= 2)
    def _():
        out[0, :, :, :n] = main[:, :, :n] + right[...]
        out[0, :, :, n:] = main[:, :, n:]


def whole(shape):
    return pl.BlockSpec(shape, lambda j, s: (0,) * len(shape))


def any_spec():
    return pl.BlockSpec(memory_space=pl.ANY)


def of_slot(shape):
    return pl.BlockSpec(
        (1,) + shape, lambda j, s: (jnp.minimum(j, s[12] - 1),) + (0,) * len(shape)
    )


def cost(flops, data):
    return pl.CostEstimate(flops=int(flops), bytes_accessed=int(data), transcendentals=0)


def params():
    return pltpu.CompilerParams(vmem_limit_bytes=VMEM_LIMIT)


FIELD_PARTS = [(2, TILE, TILE), (2, TILE, PROBE), (2, PROBE, PROBE), (2, PROBE, PROBE), (2, PROBE, PROBE)]


def sds(shape):
    return jax.ShapeDtypeStruct(shape, F32)


def permute_amplitudes(amp, tables):
    n = PROBE
    return pl.pallas_call(
        amp_kernel,
        grid=(SLOTS,),
        in_specs=[
            pl.BlockSpec((1, n, n), lambda j: (j, 0, 0)),
            pl.BlockSpec((n, 3 * n), lambda j: (0, 0)),
            pl.BlockSpec((3 * n, n), lambda j: (0, 0)),
        ],
        out_specs=pl.BlockSpec((1, n, n), lambda j: (j, 0, 0)),
        out_shape=sds((SLOTS, n, n)),
        compiler_params=params(),
        cost_estimate=cost(1.2e9, 4e6),
        name="order_amplitudes",
    )(amp, tables["perm_l"], tables["perm_r"])


def run_out(scalars, obj, halo, probe, tables):
    n = PROBE
    return pl.pallas_call(
        out_kernel,
        grid_spec=pltpu.PrefetchScalarGridSpec(
            num_scalar_prefetch=1,
            grid=(SLOTS,),
            in_specs=[any_spec()] * 6
            + [whole((2, 2, n, n)), whole((2 * n, 6 * n)), whole((6 * n, 2 * n))],
            out_specs=[of_slot((2, 2, n, n)), of_slot((2, n, n))],
            scratch_shapes=[pltpu.VMEM((2, 3 * n, 3 * n), F32), pltpu.SemaphoreType.DMA((5,))],
        ),
        out_shape=[sds((SLOTS, 2, 2, n, n)), sds((SLOTS, 2, n, n))],
        compiler_params=params(),
        cost_estimate=cost(1e10, 2e7),
        name="propagate_out",
    )(scalars, obj, *halo, probe, tables["prop_l"], tables["prop_r"])


def run_far(scalars, obj, halo, psi, amp, tables):
    n = PROBE
    return pl.pallas_call(
        far_kernel,
        grid_spec=pltpu.PrefetchScalarGridSpec(
            num_scalar_prefetch=1,
            grid=(SLOTS,),
            in_specs=[any_spec()] * 6
            + [of_slot((2, 2, n, n)), of_slot((n, n))]
            + [whole((n, 3 * n)), whole((3 * n, n))] * 2
            + [whole((2, HALF, n)), whole((2, 8, HALF))],
            out_specs=[of_slot((2, 2, n, n))] + [any_spec()] * 5,
            scratch_shapes=[
                pltpu.VMEM((2, 3 * n, 3 * n), F32),
                pltpu.VMEM((2, 3 * n, 3 * n), F32),
                pltpu.SemaphoreType.DMA((5,)),
            ],
        ),
        out_shape=[sds((SLOTS, 2, 2, n, n))] + [sds(s) for s in FIELD_PARTS],
        compiler_params=params(),
        cost_estimate=cost(1e10, 2e7),
        name="far_field",
    )(
        scalars, obj, *halo, psi, amp,
        tables["four_l"], tables["four_r"], tables["ruof_l"], tables["ruof_r"],
        tables["tw_row"], tables["tw_col"],
    )


def run_home(scalars, win, g_psi, probe, tables):
    n = PROBE
    return pl.pallas_call(
        home_kernel,
        grid_spec=pltpu.PrefetchScalarGridSpec(
            num_scalar_prefetch=1,
            grid=(SLOTS,),
            in_specs=[
                of_slot((2, n, n)),
                of_slot((2, 2, n, n)),
                whole((2, 2, n, n)),
                whole((2 * n, 6 * n)),
                whole((6 * n, 2 * n)),
            ],
            out_specs=[whole((2, 2, n, n))] + [any_spec()] * 5,
            scratch_shapes=[pltpu.VMEM((2, 3 * n, 3 * n), F32), pltpu.SemaphoreType.DMA((5,))],
        ),
        out_shape=[sds((2, 2, n, n))] + [sds(s) for s in FIELD_PARTS],
        compiler_params=params(),
        cost_estimate=cost(1e10, 2e7),
        name="propagate_home",
    )(scalars, win, g_psi, probe, tables["back_l"], tables["back_r"])


def run_join(layer, main, arrived, into):
    n, h = PROBE, HALF
    top = lambda i: (0, jnp.minimum(i, 1), 0)
    extra = [] if into is None else [into]
    return pl.pallas_call(
        join_kernel,
        grid=(4,),
        in_specs=[
            pl.BlockSpec((2, h, TILE), lambda i: (0, i, 0)),
            pl.BlockSpec((2, h, n), lambda i: (0, i, 0)),
            pl.BlockSpec((2, h, n), top),
            pl.BlockSpec((2, h, n), top),
            pl.BlockSpec((2, h, n), top),
        ]
        + [pl.BlockSpec(memory_space=pl.ANY)] * len(extra),
        out_specs=pl.BlockSpec((1, 2, h, TILE), lambda i: (layer, 0, i, 0)),
        out_shape=sds((2, 2, TILE, TILE)),
        input_output_aliases={} if into is None else {5: 0},
        compiler_params=params(),
        cost_estimate=cost(1e6, 6e6),
        name="join_gradients",
    )(main, *arrived, *extra)


def solution(mesh):
    n_gx, n_gy = mesh.shape["gx"], mesh.shape["gy"]
    axes = tuple(mesh.axis_names)
    tables = make_tables()

    def number(gx, gy):
        return gx * n_gy + gy if axes == ("gx", "gy") else gy * n_gx + gx

    def send(x, target):
        pairs = []
        for gx in range(n_gx):
            for gy in range(n_gy):
                to = target(gx, gy)
                if to is not None and 0 <= to[0] < n_gx and 0 <= to[1] < n_gy:
                    pairs.append((number(gx, gy), number(*to)))
        return lax.ppermute(x, axes, pairs)

    def flip(gx_bits, gy_bits):
        return lambda gx, gy: (gx ^ gx_bits, gy ^ gy_bits)

    def bring(obj, layer):
        n = PROBE
        low_a = send(obj[layer, :, :n, :n], lambda gx, gy: (gx, gy - 1))
        right = send(obj[layer, :, :, :n], lambda gx, gy: (gx - 1, gy))
        low_b = send(obj[layer, :, :n, n:], lambda gx, gy: (gx, gy - 1))
        diag = send(obj[layer, :, :n, :n], lambda gx, gy: (gx - 1, gy - 1) if gx % 2 == 0 else None)
        side = send(low_a, lambda gx, gy: (gx - 1, gy) if gx % 2 == 1 else None)
        return right, low_a, low_b, diag, side

    def take_back(right, low_a, low_b, corner):
        side = send(corner, lambda gx, gy: (gx + 1, gy) if gx % 2 == 0 else None)
        right = send(right, lambda gx, gy: (gx + 1, gy))
        low_b = send(low_b, lambda gx, gy: (gx, gy + 1))
        diag = send(corner, lambda gx, gy: (gx + 1, gy + 1) if gx % 2 == 1 else None)
        low_a = send(low_a + side, lambda gx, gy: (gx, gy + 1))
        return right, low_a, low_b, diag

    def gather_probe(probe):
        gx = lax.axis_index("gx")
        core, y_hi, z = gx % 2, gx // 2 % 2, gx // 4
        parts = [probe] + [send(probe, flip(4 * k, 0)) for k in (1, 2, 3)]
        stack = jnp.stack(parts)
        stack = jnp.stack([stack[k ^ 0] for k in range(4)])
        ordered = [
            jnp.where(z == 0, stack[k], jnp.where(z == 1, stack[k ^ 1], jnp.where(z == 2, stack[k ^ 2], stack[k ^ 3])))
            for k in range(4)
        ]
        mine = jnp.stack(ordered)
        other = send(mine, flip(2, 1))
        mine = jnp.where(y_hi == 0, jnp.stack([mine, other]), jnp.stack([other, mine]))
        other = send(mine, flip(1, 0))
        mine = jnp.where(core == 0, jnp.stack([mine, other]), jnp.stack([other, mine]))
        rows = probe.shape[2]
        full = jnp.transpose(mine, (3, 4, 2, 1, 0, 5, 6))
        return full.reshape(2, 2, n_gx * rows, PROBE)

    def reduce_probe(grad):
        gx = lax.axis_index("gx")
        core, y_hi, z = gx % 2, gx // 2 % 2, gx // 4
        rows = PROBE // n_gx
        parts = jnp.transpose(grad.reshape(2, 2, 4, 2, 2, rows, PROBE), (4, 2, 3, 0, 1, 5, 6))
        keep = jnp.where(core == 0, parts[0], parts[1])
        give = jnp.where(core == 0, parts[1], parts[0])
        part = keep + send(give, flip(1, 0))

        def at_z(k):
            return lax.dynamic_index_in_dim(part, z ^ k, 0, keepdims=False)

        got = [send(at_z(k), flip(4 * k, 0)) for k in (1, 2, 3)]
        part = (at_z(0) + got[0]) + (got[1] + got[2])
        keep = jnp.where(y_hi == 0, part[0], part[1])
        give = jnp.where(y_hi == 0, part[1], part[0])
        near = send(keep, flip(0, 1))
        far = send(give, flip(2, 0))
        across = send(give, flip(2, 1))
        part = (keep + near) + (far + across)
        got = [send(part, flip(0, 2 * k)) for k in (1, 2, 3)]
        return (part + got[0]) + (got[1] + got[2])

    def on_device(obj, probe, positions, counts, amplitudes):
        core = lax.axis_index("gx") % 2
        scalars = jnp.concatenate(
            [positions.reshape(2 * SLOTS), counts.reshape(1), core.astype(jnp.int32).reshape(1)]
        )
        halo_0 = bring(obj, 0)
        probe_full = gather_probe(probe)
        amp = permute_amplitudes(amplitudes[0, 0], tables)
        obj_late, halo_0 = lax.optimization_barrier((obj, halo_0))
        halo_1 = bring(obj_late, 1)
        psi, win = run_out(scalars, obj, halo_0, probe_full, tables)
        g_psi, main_1, *edges_1 = run_far(scalars, obj, halo_1, psi, amp, tables)
        back_1 = take_back(*edges_1)
        g_probe, main_0, *edges_0 = run_home(scalars, win, g_psi, probe_full, tables)
        edges_0, back_1 = lax.optimization_barrier((edges_0, back_1))
        back_0 = take_back(*edges_0)
        grad = run_join(1, main_1, back_1, None)
        probe_grad = reduce_probe(g_probe)
        grad = run_join(0, main_0, back_0, grad)
        return grad, probe_grad

    return jax.shard_map(
        on_device,
        mesh=mesh,
        in_specs=(
            P(None, None, "gy", "gx"),
            P(None, None, "gx", None),
            P("gy", "gx", None, None),
            P("gy", "gx"),
            P("gy", "gx", None, None, None),
        ),
        out_specs=(P(None, None, "gy", "gx"), P(None, None, "gx", None)),
        check_vma=False,
    )
```

```python
import functools
import math

import jax
import jax.numpy as jnp
import numpy as np
from jax import lax
from jax.experimental import pallas as pl
from jax.experimental.pallas import tpu as pltpu
from jax.sharding import PartitionSpec as P

BAND = 48
PROBE = 256
HALF = 128
TILE = 512
SLOTS = 6
F32 = jnp.float32
BF16 = jnp.bfloat16
VMEM_LIMIT = 48 * 1024 * 1024


def split_table(mat):
    hi = mat.astype(BF16)
    lo = (mat - hi.astype(np.float64)).astype(BF16)
    return hi, lo


def left_table(mat):
    hi, lo = split_table(mat)
    return np.concatenate([hi, lo, hi], axis=1)


def right_table(mat):
    hi, lo = split_table(mat)
    return np.concatenate([hi, lo, hi], axis=0)


def make_tables():
    index = np.arange(PROBE)
    offset = (index[:, None] - index[None, :]).astype(np.float64)
    prop = np.where(np.abs(offset) <= BAND, np.exp(1j * np.pi * offset**2 / (2 * BAND)), 0)
    prop = prop / math.sqrt(2 * BAND + 1)
    half = np.arange(HALF)
    four = np.exp(-2j * np.pi * ((half[:, None] * half[None, :]) % HALF) / HALF) / math.sqrt(PROBE)
    twist = np.exp(-2j * np.pi * half / PROBE)

    def from_left(mat):
        return np.block([[mat.real, -mat.imag], [mat.imag, mat.real]])

    def from_right(mat):
        return from_left(mat).T

    order = np.concatenate([np.arange(0, PROBE, 2), np.arange(1, PROBE, 2)])
    perm = np.zeros((PROBE, PROBE))
    perm[np.arange(PROBE), order] = 1
    return {
        "prop_l": left_table(from_left(prop)),
        "prop_r": right_table(from_right(prop)),
        "back_l": left_table(from_left(prop.conj())),
        "back_r": right_table(from_right(prop.conj())),
        "four_l": left_table(from_left(four)),
        "four_r": right_table(from_right(four)),
        "ruof_l": left_table(from_left(four.conj())),
        "ruof_r": right_table(from_right(four.conj())),
        "tw_row": np.stack(
            [
                np.broadcast_to(twist.real[:, None], (HALF, PROBE)),
                np.broadcast_to(twist.imag[:, None], (HALF, PROBE)),
            ]
        ).astype(np.float32),
        "tw_col": np.stack(
            [
                np.broadcast_to(twist.real[None, :], (8, HALF)),
                np.broadcast_to(twist.imag[None, :], (8, HALF)),
            ]
        ).astype(np.float32),
        "perm_l": np.concatenate([perm] * 3, axis=1).astype(BF16),
        "perm_r": np.concatenate([perm.T] * 3, axis=0).astype(BF16),
    }


def parted(x):
    hi = x.astype(BF16)
    return hi, (x - hi.astype(F32)).astype(BF16)


def lmul(table, x):
    hi, lo = parted(x)
    return jnp.dot(table, jnp.concatenate([hi, hi, lo], axis=0), preferred_element_type=F32)


def rmul(x, table):
    hi, lo = parted(x)
    return jnp.dot(jnp.concatenate([hi, hi, lo], axis=1), table, preferred_element_type=F32)


def exact_parts(x):
    hi = x.astype(BF16)
    rest = x - hi.astype(F32)
    mid = rest.astype(BF16)
    return hi, mid, (rest - mid.astype(F32)).astype(BF16)


def both_sides(re, im, table_l, table_r):
    x = jnp.concatenate(
        [jnp.concatenate(re, axis=1), jnp.concatenate(im, axis=1)], axis=0
    )
    y = lmul(table_l, x)
    n = PROBE
    x = jnp.concatenate(
        [jnp.concatenate([y[:n, m * n : (m + 1) * n], y[n:, m * n : (m + 1) * n]], axis=1) for m in (0, 1)],
        axis=0,
    )
    y = rmul(x, table_r)
    return [y[m * n : (m + 1) * n, :n] for m in (0, 1)], [y[m * n : (m + 1) * n, n:] for m in (0, 1)]


def place_of(scalars, slot):
    row = scalars[2 * slot]
    col = scalars[2 * slot + 1]
    row_base = pl.multiple_of(row // 8 * 8, 8)
    col_base = pl.multiple_of(col // 128 * 128, 128)
    return row_base, row - row_base, col_base, col - col_base


def window_of(field, part, place):
    row_base, row_off, col_base, col_off = place
    x = field[part, pl.ds(row_base, PROBE + 8), pl.ds(col_base, PROBE + 128)]
    x = pltpu.roll(x, (PROBE + 128 - col_off) % (PROBE + 128), 1)[:, :PROBE]
    return pltpu.roll(x, (PROBE + 8 - row_off) % (PROBE + 8), 0)[:PROBE]


def add_window(field, part, place, x):
    row_base, row_off, col_base, col_off = place
    x = jnp.concatenate([x, jnp.zeros((8, PROBE), F32)], axis=0)
    x = pltpu.roll(x, row_off, 0)
    x = jnp.concatenate([x, jnp.zeros((PROBE + 8, 128), F32)], axis=1)
    x = pltpu.roll(x, col_off, 1)
    at = (part, pl.ds(row_base, PROBE + 8), pl.ds(col_base, PROBE + 128))
    field[at] = field[at] + x


def fetch_field(layer, core, obj, right, low_a, low_b, diag, side, field, sems):
    n, t = PROBE, TILE
    copies = [
        pltpu.make_async_copy(obj.at[layer], field.at[:, :t, :t], sems.at[0]),
        pltpu.make_async_copy(right, field.at[:, :t, t:], sems.at[1]),
        pltpu.make_async_copy(low_a, field.at[:, t:, :n], sems.at[2]),
        pltpu.make_async_copy(low_b, field.at[:, t:, n:t], sems.at[3]),
    ]
    for copy in copies:
        copy.start()

    @pl.when(core == 0)
    def _():
        copy = pltpu.make_async_copy(side, field.at[:, t:, t:], sems.at[4])
        copy.start()
        copy.wait()

    @pl.when(core != 0)
    def _():
        copy = pltpu.make_async_copy(diag, field.at[:, t:, t:], sems.at[4])
        copy.start()
        copy.wait()

    for copy in copies:
        copy.wait()


def store_field(field, main, right, low_a, low_b, corner, sems):
    n, t = PROBE, TILE
    copies = [
        pltpu.make_async_copy(field.at[:, :t, t:], right, sems.at[0]),
        pltpu.make_async_copy(field.at[:, t:, n:t], low_b, sems.at[1]),
        pltpu.make_async_copy(field.at[:, t:, :n], low_a, sems.at[2]),
        pltpu.make_async_copy(field.at[:, t:, t:], corner, sems.at[3]),
        pltpu.make_async_copy(field.at[:, :t, :t], main, sems.at[4]),
    ]
    for copy in copies:
        copy.start()
    for copy in copies:
        copy.wait()


def amp_kernel(amp, perm_l, perm_r, out):
    hi, mid, lo = exact_parts(amp[0])
    y = jnp.dot(perm_l[...], jnp.concatenate([hi, mid, lo], axis=0), preferred_element_type=F32)
    hi, mid, lo = exact_parts(y)
    out[0] = jnp.dot(jnp.concatenate([hi, mid, lo], axis=1), perm_r[...], preferred_element_type=F32)


def out_kernel(
    scalars, obj, right, low_a, low_b, diag, side, mine, across, mine_other, across_other, table_l, table_r,
    psi, win, probe_rows, field, sems, probe_sem,
):
    slot = pl.program_id(0)
    probe = probe_rows.reshape(2, 2, PROBE, PROBE)

    @pl.when(slot == 0)
    def _():
        core, y_hi, z = scalars[13], scalars[14], scalars[15]
        copies = [
            pltpu.make_async_copy(src.at[k], probe_rows.at[:, :, z ^ k, y, c], probe_sem)
            for src, y, c in (
                (mine, y_hi, core),
                (across, 1 - y_hi, core),
                (mine_other, y_hi, 1 - core),
                (across_other, 1 - y_hi, 1 - core),
            )
            for k in range(4)
        ]
        for copy in copies:
            copy.start()
        fetch_field(0, core, obj, right, low_a, low_b, diag, side, field, sems)
        for copy in copies:
            copy.wait()

    @pl.when(slot < scalars[12])
    def _():
        place = place_of(scalars, slot)
        w_re = window_of(field, 0, place)
        w_im = window_of(field, 1, place)
        win[0, 0] = w_re
        win[0, 1] = w_im
        re = [probe[m, 0] * w_re - probe[m, 1] * w_im for m in (0, 1)]
        im = [probe[m, 0] * w_im + probe[m, 1] * w_re for m in (0, 1)]
        re, im = both_sides(re, im, table_l[...], table_r[...])
        for m in (0, 1):
            psi[0, m, 0] = re[m]
            psi[0, m, 1] = im[m]


def far_kernel(
    scalars, obj, right, low_a, low_b, diag, side, psi, amp, four_l, four_r, ruof_l, ruof_r, tw_row, tw_col,
    g_psi, g_main, g_right, g_low_a, g_low_b, g_corner, field, grad, win, gwin, sems,
):
    slot = pl.program_id(0)
    h, n = HALF, PROBE
    used = scalars[12]

    def load_window(at):
        place = place_of(scalars, at)
        win[0] = window_of(field, 0, place)
        win[1] = window_of(field, 1, place)

    def flush(at):
        place = place_of(scalars, at)
        add_window(grad, 0, place, gwin[0])
        add_window(grad, 1, place, gwin[1])

    @pl.when(slot == 0)
    def _():
        grad[...] = jnp.zeros_like(grad)
        gwin[...] = jnp.zeros_like(gwin)
        fetch_field(1, scalars[13], obj, right, low_a, low_b, diag, side, field, sems)
        load_window(0)

    @pl.when(slot < used)
    def _():
        w_re, w_im = win[0], win[1]
        tr, ti = tw_row[0], tw_row[1]
        cr, ci = tw_col[0, 0:1], tw_col[1, 0:1]
        chi = {}

        def left(m, odd):
            if m not in chi:
                p_re, p_im = psi[0, m, 0], psi[0, m, 1]
                chi[m] = (p_re * w_re - p_im * w_im, p_re * w_im + p_im * w_re)
            re, im = chi[m]
            if odd:
                d_re, d_im = re[:h] - re[h:], im[:h] - im[h:]
                x = [d_re * tr - d_im * ti, d_re * ti + d_im * tr]
            else:
                x = [re[:h] + re[h:], im[:h] + im[h:]]
            return lmul(four_l[...], jnp.concatenate(x, axis=0))

        def across(y):
            re, im = y[:h], y[h:]
            d_re, d_im = re[:, :h] - re[:, h:], im[:, :h] - im[:, h:]
            even = jnp.concatenate([re[:, :h] + re[:, h:], im[:, :h] + im[:, h:]], axis=1)
            odd = jnp.concatenate([d_re * cr - d_im * ci, d_re * ci + d_im * cr], axis=1)
            return rmul(jnp.concatenate([even, odd], axis=0), four_r[...])

        def slope_of(z0, z1, rows):
            sq = z0 * z0 + z1 * z1
            total = sq[:, :h] + sq[:, h:] + 1.0
            both = jnp.concatenate([amp[0, rows, :h], amp[0, rows, h:]], axis=0)
            slope = 2.0 - 2.0 * both * lax.rsqrt(total)
            return jnp.concatenate([slope, slope], axis=1)

        def back_across(z):
            y = rmul(z, ruof_r[...])
            q_re = y[h:, :h] * cr + y[h:, h:] * ci
            q_im = y[h:, h:] * cr - y[h:, :h] * ci
            re = jnp.concatenate([y[:h, :h] + q_re, y[:h, :h] - q_re], axis=1)
            im = jnp.concatenate([y[:h, h:] + q_im, y[:h, h:] - q_im], axis=1)
            return jnp.concatenate([re, im], axis=0)

        def finish(m, y_even, y_odd):
            q_re = y_odd[:h] * tr + y_odd[h:] * ti
            q_im = y_odd[h:] * tr - y_odd[:h] * ti
            re = jnp.concatenate([y_even[:h] + q_re, y_even[:h] - q_re], axis=0)
            im = jnp.concatenate([y_even[h:] + q_im, y_even[h:] - q_im], axis=0)
            g_psi[0, m, 0] = w_re * re + w_im * im
            g_psi[0, m, 1] = w_re * im - w_im * re
            p_re, p_im = psi[0, m, 0], psi[0, m, 1]
            return p_re * re + p_im * im, p_re * im - p_im * re

        back = ruof_l[...]
        l0e = left(0, 0)
        l1e = left(1, 0)
        l0o = left(0, 1)
        z0e = across(l0e)
        l1o = left(1, 1)
        z1e = across(l1e)
        slope_e = slope_of(z0e, z1e, slice(0, h))
        z0o = across(l0o)
        b0e = back_across(z0e * slope_e)
        z1o = across(l1o)
        flush(jnp.maximum(slot - 1, 0))
        slope_o = slope_of(z0o, z1o, slice(h, n))
        load_window(jnp.minimum(slot + 1, SLOTS - 1))
        b1e = back_across(z1e * slope_e)
        a0e = lmul(back, b0e)
        b0o = back_across(z0o * slope_o)
        a1e = lmul(back, b1e)
        b1o = back_across(z1o * slope_o)
        a0o = lmul(back, b0o)
        a1o = lmul(back, b1o)
        u_re, u_im = finish(0, a0e, a0o)
        v_re, v_im = finish(1, a1e, a1o)
        gwin[0] = u_re + v_re
        gwin[1] = u_im + v_im

    @pl.when(slot == pl.num_programs(0) - 1)
    def _():
        flush(used - 1)
        store_field(grad, g_main, g_right, g_low_a, g_low_b, g_corner, sems)


def home_kernel(
    scalars, win, g_psi, probe, table_l, table_r,
    g_probe, g_main, g_right, g_low_a, g_low_b, g_corner, grad, sems,
):
    slot = pl.program_id(0)

    @pl.when(slot == 0)
    def _():
        grad[...] = jnp.zeros_like(grad)
        g_probe[...] = jnp.zeros_like(g_probe)

    @pl.when(slot < scalars[12])
    def _():
        place = place_of(scalars, slot)
        re = [g_psi[0, m, 0] for m in (0, 1)]
        im = [g_psi[0, m, 1] for m in (0, 1)]
        re, im = both_sides(re, im, table_l[...], table_r[...])
        w_re, w_im = win[0, 0], win[0, 1]
        gw_re = gw_im = None
        for m in (0, 1):
            p_re, p_im = probe[m, 0], probe[m, 1]
            a_re = p_re * re[m] + p_im * im[m]
            a_im = p_re * im[m] - p_im * re[m]
            gw_re = a_re if m == 0 else gw_re + a_re
            gw_im = a_im if m == 0 else gw_im + a_im
            g_probe[m, 0] += w_re * re[m] + w_im * im[m]
            g_probe[m, 1] += w_re * im[m] - w_im * re[m]
        add_window(grad, 0, place, gw_re)
        add_window(grad, 1, place, gw_im)

    @pl.when(slot == pl.num_programs(0) - 1)
    def _():
        store_field(grad, g_main, g_right, g_low_a, g_low_b, g_corner, sems)


def join_kernel(main, right, low_a, low_b, diag, *rest):
    out = rest[-1]
    n, h = PROBE, HALF
    i = pl.program_id(0)

    @pl.when(i < 2)
    def _():
        out[0, :, :, :n] = main[:, :, :n] + right[...] + low_a[...] + diag[...]
        out[0, :, :, n:] = main[:, :, n:] + low_b[...]

    @pl.when(i >= 2)
    def _():
        out[0, :, :, :n] = main[:, :, :n] + right[...]
        out[0, :, :, n:] = main[:, :, n:]


def whole(shape):
    return pl.BlockSpec(shape, lambda j, s: (0,) * len(shape))


def held():
    return pl.BlockSpec(memory_space=pltpu.VMEM)


def any_spec():
    return pl.BlockSpec(memory_space=pl.ANY)


def of_slot(shape):
    return pl.BlockSpec(
        (1,) + shape, lambda j, s: (jnp.minimum(j, s[12] - 1),) + (0,) * len(shape)
    )


def cost(flops, data):
    return pl.CostEstimate(flops=int(flops), bytes_accessed=int(data), transcendentals=0)


def params():
    return pltpu.CompilerParams(vmem_limit_bytes=VMEM_LIMIT)


FIELD_PARTS = [(2, TILE, TILE), (2, TILE, PROBE), (2, PROBE, PROBE), (2, PROBE, PROBE), (2, PROBE, PROBE)]


def sds(shape):
    return jax.ShapeDtypeStruct(shape, F32)


def permute_amplitudes(amp, tables):
    n = PROBE
    return pl.pallas_call(
        amp_kernel,
        grid=(SLOTS,),
        in_specs=[
            pl.BlockSpec((1, n, n), lambda j: (j, 0, 0)),
            pl.BlockSpec((n, 3 * n), lambda j: (0, 0)),
            pl.BlockSpec((3 * n, n), lambda j: (0, 0)),
        ],
        out_specs=pl.BlockSpec((1, n, n), lambda j: (j, 0, 0)),
        out_shape=sds((SLOTS, n, n)),
        compiler_params=params(),
        cost_estimate=cost(1.2e9, 4e6),
        name="order_amplitudes",
    )(amp, tables["perm_l"], tables["perm_r"])


def run_out(scalars, obj, halo, probe, tables):
    n = PROBE
    return pl.pallas_call(
        out_kernel,
        grid_spec=pltpu.PrefetchScalarGridSpec(
            num_scalar_prefetch=1,
            grid=(SLOTS,),
            in_specs=[any_spec()] * 10 + [held()] * 2,
            out_specs=[of_slot((2, 2, n, n)), of_slot((2, n, n)), whole((2, 2, 4, 2, 2, 16, n))],
            scratch_shapes=[
                pltpu.VMEM((2, 3 * n, 3 * n), F32),
                pltpu.SemaphoreType.DMA((5,)),
                pltpu.SemaphoreType.DMA,
            ],
        ),
        out_shape=[sds((SLOTS, 2, 2, n, n)), sds((SLOTS, 2, n, n)), sds((2, 2, 4, 2, 2, 16, n))],
        compiler_params=params(),
        cost_estimate=cost(6e10, 2e7),
        name="propagate_out",
    )(scalars, obj, *halo, *probe, tables["prop_l"], tables["prop_r"])


def run_far(scalars, obj, halo, psi, amp, tables):
    n = PROBE
    return pl.pallas_call(
        far_kernel,
        grid_spec=pltpu.PrefetchScalarGridSpec(
            num_scalar_prefetch=1,
            grid=(SLOTS,),
            in_specs=[any_spec()] * 6
            + [of_slot((2, 2, n, n)), of_slot((n, n))]
            + [held()] * 6,
            out_specs=[of_slot((2, 2, n, n))] + [any_spec()] * 5,
            scratch_shapes=[
                pltpu.VMEM((2, 3 * n, 3 * n), F32),
                pltpu.VMEM((2, 3 * n, 3 * n), F32),
                pltpu.VMEM((2, n, n), F32),
                pltpu.VMEM((2, n, n), F32),
                pltpu.SemaphoreType.DMA((5,)),
            ],
        ),
        out_shape=[sds((SLOTS, 2, 2, n, n))] + [sds(s) for s in FIELD_PARTS],
        compiler_params=params(),
        cost_estimate=cost(6e10, 2e7),
        name="far_field",
    )(
        scalars, obj, *halo, psi, amp,
        tables["four_l"], tables["four_r"], tables["ruof_l"], tables["ruof_r"],
        tables["tw_row"], tables["tw_col"],
    )


def run_home(scalars, win, g_psi, probe, tables):
    n = PROBE
    return pl.pallas_call(
        home_kernel,
        grid_spec=pltpu.PrefetchScalarGridSpec(
            num_scalar_prefetch=1,
            grid=(SLOTS,),
            in_specs=[
                of_slot((2, n, n)),
                of_slot((2, 2, n, n)),
                held(),
                held(),
                held(),
            ],
            out_specs=[whole((2, 2, n, n))] + [any_spec()] * 5,
            scratch_shapes=[pltpu.VMEM((2, 3 * n, 3 * n), F32), pltpu.SemaphoreType.DMA((5,))],
        ),
        out_shape=[sds((2, 2, n, n))] + [sds(s) for s in FIELD_PARTS],
        compiler_params=params(),
        cost_estimate=cost(6e10, 2e7),
        name="propagate_home",
    )(scalars, win, g_psi, probe, tables["back_l"], tables["back_r"])


def run_join(layer, main, arrived, into):
    n, h = PROBE, HALF
    top = lambda i: (0, jnp.minimum(i, 1), 0)
    extra = [] if into is None else [into]
    return pl.pallas_call(
        join_kernel,
        grid=(4,),
        in_specs=[
            pl.BlockSpec((2, h, TILE), lambda i: (0, i, 0)),
            pl.BlockSpec((2, h, n), lambda i: (0, i, 0)),
            pl.BlockSpec((2, h, n), top),
            pl.BlockSpec((2, h, n), top),
            pl.BlockSpec((2, h, n), top),
        ]
        + [pl.BlockSpec(memory_space=pl.ANY)] * len(extra),
        out_specs=pl.BlockSpec((1, 2, h, TILE), lambda i: (layer, 0, i, 0)),
        out_shape=sds((2, 2, TILE, TILE)),
        input_output_aliases={} if into is None else {5: 0},
        compiler_params=params(),
        cost_estimate=cost(1e6, 6e6),
        name="join_gradients",
    )(main, *arrived, *extra)


def solution(mesh):
    n_gx, n_gy = mesh.shape["gx"], mesh.shape["gy"]
    axes = tuple(mesh.axis_names)
    tables = make_tables()

    def number(gx, gy):
        return gx * n_gy + gy if axes == ("gx", "gy") else gy * n_gx + gx

    def send(x, target):
        pairs = []
        for gx in range(n_gx):
            for gy in range(n_gy):
                to = target(gx, gy)
                if to is not None and 0 <= to[0] < n_gx and 0 <= to[1] < n_gy:
                    pairs.append((number(gx, gy), number(*to)))
        return lax.ppermute(x, axes, pairs)

    def flip(gx_bits, gy_bits):
        return lambda gx, gy: (gx ^ gx_bits, gy ^ gy_bits)

    def pieces(obj, layer):
        n = PROBE
        return obj[layer, :, :n, :n], obj[layer, :, :, :n], obj[layer, :, :n, n:]

    def bring(corner, edge, low):
        low_a = send(corner, lambda gx, gy: (gx, gy - 1))
        right = send(edge, lambda gx, gy: (gx - 1, gy))
        low_b = send(low, lambda gx, gy: (gx, gy - 1))
        diag = send(corner, lambda gx, gy: (gx - 1, gy - 1) if gx % 2 == 0 else None)
        side = send(low_a, lambda gx, gy: (gx - 1, gy) if gx % 2 == 1 else None)
        return right, low_a, low_b, diag, side

    def take_back(right, low_a, low_b, corner):
        side = send(corner, lambda gx, gy: (gx + 1, gy) if gx % 2 == 0 else None)
        right = send(right, lambda gx, gy: (gx + 1, gy))
        low_b = send(low_b, lambda gx, gy: (gx, gy + 1))
        diag = send(corner, lambda gx, gy: (gx + 1, gy + 1) if gx % 2 == 1 else None)
        low_a = send(low_a + side, lambda gx, gy: (gx, gy + 1))
        return right, low_a, low_b, diag

    def gather_probe(probe):
        mine = jnp.stack([probe] + [send(probe, flip(4 * k, 0)) for k in (1, 2, 3)])
        return mine, send(mine, flip(2, 1))

    def reduce_probe(grad):
        gx = lax.axis_index("gx")
        core, y_hi, z = gx % 2, gx // 2 % 2, gx // 4
        rows = PROBE // n_gx
        parts = jnp.transpose(grad.reshape(2, 2, 4, 2, 2, rows, PROBE), (4, 2, 3, 0, 1, 5, 6))
        keep = jnp.where(core == 0, parts[0], parts[1])
        give = jnp.where(core == 0, parts[1], parts[0])
        part = keep + send(give, flip(1, 0))

        def at_z(k):
            return lax.dynamic_index_in_dim(part, z ^ k, 0, keepdims=False)

        got = [send(at_z(k), flip(4 * k, 0)) for k in (1, 2, 3)]
        part = (at_z(0) + got[0]) + (got[1] + got[2])
        keep = jnp.where(y_hi == 0, part[0], part[1])
        give = jnp.where(y_hi == 0, part[1], part[0])
        near = send(keep, flip(0, 1))
        far = send(give, flip(2, 0))
        across = send(give, flip(2, 1))
        part = (keep + near) + (far + across)
        got = [send(part, flip(0, 2 * k)) for k in (1, 2, 3)]
        return (part + got[0]) + (got[1] + got[2])

    def on_device(obj, probe, positions, counts, amplitudes):
        gx = lax.axis_index("gx").astype(jnp.int32)
        scalars = jnp.concatenate(
            [positions.reshape(2 * SLOTS), counts.reshape(1), jnp.stack([gx & 1, gx >> 1 & 1, gx >> 2])]
        )
        halo_0 = bring(*pieces(obj, 0))
        probe_parts = gather_probe(probe)
        amp = permute_amplitudes(amplitudes[0, 0], tables)
        pieces_1, halo_0, amp, probe_parts = lax.optimization_barrier((pieces(obj, 1), halo_0, amp, probe_parts))
        probe_parts = [*probe_parts, *(send(x, flip(1, 0)) for x in probe_parts)]
        halo_1 = bring(*pieces_1)
        psi, win, probe_rows = run_out(scalars, obj, halo_0, probe_parts, tables)
        probe_full = probe_rows.reshape(2, 2, PROBE, PROBE)
        g_psi, main_1, *edges_1 = run_far(scalars, obj, halo_1, psi, amp, tables)
        back_1 = take_back(*edges_1)
        g_probe, main_0, *edges_0 = run_home(scalars, win, g_psi, probe_full, tables)
        edges_0, g_probe, back_1 = lax.optimization_barrier((edges_0, g_probe, back_1))
        back_0 = take_back(*edges_0)
        grad = run_join(1, main_1, back_1, None)
        probe_grad = reduce_probe(g_probe)
        grad = run_join(0, main_0, back_0, grad)
        return grad, probe_grad

    return jax.shard_map(
        on_device,
        mesh=mesh,
        in_specs=(
            P(None, None, "gy", "gx"),
            P(None, None, "gx", None),
            P("gy", "gx", None, None),
            P("gy", "gx"),
            P("gy", "gx", None, None, None),
        ),
        out_specs=(P(None, None, "gy", "gx"), P(None, None, "gx", None)),
        check_vma=False,
    )
```

```python
import functools
import math

import jax
import jax.numpy as jnp
import numpy as np
from jax import lax
from jax.experimental import pallas as pl
from jax.experimental.pallas import tpu as pltpu
from jax.sharding import PartitionSpec as P

BAND = 48
PROBE = 256
HALF = 128
TILE = 512
SLOTS = 6
F32 = jnp.float32
BF16 = jnp.bfloat16
VMEM_LIMIT = 48 * 1024 * 1024


def split_table(mat):
    hi = mat.astype(BF16)
    lo = (mat - hi.astype(np.float64)).astype(BF16)
    return hi, lo


def left_table(mat):
    hi, lo = split_table(mat)
    return np.concatenate([hi, lo, hi], axis=1)


def right_table(mat):
    hi, lo = split_table(mat)
    return np.concatenate([hi, lo, hi], axis=0)


def make_tables():
    index = np.arange(PROBE)
    offset = (index[:, None] - index[None, :]).astype(np.float64)
    prop = np.where(np.abs(offset) <= BAND, np.exp(1j * np.pi * offset**2 / (2 * BAND)), 0)
    prop = prop / math.sqrt(2 * BAND + 1)
    half = np.arange(HALF)
    four = np.exp(-2j * np.pi * ((half[:, None] * half[None, :]) % HALF) / HALF) / math.sqrt(PROBE)
    twist = np.exp(-2j * np.pi * half / PROBE)

    def from_left(mat):
        return np.block([[mat.real, -mat.imag], [mat.imag, mat.real]])

    def from_right(mat):
        return from_left(mat).T

    near = np.arange(PROBE) < HALF
    edge = (np.arange(PROBE) + HALF // 2) // HALF == 1
    cross = np.where(near[:, None] != near[None, :], prop, 0)
    assert not cross[~edge].any() and not cross[:, ~edge].any()

    def pair(table, embed, mat):
        other = np.zeros((HALF, HALF), complex)
        for a in range(HALF):
            for b in range(HALF):
                to, of = (a + HALF, b) if a < HALF // 2 else (a, b + HALF)
                if (b >= HALF // 2) == (a < HALF // 2):
                    other[a, b] = mat[to, of]
        return np.stack([table(embed(mat[:HALF, :HALF])), table(embed(other))])

    order = np.concatenate([np.arange(0, PROBE, 2), np.arange(1, PROBE, 2)])
    perm = np.zeros((PROBE, PROBE))
    perm[np.arange(PROBE), order] = 1
    return {
        "prop_l": pair(left_table, from_left, prop),
        "prop_r": pair(right_table, from_right, prop),
        "back_l": pair(left_table, from_left, prop.conj()),
        "back_r": pair(right_table, from_right, prop.conj()),
        "four_l": left_table(from_left(four)),
        "four_r": right_table(from_right(four)),
        "ruof_l": left_table(from_left(four.conj())),
        "ruof_r": right_table(from_right(four.conj())),
        "tw_row": np.stack(
            [
                np.broadcast_to(twist.real[:, None], (HALF, PROBE)),
                np.broadcast_to(twist.imag[:, None], (HALF, PROBE)),
            ]
        ).astype(np.float32),
        "tw_col": np.stack(
            [
                np.broadcast_to(twist.real[None, :], (8, HALF)),
                np.broadcast_to(twist.imag[None, :], (8, HALF)),
            ]
        ).astype(np.float32),
        "perm_l": np.concatenate([perm] * 3, axis=1).astype(BF16),
        "perm_r": np.concatenate([perm.T] * 3, axis=0).astype(BF16),
    }


def parted(x):
    hi = x.astype(BF16)
    return hi, (x - hi.astype(F32)).astype(BF16)


def lmul(table, x):
    hi, lo = parted(x)
    return jnp.dot(table, jnp.concatenate([hi, hi, lo], axis=0), preferred_element_type=F32)


def rmul(x, table):
    hi, lo = parted(x)
    return jnp.dot(jnp.concatenate([hi, hi, lo], axis=1), table, preferred_element_type=F32)


def exact_parts(x):
    hi = x.astype(BF16)
    rest = x - hi.astype(F32)
    mid = rest.astype(BF16)
    return hi, mid, (rest - mid.astype(F32)).astype(BF16)


def prop_left(re, im, table):
    h, q = HALF, HALF // 2
    x = jnp.concatenate(
        [jnp.concatenate([re[:h], im[:h]], axis=0), jnp.concatenate([re[h:], im[h:]], axis=0)], axis=1
    )
    y = lmul(table[0], x)
    v = lmul(table[1], jnp.concatenate([re[h : h + q], re[q:h], im[h : h + q], im[q:h]], axis=0))
    n = PROBE
    re = [y[:q, :n], y[q:h, :n] + v[q:h], y[:q, n:] + v[:q], y[q:h, n:]]
    im = [y[h : h + q, :n], y[h + q :, :n] + v[h + q :], y[h : h + q, n:] + v[h : h + q], y[h + q :, n:]]
    return jnp.concatenate(re, axis=0), jnp.concatenate(im, axis=0)


def prop_right(re, im, table):
    h, n = HALF, PROBE
    low = lax.broadcasted_iota(jnp.int32, (1, h), 1) < h // 2
    x = jnp.concatenate(
        [jnp.concatenate([re[:, :h], im[:, :h]], axis=1), jnp.concatenate([re[:, h:], im[:, h:]], axis=1)], axis=0
    )
    y = rmul(x, table[0])
    u = [jnp.where(low, z[:, h:], z[:, :h]) for z in (re, im)]
    v = rmul(jnp.concatenate(u, axis=1), table[1])
    out = []
    for at in (slice(0, h), slice(h, n)):
        out.append(
            jnp.concatenate(
                [y[:n, at] + jnp.where(low, 0.0, v[:, at]), y[n:, at] + jnp.where(low, v[:, at], 0.0)], axis=1
            )
        )
    return out


def place_of(scalars, slot):
    row = scalars[2 * slot]
    col = scalars[2 * slot + 1]
    row_base = pl.multiple_of(row // 8 * 8, 8)
    col_base = pl.multiple_of(col // 128 * 128, 128)
    return row_base, row - row_base, col_base, col - col_base


def window_of(field, part, place):
    row_base, row_off, col_base, col_off = place
    x = field[part, pl.ds(row_base, PROBE + 8), pl.ds(col_base, PROBE + 128)]
    x = pltpu.roll(x, (PROBE + 128 - col_off) % (PROBE + 128), 1)[:, :PROBE]
    return pltpu.roll(x, (PROBE + 8 - row_off) % (PROBE + 8), 0)[:PROBE]


def add_window(field, part, place, x):
    row_base, row_off, col_base, col_off = place
    x = jnp.concatenate([x, jnp.zeros((8, PROBE), F32)], axis=0)
    x = pltpu.roll(x, row_off, 0)
    x = jnp.concatenate([x, jnp.zeros((PROBE + 8, 128), F32)], axis=1)
    x = pltpu.roll(x, col_off, 1)
    at = (part, pl.ds(row_base, PROBE + 8), pl.ds(col_base, PROBE + 128))
    field[at] = field[at] + x


def fetch_field(layer, core, obj, right, low_a, low_b, diag, side, field, sems, meanwhile=None):
    n, t = PROBE, TILE
    copies = [
        pltpu.make_async_copy(obj.at[layer], field.at[:, :t, :t], sems.at[0]),
        pltpu.make_async_copy(right, field.at[:, :t, t:], sems.at[1]),
        pltpu.make_async_copy(low_a, field.at[:, t:, :n], sems.at[2]),
        pltpu.make_async_copy(low_b, field.at[:, t:, n:t], sems.at[3]),
    ]
    for copy in copies:
        copy.start()
    if meanwhile is not None:
        meanwhile()

    @pl.when(core == 0)
    def _():
        copy = pltpu.make_async_copy(side, field.at[:, t:, t:], sems.at[4])
        copy.start()
        copy.wait()

    @pl.when(core != 0)
    def _():
        copy = pltpu.make_async_copy(diag, field.at[:, t:, t:], sems.at[4])
        copy.start()
        copy.wait()

    for copy in copies:
        copy.wait()


def store_field(field, main, right, low_a, low_b, corner, sems):
    n, t = PROBE, TILE
    copies = [
        pltpu.make_async_copy(field.at[:, :t, t:], right, sems.at[0]),
        pltpu.make_async_copy(field.at[:, t:, n:t], low_b, sems.at[1]),
        pltpu.make_async_copy(field.at[:, t:, :n], low_a, sems.at[2]),
        pltpu.make_async_copy(field.at[:, t:, t:], corner, sems.at[3]),
        pltpu.make_async_copy(field.at[:, :t, :t], main, sems.at[4]),
    ]
    for copy in copies:
        copy.start()
    for copy in copies:
        copy.wait()


def amp_kernel(amp, perm_l, perm_r, out):
    hi, mid, lo = exact_parts(amp[0])
    y = jnp.dot(perm_l[...], jnp.concatenate([hi, mid, lo], axis=0), preferred_element_type=F32)
    hi, mid, lo = exact_parts(y)
    out[0] = jnp.dot(jnp.concatenate([hi, mid, lo], axis=1), perm_r[...], preferred_element_type=F32)


def out_kernel(
    scalars, obj, right, low_a, low_b, diag, side, mine, across, mine_other, across_other, table_l, table_r,
    psi, win, probe_rows, field, sems, probe_sem,
):
    slot = pl.program_id(0)
    probe = probe_rows.reshape(2, 2, PROBE, PROBE)

    @pl.when(slot == 0)
    def _():
        core, y_hi, z = scalars[13], scalars[14], scalars[15]
        copies = [
            pltpu.make_async_copy(src.at[k], probe_rows.at[:, :, z ^ k, y, c], probe_sem)
            for src, y, c in (
                (mine, y_hi, core),
                (across, 1 - y_hi, core),
                (mine_other, y_hi, 1 - core),
                (across_other, 1 - y_hi, 1 - core),
            )
            for k in range(4)
        ]
        for copy in copies:
            copy.start()
        fetch_field(0, core, obj, right, low_a, low_b, diag, side, field, sems)
        for copy in copies:
            copy.wait()

    @pl.when(slot < scalars[12])
    def _():
        place = place_of(scalars, slot)
        w_re = window_of(field, 0, place)
        w_im = window_of(field, 1, place)
        win[0, 0] = w_re
        win[0, 1] = w_im
        x = []
        for m in (0, 1):
            re = probe[m, 0] * w_re - probe[m, 1] * w_im
            im = probe[m, 0] * w_im + probe[m, 1] * w_re
            x.append(prop_left(re, im, table_l))
        for m in (0, 1):
            re, im = prop_right(*x[m], table_r)
            psi[0, m, 0] = re
            psi[0, m, 1] = im


def far_kernel(
    scalars, obj, right, low_a, low_b, diag, side, psi, amp, four_l, four_r, ruof_l, ruof_r, tw_row, tw_col,
    g_psi, g_main, g_right, g_low_a, g_low_b, g_corner, field, grad, win, gwin, sems,
):
    slot = pl.program_id(0)
    h, n = HALF, PROBE
    used = scalars[12]

    def load_window(at):
        place = place_of(scalars, at)
        win[0] = window_of(field, 0, place)
        win[1] = window_of(field, 1, place)

    def flush(at):
        place = place_of(scalars, at)
        add_window(grad, 0, place, gwin[0])
        add_window(grad, 1, place, gwin[1])

    @pl.when(slot == 0)
    def _():
        def clear():
            grad[...] = jnp.zeros_like(grad)
            gwin[...] = jnp.zeros_like(gwin)

        fetch_field(1, scalars[13], obj, right, low_a, low_b, diag, side, field, sems, clear)
        load_window(0)

    @pl.when(slot < used)
    def _():
        w_re, w_im = win[0], win[1]
        tr, ti = tw_row[0], tw_row[1]
        cr, ci = tw_col[0, 0:1], tw_col[1, 0:1]
        chi = {}

        def left(m, odd):
            if m not in chi:
                p_re, p_im = psi[0, m, 0], psi[0, m, 1]
                chi[m] = (p_re * w_re - p_im * w_im, p_re * w_im + p_im * w_re)
            re, im = chi[m]
            if odd:
                d_re, d_im = re[:h] - re[h:], im[:h] - im[h:]
                x = [d_re * tr - d_im * ti, d_re * ti + d_im * tr]
            else:
                x = [re[:h] + re[h:], im[:h] + im[h:]]
            return lmul(four_l[...], jnp.concatenate(x, axis=0))

        def across(y):
            re, im = y[:h], y[h:]
            d_re, d_im = re[:, :h] - re[:, h:], im[:, :h] - im[:, h:]
            even = jnp.concatenate([re[:, :h] + re[:, h:], im[:, :h] + im[:, h:]], axis=1)
            odd = jnp.concatenate([d_re * cr - d_im * ci, d_re * ci + d_im * cr], axis=1)
            return rmul(jnp.concatenate([even, odd], axis=0), four_r[...])

        def slope_of(z0, z1, rows):
            sq = z0 * z0 + z1 * z1
            total = sq[:, :h] + sq[:, h:] + 1.0
            both = jnp.concatenate([amp[0, rows, :h], amp[0, rows, h:]], axis=0)
            slope = 2.0 - 2.0 * both * lax.rsqrt(total)
            return jnp.concatenate([slope, slope], axis=1)

        def back_across(z):
            y = rmul(z, ruof_r[...])
            q_re = y[h:, :h] * cr + y[h:, h:] * ci
            q_im = y[h:, h:] * cr - y[h:, :h] * ci
            re = jnp.concatenate([y[:h, :h] + q_re, y[:h, :h] - q_re], axis=1)
            im = jnp.concatenate([y[:h, h:] + q_im, y[:h, h:] - q_im], axis=1)
            return jnp.concatenate([re, im], axis=0)

        def finish(m, y_even, y_odd):
            q_re = y_odd[:h] * tr + y_odd[h:] * ti
            q_im = y_odd[h:] * tr - y_odd[:h] * ti
            re = jnp.concatenate([y_even[:h] + q_re, y_even[:h] - q_re], axis=0)
            im = jnp.concatenate([y_even[h:] + q_im, y_even[h:] - q_im], axis=0)
            g_psi[0, m, 0] = w_re * re + w_im * im
            g_psi[0, m, 1] = w_re * im - w_im * re
            p_re, p_im = psi[0, m, 0], psi[0, m, 1]
            return p_re * re + p_im * im, p_re * im - p_im * re

        back = ruof_l[...]
        l0e = left(0, 0)
        l1e = left(1, 0)
        l0o = left(0, 1)
        z0e = across(l0e)
        l1o = left(1, 1)
        z1e = across(l1e)
        slope_e = slope_of(z0e, z1e, slice(0, h))
        z0o = across(l0o)
        b0e = back_across(z0e * slope_e)
        z1o = across(l1o)
        flush(jnp.maximum(slot - 1, 0))
        slope_o = slope_of(z0o, z1o, slice(h, n))
        load_window(jnp.minimum(slot + 1, SLOTS - 1))
        b1e = back_across(z1e * slope_e)
        a0e = lmul(back, b0e)
        b0o = back_across(z0o * slope_o)
        a1e = lmul(back, b1e)
        b1o = back_across(z1o * slope_o)
        a0o = lmul(back, b0o)
        a1o = lmul(back, b1o)
        u_re, u_im = finish(0, a0e, a0o)
        v_re, v_im = finish(1, a1e, a1o)
        gwin[0] = u_re + v_re
        gwin[1] = u_im + v_im

    @pl.when(slot == pl.num_programs(0) - 1)
    def _():
        flush(used - 1)
        store_field(grad, g_main, g_right, g_low_a, g_low_b, g_corner, sems)


def home_kernel(
    scalars, win, g_psi, probe, table_l, table_r,
    g_probe, g_main, g_right, g_low_a, g_low_b, g_corner, grad, sems,
):
    slot = pl.program_id(0)

    @pl.when(slot == 0)
    def _():
        grad[...] = jnp.zeros_like(grad)
        g_probe[...] = jnp.zeros_like(g_probe)

    @pl.when(slot < scalars[12])
    def _():
        place = place_of(scalars, slot)
        x = [prop_left(g_psi[0, m, 0], g_psi[0, m, 1], table_l) for m in (0, 1)]
        w_re, w_im = win[0, 0], win[0, 1]
        gw_re = gw_im = None
        for m in (0, 1):
            re, im = prop_right(*x[m], table_r)
            p_re, p_im = probe[m, 0], probe[m, 1]
            a_re = p_re * re + p_im * im
            a_im = p_re * im - p_im * re
            gw_re = a_re if m == 0 else gw_re + a_re
            gw_im = a_im if m == 0 else gw_im + a_im
            g_probe[m, 0] += w_re * re + w_im * im
            g_probe[m, 1] += w_re * im - w_im * re
        add_window(grad, 0, place, gw_re)
        add_window(grad, 1, place, gw_im)

    @pl.when(slot == pl.num_programs(0) - 1)
    def _():
        store_field(grad, g_main, g_right, g_low_a, g_low_b, g_corner, sems)


def join_kernel(main, right, low_a, low_b, diag, *rest):
    out = rest[-1]
    n, h = PROBE, HALF
    i = pl.program_id(0)

    @pl.when(i < 2)
    def _():
        out[0, :, :, :n] = main[:, :, :n] + right[...] + low_a[...] + diag[...]
        out[0, :, :, n:] = main[:, :, n:] + low_b[...]

    @pl.when(i >= 2)
    def _():
        out[0, :, :, :n] = main[:, :, :n] + right[...]
        out[0, :, :, n:] = main[:, :, n:]


def whole(shape):
    return pl.BlockSpec(shape, lambda j, s: (0,) * len(shape))


def held():
    return pl.BlockSpec(memory_space=pltpu.VMEM)


def any_spec():
    return pl.BlockSpec(memory_space=pl.ANY)


def of_slot(shape):
    return pl.BlockSpec(
        (1,) + shape, lambda j, s: (jnp.minimum(j, s[12] - 1),) + (0,) * len(shape)
    )


def cost(flops, data):
    return pl.CostEstimate(flops=int(flops), bytes_accessed=int(data), transcendentals=0)


def params():
    return pltpu.CompilerParams(vmem_limit_bytes=VMEM_LIMIT)


FIELD_PARTS = [(2, TILE, TILE), (2, TILE, PROBE), (2, PROBE, PROBE), (2, PROBE, PROBE), (2, PROBE, PROBE)]


def sds(shape):
    return jax.ShapeDtypeStruct(shape, F32)


def permute_amplitudes(amp, tables):
    n = PROBE
    return pl.pallas_call(
        amp_kernel,
        grid=(SLOTS,),
        in_specs=[
            pl.BlockSpec((1, n, n), lambda j: (j, 0, 0)),
            pl.BlockSpec((n, 3 * n), lambda j: (0, 0)),
            pl.BlockSpec((3 * n, n), lambda j: (0, 0)),
        ],
        out_specs=pl.BlockSpec((1, n, n), lambda j: (j, 0, 0)),
        out_shape=sds((SLOTS, n, n)),
        compiler_params=params(),
        cost_estimate=cost(1.2e9, 4e6),
        name="order_amplitudes",
    )(amp, tables["perm_l"], tables["perm_r"])


def run_out(scalars, obj, halo, probe, tables):
    n = PROBE
    return pl.pallas_call(
        out_kernel,
        grid_spec=pltpu.PrefetchScalarGridSpec(
            num_scalar_prefetch=1,
            grid=(SLOTS,),
            in_specs=[any_spec()] * 10 + [held()] * 2,
            out_specs=[of_slot((2, 2, n, n)), of_slot((2, n, n)), whole((2, 2, 4, 2, 2, 16, n))],
            scratch_shapes=[
                pltpu.VMEM((2, 3 * n, 3 * n), F32),
                pltpu.SemaphoreType.DMA((5,)),
                pltpu.SemaphoreType.DMA,
            ],
        ),
        out_shape=[sds((SLOTS, 2, 2, n, n)), sds((SLOTS, 2, n, n)), sds((2, 2, 4, 2, 2, 16, n))],
        compiler_params=params(),
        cost_estimate=cost(6e10, 2e7),
        name="propagate_out",
    )(scalars, obj, *halo, *probe, tables["prop_l"], tables["prop_r"])


def run_far(scalars, obj, halo, psi, amp, tables):
    n = PROBE
    return pl.pallas_call(
        far_kernel,
        grid_spec=pltpu.PrefetchScalarGridSpec(
            num_scalar_prefetch=1,
            grid=(SLOTS,),
            in_specs=[any_spec()] * 6
            + [of_slot((2, 2, n, n)), of_slot((n, n))]
            + [held()] * 6,
            out_specs=[of_slot((2, 2, n, n))] + [any_spec()] * 5,
            scratch_shapes=[
                pltpu.VMEM((2, 3 * n, 3 * n), F32),
                pltpu.VMEM((2, 3 * n, 3 * n), F32),
                pltpu.VMEM((2, n, n), F32),
                pltpu.VMEM((2, n, n), F32),
                pltpu.SemaphoreType.DMA((5,)),
            ],
        ),
        out_shape=[sds((SLOTS, 2, 2, n, n))] + [sds(s) for s in FIELD_PARTS],
        compiler_params=params(),
        cost_estimate=cost(6e10, 2e7),
        name="far_field",
    )(
        scalars, obj, *halo, psi, amp,
        tables["four_l"], tables["four_r"], tables["ruof_l"], tables["ruof_r"],
        tables["tw_row"], tables["tw_col"],
    )


def run_home(scalars, win, g_psi, probe, tables):
    n = PROBE
    return pl.pallas_call(
        home_kernel,
        grid_spec=pltpu.PrefetchScalarGridSpec(
            num_scalar_prefetch=1,
            grid=(SLOTS,),
            in_specs=[
                of_slot((2, n, n)),
                of_slot((2, 2, n, n)),
                held(),
                held(),
                held(),
            ],
            out_specs=[whole((2, 2, n, n))] + [any_spec()] * 5,
            scratch_shapes=[pltpu.VMEM((2, 3 * n, 3 * n), F32), pltpu.SemaphoreType.DMA((5,))],
        ),
        out_shape=[sds((2, 2, n, n))] + [sds(s) for s in FIELD_PARTS],
        compiler_params=params(),
        cost_estimate=cost(6e10, 2e7),
        name="propagate_home",
    )(scalars, win, g_psi, probe, tables["back_l"], tables["back_r"])


def run_join(layer, main, arrived, into):
    n, h = PROBE, HALF
    top = lambda i: (0, jnp.minimum(i, 1), 0)
    extra = [] if into is None else [into]
    return pl.pallas_call(
        join_kernel,
        grid=(4,),
        in_specs=[
            pl.BlockSpec((2, h, TILE), lambda i: (0, i, 0)),
            pl.BlockSpec((2, h, n), lambda i: (0, i, 0)),
            pl.BlockSpec((2, h, n), top),
            pl.BlockSpec((2, h, n), top),
            pl.BlockSpec((2, h, n), top),
        ]
        + [pl.BlockSpec(memory_space=pl.ANY)] * len(extra),
        out_specs=pl.BlockSpec((1, 2, h, TILE), lambda i: (layer, 0, i, 0)),
        out_shape=sds((2, 2, TILE, TILE)),
        input_output_aliases={} if into is None else {5: 0},
        compiler_params=params(),
        cost_estimate=cost(1e6, 6e6),
        name="join_gradients",
    )(main, *arrived, *extra)


def solution(mesh):
    n_gx, n_gy = mesh.shape["gx"], mesh.shape["gy"]
    axes = tuple(mesh.axis_names)
    tables = make_tables()

    def number(gx, gy):
        return gx * n_gy + gy if axes == ("gx", "gy") else gy * n_gx + gx

    def send(x, target):
        pairs = []
        for gx in range(n_gx):
            for gy in range(n_gy):
                to = target(gx, gy)
                if to is not None and 0 <= to[0] < n_gx and 0 <= to[1] < n_gy:
                    pairs.append((number(gx, gy), number(*to)))
        return lax.ppermute(x, axes, pairs)

    def flip(gx_bits, gy_bits):
        return lambda gx, gy: (gx ^ gx_bits, gy ^ gy_bits)

    def pieces(obj, layer):
        n = PROBE
        return obj[layer, :, :n, :n], obj[layer, :, :, :n], obj[layer, :, :n, n:]

    def bring(corner, edge, low):
        low_a = send(corner, lambda gx, gy: (gx, gy - 1))
        right = send(edge, lambda gx, gy: (gx - 1, gy))
        low_b = send(low, lambda gx, gy: (gx, gy - 1))
        diag = send(corner, lambda gx, gy: (gx - 1, gy - 1) if gx % 2 == 0 else None)
        side = send(low_a, lambda gx, gy: (gx - 1, gy) if gx % 2 == 1 else None)
        return right, low_a, low_b, diag, side

    def take_back(right, low_a, low_b, corner):
        side = send(corner, lambda gx, gy: (gx + 1, gy) if gx % 2 == 0 else None)
        right = send(right, lambda gx, gy: (gx + 1, gy))
        low_b = send(low_b, lambda gx, gy: (gx, gy + 1))
        diag = send(corner, lambda gx, gy: (gx + 1, gy + 1) if gx % 2 == 1 else None)
        low_a = send(low_a + side, lambda gx, gy: (gx, gy + 1))
        return right, low_a, low_b, diag

    def gather_probe(probe):
        return jnp.stack([probe] + [send(probe, flip(4 * k, 0)) for k in (1, 2, 3)])

    def reduce_chip(grad):
        gx = lax.axis_index("gx")
        core, z = gx % 2, gx // 4
        rows = PROBE // n_gx
        parts = jnp.transpose(grad.reshape(2, 2, 4, 2, 2, rows, PROBE), (4, 2, 3, 0, 1, 5, 6))
        keep = jnp.where(core == 0, parts[0], parts[1])
        give = jnp.where(core == 0, parts[1], parts[0])
        return keep + send(give, flip(1, 0))

    def halved(part, bit, there):
        keep = jnp.where(bit == 0, part[0], part[1])
        give = jnp.where(bit == 0, part[1], part[0])
        return keep + send(give, there)

    def halved(part, bit, there):
        keep = jnp.where(bit == 0, part[0], part[1])
        give = jnp.where(bit == 0, part[1], part[0])
        return keep + send(give, there)

    def reduce_rest(part):
        gx = lax.axis_index("gx")
        z = gx // 4
        part = halved(part.reshape(2, 2, *part.shape[1:]), z // 2, flip(8, 0))
        part = halved(part, z % 2, flip(4, 0))
        for bit in (2, 4):
            part = part + send(part, flip(0, bit))
        part = halved(part, gx // 2 % 2, flip(2, 1))
        return part + send(part, flip(0, 1))

    def on_device(obj, probe, positions, counts, amplitudes):
        gx = lax.axis_index("gx").astype(jnp.int32)
        scalars = jnp.concatenate(
            [positions.reshape(2 * SLOTS), counts.reshape(1), jnp.stack([gx & 1, gx >> 1 & 1, gx >> 2])]
        )
        pieces_0, mine = lax.optimization_barrier((pieces(obj, 0), gather_probe(probe)))
        halo_0 = bring(*pieces_0)
        probe_parts = mine, send(mine, flip(2, 1))
        amp = permute_amplitudes(amplitudes[0, 0], tables)
        pieces_1, halo_0, amp, probe_parts = lax.optimization_barrier((pieces(obj, 1), halo_0, amp, probe_parts))
        probe_parts = [*probe_parts, *(send(x, flip(1, 0)) for x in probe_parts)]
        halo_1 = bring(*pieces_1)
        psi, win, probe_rows = run_out(scalars, obj, halo_0, probe_parts, tables)
        probe_full = probe_rows.reshape(2, 2, PROBE, PROBE)
        g_psi, main_1, *edges_1 = run_far(scalars, obj, halo_1, psi, amp, tables)
        back_1 = take_back(*edges_1)
        used = counts[0, 0] > 0

        def home(operands):
            g_probe, *fields = run_home(*operands, tables)
            return reduce_chip(g_probe), *fields

        def idle(operands):
            return tuple(jnp.zeros(x.shape, x.dtype) for x in jax.eval_shape(home, operands))

        part, main_0, *edges_0 = lax.cond(used, home, idle, (scalars, win, g_psi, probe_full))
        edges_0, part, back_1 = lax.optimization_barrier((edges_0, part, back_1))
        back_0 = take_back(*edges_0)

        def rest(operands):
            part, main, back = operands
            return reduce_rest(part), run_join(1, main, back, None)

        def nothing(operands):
            return tuple(jnp.zeros(x.shape, x.dtype) for x in jax.eval_shape(rest, operands))

        probe_grad, grad = lax.cond(used, rest, nothing, (part, main_1, back_1))
        grad = run_join(0, main_0, back_0, grad)
        return grad, probe_grad

    return jax.shard_map(
        on_device,
        mesh=mesh,
        in_specs=(
            P(None, None, "gy", "gx"),
            P(None, None, "gx", None),
            P("gy", "gx", None, None),
            P("gy", "gx"),
            P("gy", "gx", None, None, None),
        ),
        out_specs=(P(None, None, "gy", "gx"), P(None, None, "gx", None)),
        check_vma=False,
    )
```

```python
import functools
import math

import jax
import jax.numpy as jnp
import numpy as np
from jax import lax
from jax.experimental import pallas as pl
from jax.experimental.pallas import tpu as pltpu
from jax.sharding import PartitionSpec as P

BAND = 48
PROBE = 256
HALF = 128
TILE = 512
SLOTS = 6
F32 = jnp.float32
BF16 = jnp.bfloat16
VMEM_LIMIT = 60 * 1024 * 1024


def split_table(mat):
    hi = mat.astype(BF16)
    lo = (mat - hi.astype(np.float64)).astype(BF16)
    return hi, lo


def left_table(mat):
    hi, lo = split_table(mat)
    return np.concatenate([hi, lo, hi], axis=1)


def right_table(mat):
    hi, lo = split_table(mat)
    return np.concatenate([hi, lo, hi], axis=0)


def make_tables():
    index = np.arange(PROBE)
    offset = (index[:, None] - index[None, :]).astype(np.float64)
    prop = np.where(np.abs(offset) <= BAND, np.exp(1j * np.pi * offset**2 / (2 * BAND)), 0)
    prop = prop / math.sqrt(2 * BAND + 1)
    half = np.arange(HALF)
    four = np.exp(-2j * np.pi * ((half[:, None] * half[None, :]) % HALF) / HALF) / math.sqrt(PROBE)
    twist = np.exp(-2j * np.pi * half / PROBE)

    def from_left(mat):
        return np.block([[mat.real, -mat.imag], [mat.imag, mat.real]])

    def from_right(mat):
        return from_left(mat).T

    near = np.arange(PROBE) < HALF
    edge = (np.arange(PROBE) + HALF // 2) // HALF == 1
    cross = np.where(near[:, None] != near[None, :], prop, 0)
    assert not cross[~edge].any() and not cross[:, ~edge].any()

    def pair(table, embed, mat):
        other = np.zeros((HALF, HALF), complex)
        for a in range(HALF):
            for b in range(HALF):
                to, of = (a + HALF, b) if a < HALF // 2 else (a, b + HALF)
                if (b >= HALF // 2) == (a < HALF // 2):
                    other[a, b] = mat[to, of]
        return np.stack([table(embed(mat[:HALF, :HALF])), table(embed(other))])

    order = np.concatenate([np.arange(0, PROBE, 2), np.arange(1, PROBE, 2)])
    perm = np.zeros((PROBE, PROBE))
    perm[np.arange(PROBE), order] = 1
    return {
        "prop_l": pair(left_table, from_left, prop),
        "prop_r": pair(right_table, from_right, prop),
        "back_l": pair(left_table, from_left, prop.conj()),
        "back_r": pair(right_table, from_right, prop.conj()),
        "four_l": left_table(from_left(four)),
        "four_r": right_table(from_right(four)),
        "ruof_l": left_table(from_left(four.conj())),
        "ruof_r": right_table(from_right(four.conj())),
        "tw_row": np.stack(
            [
                np.broadcast_to(twist.real[:, None], (HALF, PROBE)),
                np.broadcast_to(twist.imag[:, None], (HALF, PROBE)),
            ]
        ).astype(np.float32),
        "tw_col": np.stack(
            [
                np.broadcast_to(twist.real[None, :], (8, HALF)),
                np.broadcast_to(twist.imag[None, :], (8, HALF)),
            ]
        ).astype(np.float32),
        "perm_l": np.concatenate([perm] * 3, axis=1).astype(BF16),
        "perm_r": np.concatenate([perm.T] * 3, axis=0).astype(BF16),
    }


def parted(x):
    hi = x.astype(BF16)
    return hi, (x - hi.astype(F32)).astype(BF16)


def lmul(table, x):
    hi, lo = parted(x)
    return jnp.dot(table, jnp.concatenate([hi, hi, lo], axis=0), preferred_element_type=F32)


def rmul(x, table):
    hi, lo = parted(x)
    return jnp.dot(jnp.concatenate([hi, hi, lo], axis=1), table, preferred_element_type=F32)


def exact_parts(x):
    hi = x.astype(BF16)
    rest = x - hi.astype(F32)
    mid = rest.astype(BF16)
    return hi, mid, (rest - mid.astype(F32)).astype(BF16)


def prop_left(re, im, table):
    h, q = HALF, HALF // 2
    x = jnp.concatenate(
        [jnp.concatenate([re[:h], im[:h]], axis=0), jnp.concatenate([re[h:], im[h:]], axis=0)], axis=1
    )
    y = lmul(table[0], x)
    v = lmul(table[1], jnp.concatenate([re[h : h + q], re[q:h], im[h : h + q], im[q:h]], axis=0))
    n = PROBE
    re = [y[:q, :n], y[q:h, :n] + v[q:h], y[:q, n:] + v[:q], y[q:h, n:]]
    im = [y[h : h + q, :n], y[h + q :, :n] + v[h + q :], y[h : h + q, n:] + v[h : h + q], y[h + q :, n:]]
    return jnp.concatenate(re, axis=0), jnp.concatenate(im, axis=0)


def prop_right(re, im, table):
    h, n = HALF, PROBE
    low = lax.broadcasted_iota(jnp.int32, (1, h), 1) < h // 2
    x = jnp.concatenate(
        [jnp.concatenate([re[:, :h], im[:, :h]], axis=1), jnp.concatenate([re[:, h:], im[:, h:]], axis=1)], axis=0
    )
    y = rmul(x, table[0])
    u = [jnp.where(low, z[:, h:], z[:, :h]) for z in (re, im)]
    v = rmul(jnp.concatenate(u, axis=1), table[1])
    out = []
    for at in (slice(0, h), slice(h, n)):
        out.append(
            jnp.concatenate(
                [y[:n, at] + jnp.where(low, 0.0, v[:, at]), y[n:, at] + jnp.where(low, v[:, at], 0.0)], axis=1
            )
        )
    return out


def place_of(scalars, slot):
    row = scalars[2 * slot]
    col = scalars[2 * slot + 1]
    row_base = pl.multiple_of(row // 8 * 8, 8)
    col_base = pl.multiple_of(col // 128 * 128, 128)
    return row_base, row - row_base, col_base, col - col_base


def window_of(field, part, place):
    row_base, row_off, col_base, col_off = place
    x = field[part, pl.ds(row_base, PROBE + 8), pl.ds(col_base, PROBE + 128)]
    x = pltpu.roll(x, (PROBE + 128 - col_off) % (PROBE + 128), 1)[:, :PROBE]
    return pltpu.roll(x, (PROBE + 8 - row_off) % (PROBE + 8), 0)[:PROBE]


def add_window(field, part, place, x):
    row_base, row_off, col_base, col_off = place
    x = jnp.concatenate([x, jnp.zeros((8, PROBE), F32)], axis=0)
    x = pltpu.roll(x, row_off, 0)
    x = jnp.concatenate([x, jnp.zeros((PROBE + 8, 128), F32)], axis=1)
    x = pltpu.roll(x, col_off, 1)
    at = (part, pl.ds(row_base, PROBE + 8), pl.ds(col_base, PROBE + 128))
    field[at] = field[at] + x


def fetch_field(layer, core, obj, right, low_a, low_b, diag, side, field, sems, meanwhile=None):
    n, t = PROBE, TILE
    copies = [
        pltpu.make_async_copy(obj.at[layer], field.at[:, :t, :t], sems.at[0]),
        pltpu.make_async_copy(right, field.at[:, :t, t:], sems.at[1]),
        pltpu.make_async_copy(low_a, field.at[:, t:, :n], sems.at[2]),
        pltpu.make_async_copy(low_b, field.at[:, t:, n:t], sems.at[3]),
    ]
    for copy in copies:
        copy.start()
    if meanwhile is not None:
        meanwhile()

    @pl.when(core == 0)
    def _():
        copy = pltpu.make_async_copy(side, field.at[:, t:, t:], sems.at[4])
        copy.start()
        copy.wait()

    @pl.when(core != 0)
    def _():
        copy = pltpu.make_async_copy(diag, field.at[:, t:, t:], sems.at[4])
        copy.start()
        copy.wait()

    for copy in copies:
        copy.wait()


def store_field(field, main, right, low_a, low_b, corner, sems):
    n, t = PROBE, TILE
    copies = [
        pltpu.make_async_copy(field.at[:, :t, t:], right, sems.at[0]),
        pltpu.make_async_copy(field.at[:, t:, n:t], low_b, sems.at[1]),
        pltpu.make_async_copy(field.at[:, t:, :n], low_a, sems.at[2]),
        pltpu.make_async_copy(field.at[:, t:, t:], corner, sems.at[3]),
        pltpu.make_async_copy(field.at[:, :t, :t], main, sems.at[4]),
    ]
    for copy in copies:
        copy.start()
    for copy in copies:
        copy.wait()


def amp_kernel(amp, perm_l, perm_r, out):
    hi, mid, lo = exact_parts(amp[0])
    y = jnp.dot(perm_l[...], jnp.concatenate([hi, mid, lo], axis=0), preferred_element_type=F32)
    hi, mid, lo = exact_parts(y)
    out[0] = jnp.dot(jnp.concatenate([hi, mid, lo], axis=1), perm_r[...], preferred_element_type=F32)


def out_kernel(
    scalars, obj, right, low_a, low_b, diag, side, mine, across, mine_other, across_other, table_l, table_r,
    psi, win, probe_rows, field, sems, probe_sem,
):
    slot = pl.program_id(0)
    probe = probe_rows.reshape(2, 2, PROBE, PROBE)

    @pl.when(slot == 0)
    def _():
        core, y_hi, z = scalars[13], scalars[14], scalars[15]
        copies = [
            pltpu.make_async_copy(src.at[k], probe_rows.at[:, :, z ^ k, y, c], probe_sem)
            for src, y, c in (
                (mine, y_hi, core),
                (across, 1 - y_hi, core),
                (mine_other, y_hi, 1 - core),
                (across_other, 1 - y_hi, 1 - core),
            )
            for k in range(4)
        ]
        for copy in copies:
            copy.start()
        fetch_field(0, core, obj, right, low_a, low_b, diag, side, field, sems)
        for copy in copies:
            copy.wait()

    @pl.when(slot < scalars[12])
    def _():
        place = place_of(scalars, slot)
        w_re = window_of(field, 0, place)
        w_im = window_of(field, 1, place)
        win[0, 0] = w_re
        win[0, 1] = w_im
        x = []
        for m in (0, 1):
            re = probe[m, 0] * w_re - probe[m, 1] * w_im
            im = probe[m, 0] * w_im + probe[m, 1] * w_re
            x.append(prop_left(re, im, table_l))
        for m in (0, 1):
            re, im = prop_right(*x[m], table_r)
            psi[0, m, 0] = re
            psi[0, m, 1] = im


def far_kernel(
    scalars, obj, right, low_a, low_b, diag, side, psi, amp, four_l, four_r, ruof_l, ruof_r, tw_row, tw_col,
    g_psi, g_main, g_right, g_low_a, g_low_b, g_corner, field, grad, win, gwin, sems,
):
    slot = pl.program_id(0)
    h, n = HALF, PROBE
    used = scalars[12]

    def load_window(at):
        place = place_of(scalars, at)
        win[0] = window_of(field, 0, place)
        win[1] = window_of(field, 1, place)

    def flush(at):
        place = place_of(scalars, at)
        add_window(grad, 0, place, gwin[0])
        add_window(grad, 1, place, gwin[1])

    @pl.when(slot == 0)
    def _():
        def clear():
            grad[...] = jnp.zeros_like(grad)
            gwin[...] = jnp.zeros_like(gwin)

        fetch_field(1, scalars[13], obj, right, low_a, low_b, diag, side, field, sems, clear)
        load_window(0)

    @pl.when(slot < used)
    def _():
        w_re, w_im = win[0], win[1]
        tr, ti = tw_row[0], tw_row[1]
        cr, ci = tw_col[0, 0:1], tw_col[1, 0:1]
        chi = {}

        def left(m, odd):
            if m not in chi:
                p_re, p_im = psi[0, m, 0], psi[0, m, 1]
                chi[m] = (p_re * w_re - p_im * w_im, p_re * w_im + p_im * w_re)
            re, im = chi[m]
            if odd:
                d_re, d_im = re[:h] - re[h:], im[:h] - im[h:]
                x = [d_re * tr - d_im * ti, d_re * ti + d_im * tr]
            else:
                x = [re[:h] + re[h:], im[:h] + im[h:]]
            return lmul(four_l[...], jnp.concatenate(x, axis=0))

        def across(y):
            re, im = y[:h], y[h:]
            d_re, d_im = re[:, :h] - re[:, h:], im[:, :h] - im[:, h:]
            even = jnp.concatenate([re[:, :h] + re[:, h:], im[:, :h] + im[:, h:]], axis=1)
            odd = jnp.concatenate([d_re * cr - d_im * ci, d_re * ci + d_im * cr], axis=1)
            return rmul(jnp.concatenate([even, odd], axis=0), four_r[...])

        def slope_of(z0, z1, rows):
            sq = z0 * z0 + z1 * z1
            total = sq[:, :h] + sq[:, h:] + 1.0
            both = jnp.concatenate([amp[0, rows, :h], amp[0, rows, h:]], axis=0)
            slope = 2.0 - 2.0 * both * lax.rsqrt(total)
            return jnp.concatenate([slope, slope], axis=1)

        def back_across(z):
            y = rmul(z, ruof_r[...])
            q_re = y[h:, :h] * cr + y[h:, h:] * ci
            q_im = y[h:, h:] * cr - y[h:, :h] * ci
            re = jnp.concatenate([y[:h, :h] + q_re, y[:h, :h] - q_re], axis=1)
            im = jnp.concatenate([y[:h, h:] + q_im, y[:h, h:] - q_im], axis=1)
            return jnp.concatenate([re, im], axis=0)

        def finish(m, y_even, y_odd):
            q_re = y_odd[:h] * tr + y_odd[h:] * ti
            q_im = y_odd[h:] * tr - y_odd[:h] * ti
            re = jnp.concatenate([y_even[:h] + q_re, y_even[:h] - q_re], axis=0)
            im = jnp.concatenate([y_even[h:] + q_im, y_even[h:] - q_im], axis=0)
            g_psi[0, m, 0] = w_re * re + w_im * im
            g_psi[0, m, 1] = w_re * im - w_im * re
            p_re, p_im = psi[0, m, 0], psi[0, m, 1]
            return p_re * re + p_im * im, p_re * im - p_im * re

        back = ruof_l[...]
        l0e = left(0, 0)
        l1e = left(1, 0)
        l0o = left(0, 1)
        z0e = across(l0e)
        l1o = left(1, 1)
        z1e = across(l1e)
        slope_e = slope_of(z0e, z1e, slice(0, h))
        z0o = across(l0o)
        b0e = back_across(z0e * slope_e)
        z1o = across(l1o)
        flush(jnp.maximum(slot - 1, 0))
        slope_o = slope_of(z0o, z1o, slice(h, n))
        load_window(jnp.minimum(slot + 1, SLOTS - 1))
        b1e = back_across(z1e * slope_e)
        a0e = lmul(back, b0e)
        b0o = back_across(z0o * slope_o)
        a1e = lmul(back, b1e)
        b1o = back_across(z1o * slope_o)
        a0o = lmul(back, b0o)
        a1o = lmul(back, b1o)
        u_re, u_im = finish(0, a0e, a0o)
        v_re, v_im = finish(1, a1e, a1o)
        gwin[0] = u_re + v_re
        gwin[1] = u_im + v_im

    @pl.when(slot == pl.num_programs(0) - 1)
    def _():
        flush(used - 1)
        store_field(grad, g_main, g_right, g_low_a, g_low_b, g_corner, sems)


def home_kernel(
    scalars, win, g_psi, probe, table_l, table_r,
    g_probe, g_main, g_right, g_low_a, g_low_b, g_corner, grad, sems,
):
    slot = pl.program_id(0)

    @pl.when(slot == 0)
    def _():
        grad[...] = jnp.zeros_like(grad)
        g_probe[...] = jnp.zeros_like(g_probe)

    @pl.when(slot < scalars[12])
    def _():
        place = place_of(scalars, slot)
        x = [prop_left(g_psi[0, m, 0], g_psi[0, m, 1], table_l) for m in (0, 1)]
        w_re, w_im = win[0, 0], win[0, 1]
        gw_re = gw_im = None
        for m in (0, 1):
            re, im = prop_right(*x[m], table_r)
            p_re, p_im = probe[m, 0], probe[m, 1]
            a_re = p_re * re + p_im * im
            a_im = p_re * im - p_im * re
            gw_re = a_re if m == 0 else gw_re + a_re
            gw_im = a_im if m == 0 else gw_im + a_im
            g_probe[m, 0] += w_re * re + w_im * im
            g_probe[m, 1] += w_re * im - w_im * re
        add_window(grad, 0, place, gw_re)
        add_window(grad, 1, place, gw_im)

    @pl.when(slot == pl.num_programs(0) - 1)
    def _():
        store_field(grad, g_main, g_right, g_low_a, g_low_b, g_corner, sems)


def join_kernel(main, right, low_a, low_b, diag, *rest):
    out = rest[-1]
    n, h = PROBE, HALF
    i = pl.program_id(0)

    @pl.when(i < 2)
    def _():
        out[0, :, :, :n] = main[:, :, :n] + right[...] + low_a[...] + diag[...]
        out[0, :, :, n:] = main[:, :, n:] + low_b[...]

    @pl.when(i >= 2)
    def _():
        out[0, :, :, :n] = main[:, :, :n] + right[...]
        out[0, :, :, n:] = main[:, :, n:]


def whole(shape):
    return pl.BlockSpec(shape, lambda j, s: (0,) * len(shape))


def held():
    return pl.BlockSpec(memory_space=pltpu.VMEM)


def any_spec():
    return pl.BlockSpec(memory_space=pl.ANY)


def of_slot(shape):
    return pl.BlockSpec(
        (1,) + shape, lambda j, s: (jnp.minimum(j, s[12] - 1),) + (0,) * len(shape)
    )


def cost(flops, data):
    return pl.CostEstimate(flops=int(flops), bytes_accessed=int(data), transcendentals=0)


def params():
    return pltpu.CompilerParams(vmem_limit_bytes=VMEM_LIMIT)


FIELD_PARTS = [(2, TILE, TILE), (2, TILE, PROBE), (2, PROBE, PROBE), (2, PROBE, PROBE), (2, PROBE, PROBE)]


def sds(shape):
    return jax.ShapeDtypeStruct(shape, F32)


def permute_amplitudes(amp, tables):
    n = PROBE
    return pl.pallas_call(
        amp_kernel,
        grid=(SLOTS,),
        in_specs=[
            pl.BlockSpec((1, n, n), lambda j: (j, 0, 0)),
            pl.BlockSpec((n, 3 * n), lambda j: (0, 0)),
            pl.BlockSpec((3 * n, n), lambda j: (0, 0)),
        ],
        out_specs=pl.BlockSpec((1, n, n), lambda j: (j, 0, 0)),
        out_shape=sds((SLOTS, n, n)),
        compiler_params=params(),
        cost_estimate=cost(1.2e9, 4e6),
        name="order_amplitudes",
    )(amp, tables["perm_l"], tables["perm_r"])


def run_out(scalars, obj, halo, probe, tables):
    n = PROBE
    return pl.pallas_call(
        out_kernel,
        grid_spec=pltpu.PrefetchScalarGridSpec(
            num_scalar_prefetch=1,
            grid=(SLOTS,),
            in_specs=[any_spec()] * 10 + [held()] * 2,
            out_specs=[of_slot((2, 2, n, n)), of_slot((2, n, n)), whole((2, 2, 4, 2, 2, 16, n))],
            scratch_shapes=[
                pltpu.VMEM((2, 3 * n, 3 * n), F32),
                pltpu.SemaphoreType.DMA((5,)),
                pltpu.SemaphoreType.DMA,
            ],
        ),
        out_shape=[sds((SLOTS, 2, 2, n, n)), sds((SLOTS, 2, n, n)), sds((2, 2, 4, 2, 2, 16, n))],
        compiler_params=params(),
        cost_estimate=cost(6e10, 2e7),
        name="propagate_out",
    )(scalars, obj, *halo, *probe, tables["prop_l"], tables["prop_r"])


def run_far(scalars, obj, halo, psi, amp, tables):
    n = PROBE
    return pl.pallas_call(
        far_kernel,
        grid_spec=pltpu.PrefetchScalarGridSpec(
            num_scalar_prefetch=1,
            grid=(SLOTS,),
            in_specs=[any_spec()] * 6
            + [of_slot((2, 2, n, n)), of_slot((n, n))]
            + [held()] * 6,
            out_specs=[of_slot((2, 2, n, n))] + [any_spec()] * 5,
            scratch_shapes=[
                pltpu.VMEM((2, 3 * n, 3 * n), F32),
                pltpu.VMEM((2, 3 * n, 3 * n), F32),
                pltpu.VMEM((2, n, n), F32),
                pltpu.VMEM((2, n, n), F32),
                pltpu.SemaphoreType.DMA((5,)),
            ],
        ),
        out_shape=[sds((SLOTS, 2, 2, n, n))] + [sds(s) for s in FIELD_PARTS],
        compiler_params=params(),
        cost_estimate=cost(6e10, 2e7),
        name="far_field",
    )(
        scalars, obj, *halo, psi, amp,
        tables["four_l"], tables["four_r"], tables["ruof_l"], tables["ruof_r"],
        tables["tw_row"], tables["tw_col"],
    )


def run_home(scalars, win, g_psi, probe, tables):
    n = PROBE
    return pl.pallas_call(
        home_kernel,
        grid_spec=pltpu.PrefetchScalarGridSpec(
            num_scalar_prefetch=1,
            grid=(SLOTS,),
            in_specs=[
                of_slot((2, n, n)),
                of_slot((2, 2, n, n)),
                held(),
                held(),
                held(),
            ],
            out_specs=[whole((2, 2, n, n))] + [any_spec()] * 5,
            scratch_shapes=[pltpu.VMEM((2, 3 * n, 3 * n), F32), pltpu.SemaphoreType.DMA((5,))],
        ),
        out_shape=[sds((2, 2, n, n))] + [sds(s) for s in FIELD_PARTS],
        compiler_params=params(),
        cost_estimate=cost(6e10, 2e7),
        name="propagate_home",
    )(scalars, win, g_psi, probe, tables["back_l"], tables["back_r"])


def run_join(layer, main, arrived, into):
    n, h = PROBE, HALF
    top = lambda i: (0, jnp.minimum(i, 1), 0)
    extra = [] if into is None else [into]
    return pl.pallas_call(
        join_kernel,
        grid=(4,),
        in_specs=[
            pl.BlockSpec((2, h, TILE), lambda i: (0, i, 0)),
            pl.BlockSpec((2, h, n), lambda i: (0, i, 0)),
            pl.BlockSpec((2, h, n), top),
            pl.BlockSpec((2, h, n), top),
            pl.BlockSpec((2, h, n), top),
        ]
        + [pl.BlockSpec(memory_space=pl.ANY)] * len(extra),
        out_specs=pl.BlockSpec((1, 2, h, TILE), lambda i: (layer, 0, i, 0)),
        out_shape=sds((2, 2, TILE, TILE)),
        input_output_aliases={} if into is None else {5: 0},
        compiler_params=params(),
        cost_estimate=cost(1e6, 6e6),
        name="join_gradients",
    )(main, *arrived, *extra)


def solution(mesh):
    n_gx, n_gy = mesh.shape["gx"], mesh.shape["gy"]
    axes = tuple(mesh.axis_names)
    tables = make_tables()

    def number(gx, gy):
        return gx * n_gy + gy if axes == ("gx", "gy") else gy * n_gx + gx

    def send(x, target):
        pairs = []
        for gx in range(n_gx):
            for gy in range(n_gy):
                to = target(gx, gy)
                if to is not None and 0 <= to[0] < n_gx and 0 <= to[1] < n_gy:
                    pairs.append((number(gx, gy), number(*to)))
        return lax.ppermute(x, axes, pairs)

    def flip(gx_bits, gy_bits):
        return lambda gx, gy: (gx ^ gx_bits, gy ^ gy_bits)

    def pieces(obj, layer):
        n = PROBE
        return obj[layer, :, :n, :n], obj[layer, :, :, :n], obj[layer, :, :n, n:]

    def bring(corner, edge, low):
        low_a = send(corner, lambda gx, gy: (gx, gy - 1))
        right = send(edge, lambda gx, gy: (gx - 1, gy))
        low_b = send(low, lambda gx, gy: (gx, gy - 1))
        diag = send(corner, lambda gx, gy: (gx - 1, gy - 1) if gx % 2 == 0 else None)
        return right, low_a, low_b, diag

    def bring_side(low_a):
        return send(low_a, lambda gx, gy: (gx - 1, gy) if gx % 2 == 1 else None)

    def take_back(right, low_a, low_b, corner):
        side = send(corner, lambda gx, gy: (gx + 1, gy) if gx % 2 == 0 else None)
        right = send(right, lambda gx, gy: (gx + 1, gy))
        low_b = send(low_b, lambda gx, gy: (gx, gy + 1))
        diag = send(corner, lambda gx, gy: (gx + 1, gy + 1) if gx % 2 == 1 else None)
        low_a = send(low_a + side, lambda gx, gy: (gx, gy + 1))
        return right, low_a, low_b, diag

    def gather_probe(probe):
        return jnp.stack([probe] + [send(probe, flip(4 * k, 0)) for k in (1, 2, 3)])

    def reduce_chip(grad):
        gx = lax.axis_index("gx")
        core, z = gx % 2, gx // 4
        rows = PROBE // n_gx
        parts = jnp.transpose(grad.reshape(2, 2, 4, 2, 2, rows, PROBE), (4, 2, 3, 0, 1, 5, 6))
        keep = jnp.where(core == 0, parts[0], parts[1])
        give = jnp.where(core == 0, parts[1], parts[0])
        return keep + send(give, flip(1, 0))

    def halved(part, bit, there):
        keep = jnp.where(bit == 0, part[0], part[1])
        give = jnp.where(bit == 0, part[1], part[0])
        return keep + send(give, there)

    def halved(part, bit, there):
        keep = jnp.where(bit == 0, part[0], part[1])
        give = jnp.where(bit == 0, part[1], part[0])
        return keep + send(give, there)

    def reduce_rest(part):
        gx = lax.axis_index("gx")
        z = gx // 4
        part = halved(part, z % 2, flip(4, 0))
        for bit in (2, 4):
            part = part + send(part, flip(0, bit))
        part = halved(part, gx // 2 % 2, flip(2, 1))
        return part + send(part, flip(0, 1))

    def on_device(obj, probe, positions, counts, amplitudes):
        gx = lax.axis_index("gx").astype(jnp.int32)
        scalars = jnp.concatenate(
            [positions.reshape(2 * SLOTS), counts.reshape(1), jnp.stack([gx & 1, gx >> 1 & 1, gx >> 2])]
        )
        pieces_0, mine = lax.optimization_barrier((pieces(obj, 0), gather_probe(probe)))
        halo_0 = bring(*pieces_0)
        probe_parts = mine, send(mine, flip(2, 1))
        obj_late, low_a = lax.optimization_barrier((obj, halo_0[1]))
        halo_0 = (halo_0[0], low_a, *halo_0[2:], bring_side(low_a))
        amp = permute_amplitudes(amplitudes[0, 0], tables)
        pieces_1, halo_0, amp, probe_parts = lax.optimization_barrier((pieces(obj_late, 1), halo_0, amp, probe_parts))
        probe_parts = [*probe_parts, *(send(x, flip(1, 0)) for x in probe_parts)]
        right, low_a, *others = bring(*pieces_1)
        psi, win, probe_rows = run_out(scalars, obj, halo_0, probe_parts, tables)
        low_a, psi = lax.optimization_barrier((low_a, psi))
        halo_1 = (right, low_a, *others, bring_side(low_a))
        probe_full = probe_rows.reshape(2, 2, PROBE, PROBE)
        g_psi, main_1, *edges_1 = run_far(scalars, obj, halo_1, psi, amp, tables)
        back_1 = take_back(*edges_1)
        used = counts[0, 0] > 0

        def home(operands):
            g_probe, *fields = run_home(*operands, tables)
            part = reduce_chip(g_probe)
            part = part.reshape(2, 2, *part.shape[1:])
            return halved(part, lax.axis_index("gx") // 8, flip(8, 0)), *fields

        def idle(operands):
            return tuple(jnp.zeros(x.shape, x.dtype) for x in jax.eval_shape(home, operands))

        part, main_0, *edges_0 = lax.cond(used, home, idle, (scalars, win, g_psi, probe_full))
        edges_0, part, back_1 = lax.optimization_barrier((edges_0, part, back_1))
        back_0 = take_back(*edges_0)

        def rest(operands):
            part, main, back = operands
            return reduce_rest(part), run_join(1, main, back, None)

        def nothing(operands):
            return tuple(jnp.zeros(x.shape, x.dtype) for x in jax.eval_shape(rest, operands))

        probe_grad, grad = lax.cond(used, rest, nothing, (part, main_1, back_1))
        grad = run_join(0, main_0, back_0, grad)
        return grad, probe_grad

    return jax.shard_map(
        on_device,
        mesh=mesh,
        in_specs=(
            P(None, None, "gy", "gx"),
            P(None, None, "gx", None),
            P("gy", "gx", None, None),
            P("gy", "gx"),
            P("gy", "gx", None, None, None),
        ),
        out_specs=(P(None, None, "gy", "gx"), P(None, None, "gx", None)),
        check_vma=False,
    )
```

```python
import functools
import math

import jax
import jax.numpy as jnp
import numpy as np
from jax import lax
from jax.experimental import pallas as pl
from jax.experimental.pallas import tpu as pltpu
from jax.sharding import PartitionSpec as P

BAND = 48
PROBE = 256
HALF = 128
TILE = 512
SLOTS = 6
F32 = jnp.float32
BF16 = jnp.bfloat16
VMEM_LIMIT = 48 * 1024 * 1024


def split_table(mat):
    hi = mat.astype(BF16)
    lo = (mat - hi.astype(np.float64)).astype(BF16)
    return hi, lo


def left_table(mat):
    hi, lo = split_table(mat)
    return np.concatenate([hi, lo, hi], axis=1)


def right_table(mat):
    hi, lo = split_table(mat)
    return np.concatenate([hi, lo, hi], axis=0)


def make_tables():
    index = np.arange(PROBE)
    offset = (index[:, None] - index[None, :]).astype(np.float64)
    prop = np.where(np.abs(offset) <= BAND, np.exp(1j * np.pi * offset**2 / (2 * BAND)), 0)
    prop = prop / math.sqrt(2 * BAND + 1)
    half = np.arange(HALF)
    four = np.exp(-2j * np.pi * ((half[:, None] * half[None, :]) % HALF) / HALF) / math.sqrt(PROBE)
    twist = np.exp(-2j * np.pi * half / PROBE)

    def from_left(mat):
        return np.block([[mat.real, -mat.imag], [mat.imag, mat.real]])

    def from_right(mat):
        return from_left(mat).T

    near = np.arange(PROBE) < HALF
    edge = (np.arange(PROBE) + HALF // 2) // HALF == 1
    cross = np.where(near[:, None] != near[None, :], prop, 0)
    assert not cross[~edge].any() and not cross[:, ~edge].any()

    def pair(table, embed, mat):
        other = np.zeros((HALF, HALF), complex)
        for a in range(HALF):
            for b in range(HALF):
                to, of = (a + HALF, b) if a < HALF // 2 else (a, b + HALF)
                if (b >= HALF // 2) == (a < HALF // 2):
                    other[a, b] = mat[to, of]
        return np.stack([table(embed(mat[:HALF, :HALF])), table(embed(other))])

    order = np.concatenate([np.arange(0, PROBE, 2), np.arange(1, PROBE, 2)])
    perm = np.zeros((PROBE, PROBE))
    perm[np.arange(PROBE), order] = 1
    return {
        "prop_l": pair(left_table, from_left, prop),
        "prop_r": pair(right_table, from_right, prop),
        "back_l": pair(left_table, from_left, prop.conj()),
        "back_r": pair(right_table, from_right, prop.conj()),
        "four_l": left_table(from_left(four)),
        "four_r": right_table(from_right(four)),
        "ruof_l": left_table(from_left(four.conj())),
        "ruof_r": right_table(from_right(four.conj())),
        "tw_row": np.stack(
            [
                np.broadcast_to(twist.real[:, None], (HALF, PROBE)),
                np.broadcast_to(twist.imag[:, None], (HALF, PROBE)),
            ]
        ).astype(np.float32),
        "tw_col": np.stack(
            [
                np.broadcast_to(twist.real[None, :], (8, HALF)),
                np.broadcast_to(twist.imag[None, :], (8, HALF)),
            ]
        ).astype(np.float32),
        "perm_l": np.concatenate([perm] * 3, axis=1).astype(BF16),
        "perm_r": np.concatenate([perm.T] * 3, axis=0).astype(BF16),
    }


def parted(x):
    hi = x.astype(BF16)
    return hi, (x - hi.astype(F32)).astype(BF16)


def lmul(table, x):
    hi, lo = parted(x)
    return jnp.dot(table, jnp.concatenate([hi, hi, lo], axis=0), preferred_element_type=F32)


def rmul(x, table):
    hi, lo = parted(x)
    return jnp.dot(jnp.concatenate([hi, hi, lo], axis=1), table, preferred_element_type=F32)


def exact_parts(x):
    hi = x.astype(BF16)
    rest = x - hi.astype(F32)
    mid = rest.astype(BF16)
    return hi, mid, (rest - mid.astype(F32)).astype(BF16)


def prop_left(re, im, table):
    h, q = HALF, HALF // 2
    x = jnp.concatenate(
        [jnp.concatenate([re[:h], im[:h]], axis=0), jnp.concatenate([re[h:], im[h:]], axis=0)], axis=1
    )
    y = lmul(table[0], x)
    v = lmul(table[1], jnp.concatenate([re[h : h + q], re[q:h], im[h : h + q], im[q:h]], axis=0))
    n = PROBE
    re = [y[:q, :n], y[q:h, :n] + v[q:h], y[:q, n:] + v[:q], y[q:h, n:]]
    im = [y[h : h + q, :n], y[h + q :, :n] + v[h + q :], y[h : h + q, n:] + v[h : h + q], y[h + q :, n:]]
    return jnp.concatenate(re, axis=0), jnp.concatenate(im, axis=0)


def prop_right(re, im, table):
    h, n = HALF, PROBE
    low = lax.broadcasted_iota(jnp.int32, (1, h), 1) < h // 2
    x = jnp.concatenate(
        [jnp.concatenate([re[:, :h], im[:, :h]], axis=1), jnp.concatenate([re[:, h:], im[:, h:]], axis=1)], axis=0
    )
    y = rmul(x, table[0])
    u = [jnp.where(low, z[:, h:], z[:, :h]) for z in (re, im)]
    v = rmul(jnp.concatenate(u, axis=1), table[1])
    out = []
    for at in (slice(0, h), slice(h, n)):
        out.append(
            jnp.concatenate(
                [y[:n, at] + jnp.where(low, 0.0, v[:, at]), y[n:, at] + jnp.where(low, v[:, at], 0.0)], axis=1
            )
        )
    return out


def place_of(scalars, slot):
    row = scalars[2 * slot]
    col = scalars[2 * slot + 1]
    row_base = pl.multiple_of(row // 8 * 8, 8)
    col_base = pl.multiple_of(col // 128 * 128, 128)
    return row_base, row - row_base, col_base, col - col_base


def window_of(field, part, place):
    row_base, row_off, col_base, col_off = place
    x = field[part, pl.ds(row_base, PROBE + 8), pl.ds(col_base, PROBE + 128)]
    x = pltpu.roll(x, (PROBE + 128 - col_off) % (PROBE + 128), 1)[:, :PROBE]
    return pltpu.roll(x, (PROBE + 8 - row_off) % (PROBE + 8), 0)[:PROBE]


def add_window(field, part, place, x):
    row_base, row_off, col_base, col_off = place
    x = jnp.concatenate([x, jnp.zeros((8, PROBE), F32)], axis=0)
    x = pltpu.roll(x, row_off, 0)
    x = jnp.concatenate([x, jnp.zeros((PROBE + 8, 128), F32)], axis=1)
    x = pltpu.roll(x, col_off, 1)
    at = (part, pl.ds(row_base, PROBE + 8), pl.ds(col_base, PROBE + 128))
    field[at] = field[at] + x


def fetch_field(layer, core, obj, right, low_a, low_b, diag, side, field, sems, meanwhile=None):
    n, t = PROBE, TILE
    copies = [
        pltpu.make_async_copy(obj.at[layer], field.at[:, :t, :t], sems.at[0]),
        pltpu.make_async_copy(right, field.at[:, :t, t:], sems.at[1]),
        pltpu.make_async_copy(low_a, field.at[:, t:, :n], sems.at[2]),
        pltpu.make_async_copy(low_b, field.at[:, t:, n:t], sems.at[3]),
    ]
    for copy in copies:
        copy.start()
    if meanwhile is not None:
        meanwhile()

    @pl.when(core == 0)
    def _():
        copy = pltpu.make_async_copy(side, field.at[:, t:, t:], sems.at[4])
        copy.start()
        copy.wait()

    @pl.when(core != 0)
    def _():
        copy = pltpu.make_async_copy(diag, field.at[:, t:, t:], sems.at[4])
        copy.start()
        copy.wait()

    for copy in copies:
        copy.wait()


def store_field(field, main, right, low_a, low_b, corner, sems):
    n, t = PROBE, TILE
    copies = [
        pltpu.make_async_copy(field.at[:, :t, t:], right, sems.at[0]),
        pltpu.make_async_copy(field.at[:, t:, n:t], low_b, sems.at[1]),
        pltpu.make_async_copy(field.at[:, t:, :n], low_a, sems.at[2]),
        pltpu.make_async_copy(field.at[:, t:, t:], corner, sems.at[3]),
        pltpu.make_async_copy(field.at[:, :t, :t], main, sems.at[4]),
    ]
    for copy in copies:
        copy.start()
    for copy in copies:
        copy.wait()


def amp_kernel(amp, perm_l, perm_r, out):
    hi, mid, lo = exact_parts(amp[0])
    y = jnp.dot(perm_l[...], jnp.concatenate([hi, mid, lo], axis=0), preferred_element_type=F32)
    hi, mid, lo = exact_parts(y)
    out[0] = jnp.dot(jnp.concatenate([hi, mid, lo], axis=1), perm_r[...], preferred_element_type=F32)


def out_kernel(
    scalars, obj, right, low_a, low_b, diag, side, mine, across, mine_other, across_other, table_l, table_r,
    psi, win, probe_rows, field, sems, probe_sem,
):
    slot = pl.program_id(0)
    probe = probe_rows.reshape(2, 2, PROBE, PROBE)

    @pl.when(slot == 0)
    def _():
        core, y_hi, z = scalars[13], scalars[14], scalars[15]
        copies = [
            pltpu.make_async_copy(src.at[k], probe_rows.at[:, :, z ^ k, y, c], probe_sem)
            for src, y, c in (
                (mine, y_hi, core),
                (across, 1 - y_hi, core),
                (mine_other, y_hi, 1 - core),
                (across_other, 1 - y_hi, 1 - core),
            )
            for k in range(4)
        ]
        for copy in copies:
            copy.start()
        fetch_field(0, core, obj, right, low_a, low_b, diag, side, field, sems)
        for copy in copies:
            copy.wait()

    @pl.when(slot < scalars[12])
    def _():
        place = place_of(scalars, slot)
        w_re = window_of(field, 0, place)
        w_im = window_of(field, 1, place)
        win[0, 0] = w_re
        win[0, 1] = w_im
        x = []
        for m in (0, 1):
            re = probe[m, 0] * w_re - probe[m, 1] * w_im
            im = probe[m, 0] * w_im + probe[m, 1] * w_re
            x.append(prop_left(re, im, table_l))
        for m in (0, 1):
            re, im = prop_right(*x[m], table_r)
            psi[0, m, 0] = re
            psi[0, m, 1] = im


def far_kernel(
    scalars, obj, right, low_a, low_b, diag, side, psi, amp, four_l, four_r, ruof_l, ruof_r, tw_row, tw_col,
    g_psi, g_main, g_right, g_low_a, g_low_b, g_corner, field, grad, win, gwin, sems,
):
    slot = pl.program_id(0)
    h, n = HALF, PROBE
    used = scalars[12]

    def load_window(at):
        place = place_of(scalars, at)
        win[0] = window_of(field, 0, place)
        win[1] = window_of(field, 1, place)

    def flush(at):
        place = place_of(scalars, at)
        add_window(grad, 0, place, gwin[0])
        add_window(grad, 1, place, gwin[1])

    @pl.when(slot == 0)
    def _():
        def clear():
            grad[...] = jnp.zeros_like(grad)
            gwin[...] = jnp.zeros_like(gwin)

        fetch_field(1, scalars[13], obj, right, low_a, low_b, diag, side, field, sems, clear)
        load_window(0)

    @pl.when(slot < used)
    def _():
        w_re, w_im = win[0], win[1]
        tr, ti = tw_row[0], tw_row[1]
        cr, ci = tw_col[0, 0:1], tw_col[1, 0:1]
        chi = {}

        def left(m, odd):
            if m not in chi:
                p_re, p_im = psi[0, m, 0], psi[0, m, 1]
                chi[m] = (p_re * w_re - p_im * w_im, p_re * w_im + p_im * w_re)
            re, im = chi[m]
            if odd:
                d_re, d_im = re[:h] - re[h:], im[:h] - im[h:]
                x = [d_re * tr - d_im * ti, d_re * ti + d_im * tr]
            else:
                x = [re[:h] + re[h:], im[:h] + im[h:]]
            return lmul(four_l[...], jnp.concatenate(x, axis=0))

        def across(y):
            re, im = y[:h], y[h:]
            d_re, d_im = re[:, :h] - re[:, h:], im[:, :h] - im[:, h:]
            even = jnp.concatenate([re[:, :h] + re[:, h:], im[:, :h] + im[:, h:]], axis=1)
            odd = jnp.concatenate([d_re * cr - d_im * ci, d_re * ci + d_im * cr], axis=1)
            return rmul(jnp.concatenate([even, odd], axis=0), four_r[...])

        def slope_of(z0, z1, rows):
            sq = z0 * z0 + z1 * z1
            total = sq[:, :h] + sq[:, h:] + 1.0
            both = jnp.concatenate([amp[0, rows, :h], amp[0, rows, h:]], axis=0)
            slope = 2.0 - 2.0 * both * lax.rsqrt(total)
            return jnp.concatenate([slope, slope], axis=1)

        def back_across(z):
            y = rmul(z, ruof_r[...])
            q_re = y[h:, :h] * cr + y[h:, h:] * ci
            q_im = y[h:, h:] * cr - y[h:, :h] * ci
            re = jnp.concatenate([y[:h, :h] + q_re, y[:h, :h] - q_re], axis=1)
            im = jnp.concatenate([y[:h, h:] + q_im, y[:h, h:] - q_im], axis=1)
            return jnp.concatenate([re, im], axis=0)

        def finish(m, y_even, y_odd):
            q_re = y_odd[:h] * tr + y_odd[h:] * ti
            q_im = y_odd[h:] * tr - y_odd[:h] * ti
            re = jnp.concatenate([y_even[:h] + q_re, y_even[:h] - q_re], axis=0)
            im = jnp.concatenate([y_even[h:] + q_im, y_even[h:] - q_im], axis=0)
            g_psi[0, m, 0] = w_re * re + w_im * im
            g_psi[0, m, 1] = w_re * im - w_im * re
            p_re, p_im = psi[0, m, 0], psi[0, m, 1]
            return p_re * re + p_im * im, p_re * im - p_im * re

        back = ruof_l[...]
        l0e = left(0, 0)
        l1e = left(1, 0)
        l0o = left(0, 1)
        z0e = across(l0e)
        l1o = left(1, 1)
        z1e = across(l1e)
        slope_e = slope_of(z0e, z1e, slice(0, h))
        z0o = across(l0o)
        b0e = back_across(z0e * slope_e)
        z1o = across(l1o)
        flush(jnp.maximum(slot - 1, 0))
        slope_o = slope_of(z0o, z1o, slice(h, n))
        load_window(jnp.minimum(slot + 1, SLOTS - 1))
        b1e = back_across(z1e * slope_e)
        a0e = lmul(back, b0e)
        b0o = back_across(z0o * slope_o)
        a1e = lmul(back, b1e)
        b1o = back_across(z1o * slope_o)
        a0o = lmul(back, b0o)
        a1o = lmul(back, b1o)
        u_re, u_im = finish(0, a0e, a0o)
        v_re, v_im = finish(1, a1e, a1o)
        gwin[0] = u_re + v_re
        gwin[1] = u_im + v_im

    @pl.when(slot == pl.num_programs(0) - 1)
    def _():
        flush(used - 1)
        store_field(grad, g_main, g_right, g_low_a, g_low_b, g_corner, sems)


def home_kernel(
    scalars, win, g_psi, probe, table_l, table_r,
    g_probe, g_main, g_right, g_low_a, g_low_b, g_corner, grad, sems,
):
    slot = pl.program_id(0)

    @pl.when(slot == 0)
    def _():
        grad[...] = jnp.zeros_like(grad)
        g_probe[...] = jnp.zeros_like(g_probe)

    @pl.when(slot < scalars[12])
    def _():
        place = place_of(scalars, slot)
        x = [prop_left(g_psi[0, m, 0], g_psi[0, m, 1], table_l) for m in (0, 1)]
        w_re, w_im = win[0, 0], win[0, 1]
        gw_re = gw_im = None
        for m in (0, 1):
            re, im = prop_right(*x[m], table_r)
            p_re, p_im = probe[m, 0], probe[m, 1]
            a_re = p_re * re + p_im * im
            a_im = p_re * im - p_im * re
            gw_re = a_re if m == 0 else gw_re + a_re
            gw_im = a_im if m == 0 else gw_im + a_im
            g_probe[m, 0] += w_re * re + w_im * im
            g_probe[m, 1] += w_re * im - w_im * re
        add_window(grad, 0, place, gw_re)
        add_window(grad, 1, place, gw_im)

    @pl.when(slot == pl.num_programs(0) - 1)
    def _():
        store_field(grad, g_main, g_right, g_low_a, g_low_b, g_corner, sems)


def join_kernel(main, right, low_a, low_b, diag, *rest):
    out = rest[-1]
    n, h = PROBE, HALF
    i = pl.program_id(0)

    @pl.when(i < 2)
    def _():
        out[0, :, :, :n] = main[:, :, :n] + right[...] + low_a[...] + diag[...]
        out[0, :, :, n:] = main[:, :, n:] + low_b[...]

    @pl.when(i >= 2)
    def _():
        out[0, :, :, :n] = main[:, :, :n] + right[...]
        out[0, :, :, n:] = main[:, :, n:]


def whole(shape):
    return pl.BlockSpec(shape, lambda j, s: (0,) * len(shape))


def held():
    return pl.BlockSpec(memory_space=pltpu.VMEM)


def any_spec():
    return pl.BlockSpec(memory_space=pl.ANY)


def of_slot(shape):
    return pl.BlockSpec(
        (1,) + shape, lambda j, s: (jnp.minimum(j, s[12] - 1),) + (0,) * len(shape)
    )


def cost(flops, data):
    return pl.CostEstimate(flops=int(flops), bytes_accessed=int(data), transcendentals=0)


def params():
    return pltpu.CompilerParams(vmem_limit_bytes=VMEM_LIMIT)


FIELD_PARTS = [(2, TILE, TILE), (2, TILE, PROBE), (2, PROBE, PROBE), (2, PROBE, PROBE), (2, PROBE, PROBE)]


def sds(shape):
    return jax.ShapeDtypeStruct(shape, F32)


def permute_amplitudes(amp, tables):
    n = PROBE
    return pl.pallas_call(
        amp_kernel,
        grid=(SLOTS,),
        in_specs=[
            pl.BlockSpec((1, n, n), lambda j: (j, 0, 0)),
            pl.BlockSpec((n, 3 * n), lambda j: (0, 0)),
            pl.BlockSpec((3 * n, n), lambda j: (0, 0)),
        ],
        out_specs=pl.BlockSpec((1, n, n), lambda j: (j, 0, 0)),
        out_shape=sds((SLOTS, n, n)),
        compiler_params=params(),
        cost_estimate=cost(1.2e9, 4e6),
        name="order_amplitudes",
    )(amp, tables["perm_l"], tables["perm_r"])


def run_out(scalars, obj, halo, probe, tables):
    n = PROBE
    return pl.pallas_call(
        out_kernel,
        grid_spec=pltpu.PrefetchScalarGridSpec(
            num_scalar_prefetch=1,
            grid=(SLOTS,),
            in_specs=[any_spec()] * 10 + [held()] * 2,
            out_specs=[of_slot((2, 2, n, n)), of_slot((2, n, n)), whole((2, 2, 4, 2, 2, 16, n))],
            scratch_shapes=[
                pltpu.VMEM((2, 3 * n, 3 * n), F32),
                pltpu.SemaphoreType.DMA((5,)),
                pltpu.SemaphoreType.DMA,
            ],
        ),
        out_shape=[sds((SLOTS, 2, 2, n, n)), sds((SLOTS, 2, n, n)), sds((2, 2, 4, 2, 2, 16, n))],
        compiler_params=params(),
        cost_estimate=cost(6e10, 2e7),
        name="propagate_out",
    )(scalars, obj, *halo, *probe, tables["prop_l"], tables["prop_r"])


def run_far(scalars, obj, halo, psi, amp, tables):
    n = PROBE
    return pl.pallas_call(
        far_kernel,
        grid_spec=pltpu.PrefetchScalarGridSpec(
            num_scalar_prefetch=1,
            grid=(SLOTS,),
            in_specs=[any_spec()] * 6
            + [of_slot((2, 2, n, n)), of_slot((n, n))]
            + [held()] * 6,
            out_specs=[of_slot((2, 2, n, n))] + [any_spec()] * 5,
            scratch_shapes=[
                pltpu.VMEM((2, 3 * n, 3 * n), F32),
                pltpu.VMEM((2, 3 * n, 3 * n), F32),
                pltpu.VMEM((2, n, n), F32),
                pltpu.VMEM((2, n, n), F32),
                pltpu.SemaphoreType.DMA((5,)),
            ],
        ),
        out_shape=[sds((SLOTS, 2, 2, n, n))] + [sds(s) for s in FIELD_PARTS],
        compiler_params=params(),
        cost_estimate=cost(6e10, 2e7),
        name="far_field",
    )(
        scalars, obj, *halo, psi, amp,
        tables["four_l"], tables["four_r"], tables["ruof_l"], tables["ruof_r"],
        tables["tw_row"], tables["tw_col"],
    )


def run_home(scalars, win, g_psi, probe, tables):
    n = PROBE
    return pl.pallas_call(
        home_kernel,
        grid_spec=pltpu.PrefetchScalarGridSpec(
            num_scalar_prefetch=1,
            grid=(SLOTS,),
            in_specs=[
                of_slot((2, n, n)),
                of_slot((2, 2, n, n)),
                held(),
                held(),
                held(),
            ],
            out_specs=[whole((2, 2, n, n))] + [any_spec()] * 5,
            scratch_shapes=[pltpu.VMEM((2, 3 * n, 3 * n), F32), pltpu.SemaphoreType.DMA((5,))],
        ),
        out_shape=[sds((2, 2, n, n))] + [sds(s) for s in FIELD_PARTS],
        compiler_params=params(),
        cost_estimate=cost(6e10, 2e7),
        name="propagate_home",
    )(scalars, win, g_psi, probe, tables["back_l"], tables["back_r"])


def run_join(layer, main, arrived, into):
    n, h = PROBE, HALF
    top = lambda i: (0, jnp.minimum(i, 1), 0)
    extra = [] if into is None else [into]
    return pl.pallas_call(
        join_kernel,
        grid=(4,),
        in_specs=[
            pl.BlockSpec((2, h, TILE), lambda i: (0, i, 0)),
            pl.BlockSpec((2, h, n), lambda i: (0, i, 0)),
            pl.BlockSpec((2, h, n), top),
            pl.BlockSpec((2, h, n), top),
            pl.BlockSpec((2, h, n), top),
        ]
        + [pl.BlockSpec(memory_space=pl.ANY)] * len(extra),
        out_specs=pl.BlockSpec((1, 2, h, TILE), lambda i: (layer, 0, i, 0)),
        out_shape=sds((2, 2, TILE, TILE)),
        input_output_aliases={} if into is None else {5: 0},
        compiler_params=params(),
        cost_estimate=cost(1e6, 6e6),
        name="join_gradients",
    )(main, *arrived, *extra)


def solution(mesh):
    n_gx, n_gy = mesh.shape["gx"], mesh.shape["gy"]
    axes = tuple(mesh.axis_names)
    tables = make_tables()

    def number(gx, gy):
        return gx * n_gy + gy if axes == ("gx", "gy") else gy * n_gx + gx

    def send(x, target):
        pairs = []
        for gx in range(n_gx):
            for gy in range(n_gy):
                to = target(gx, gy)
                if to is not None and 0 <= to[0] < n_gx and 0 <= to[1] < n_gy:
                    pairs.append((number(gx, gy), number(*to)))
        return lax.ppermute(x, axes, pairs)

    def flip(gx_bits, gy_bits):
        return lambda gx, gy: (gx ^ gx_bits, gy ^ gy_bits)

    def pieces(obj, layer):
        n = PROBE
        return obj[layer, :, :n, :n], obj[layer, :, :, :n], obj[layer, :, :n, n:]

    def bring(corner, edge, low):
        low_a = send(corner, lambda gx, gy: (gx, gy - 1))
        right = send(edge, lambda gx, gy: (gx - 1, gy))
        low_b = send(low, lambda gx, gy: (gx, gy - 1))
        diag = send(corner, lambda gx, gy: (gx - 1, gy - 1) if gx % 2 == 0 else None)
        return right, low_a, low_b, diag

    def bring_side(low_a):
        return send(low_a, lambda gx, gy: (gx - 1, gy) if gx % 2 == 1 else None)

    def take_back(right, low_a, low_b, corner):
        side = send(corner, lambda gx, gy: (gx + 1, gy) if gx % 2 == 0 else None)
        right = send(right, lambda gx, gy: (gx + 1, gy))
        low_b = send(low_b, lambda gx, gy: (gx, gy + 1))
        diag = send(corner, lambda gx, gy: (gx + 1, gy + 1) if gx % 2 == 1 else None)
        low_a = send(low_a + side, lambda gx, gy: (gx, gy + 1))
        return right, low_a, low_b, diag

    def gather_probe(probe):
        return jnp.stack([probe] + [send(probe, flip(4 * k, 0)) for k in (1, 2, 3)])

    def reduce_chip(grad):
        gx = lax.axis_index("gx")
        core, z = gx % 2, gx // 4
        rows = PROBE // n_gx
        parts = jnp.transpose(grad.reshape(2, 2, 4, 2, 2, rows, PROBE), (4, 2, 3, 0, 1, 5, 6))
        keep = jnp.where(core == 0, parts[0], parts[1])
        give = jnp.where(core == 0, parts[1], parts[0])
        return keep + send(give, flip(1, 0))

    def halved(part, bit, there):
        keep = jnp.where(bit == 0, part[0], part[1])
        give = jnp.where(bit == 0, part[1], part[0])
        return keep + send(give, there)

    def halved(part, bit, there):
        keep = jnp.where(bit == 0, part[0], part[1])
        give = jnp.where(bit == 0, part[1], part[0])
        return keep + send(give, there)

    def reduce_z(part):
        z = lax.axis_index("gx") // 4
        part = halved(part.reshape(2, 2, *part.shape[1:]), z // 2, flip(8, 0))
        return halved(part, z % 2, flip(4, 0))

    def reduce_xy(part):
        for bit in (2, 4):
            part = part + send(part, flip(0, bit))
        part = halved(part, lax.axis_index("gx") // 2 % 2, flip(2, 1))
        return part + send(part, flip(0, 1))

    def on_device(obj, probe, positions, counts, amplitudes):
        gx = lax.axis_index("gx").astype(jnp.int32)
        scalars = jnp.concatenate(
            [positions.reshape(2 * SLOTS), counts.reshape(1), jnp.stack([gx & 1, gx >> 1 & 1, gx >> 2])]
        )
        pieces_0, mine = lax.optimization_barrier((pieces(obj, 0), gather_probe(probe)))
        halo_0 = bring(*pieces_0)
        across = send(mine, flip(2, 1))
        probe_parts = [mine, across, send(mine, flip(1, 0)), send(across, flip(1, 0))]
        obj_late, low_a = lax.optimization_barrier((obj, halo_0[1]))
        halo_0 = (halo_0[0], low_a, *halo_0[2:], bring_side(low_a))
        amp = permute_amplitudes(amplitudes[0, 0], tables)
        pieces_1, halo_0, amp, probe_parts = lax.optimization_barrier((pieces(obj_late, 1), halo_0, amp, probe_parts))
        right, low_a, *others = bring(*pieces_1)
        psi, win, probe_rows = run_out(scalars, obj, halo_0, probe_parts, tables)
        low_a, psi = lax.optimization_barrier((low_a, psi))
        halo_1 = (right, low_a, *others, bring_side(low_a))
        probe_full = probe_rows.reshape(2, 2, PROBE, PROBE)
        g_psi, main_1, *edges_1 = run_far(scalars, obj, halo_1, psi, amp, tables)
        back_1 = take_back(*edges_1)
        used = counts[0, 0] > 0

        def home(operands):
            g_probe, *fields = run_home(*operands, tables)
            return reduce_chip(g_probe), *fields

        def idle(operands):
            return tuple(jnp.zeros(x.shape, x.dtype) for x in jax.eval_shape(home, operands))

        part, main_0, *edges_0 = lax.cond(used, home, idle, (scalars, win, g_psi, probe_full))
        edges_0, part, back_1 = lax.optimization_barrier((edges_0, part, back_1))
        back_0 = take_back(*edges_0)

        def rest(operands):
            part, main, back = operands
            part, grad = lax.optimization_barrier((reduce_z(part), run_join(1, main, back, None)))
            return reduce_xy(part), grad

        def nothing(operands):
            return tuple(jnp.zeros(x.shape, x.dtype) for x in jax.eval_shape(rest, operands))

        probe_grad, grad = lax.cond(used, rest, nothing, (part, main_1, back_1))
        grad = run_join(0, main_0, back_0, grad)
        return grad, probe_grad

    return jax.shard_map(
        on_device,
        mesh=mesh,
        in_specs=(
            P(None, None, "gy", "gx"),
            P(None, None, "gx", None),
            P("gy", "gx", None, None),
            P("gy", "gx"),
            P("gy", "gx", None, None, None),
        ),
        out_specs=(P(None, None, "gy", "gx"), P(None, None, "gx", None)),
        check_vma=False,
    )
```

```python
import functools
import math

import jax
import jax.numpy as jnp
import numpy as np
from jax import lax
from jax.experimental import pallas as pl
from jax.experimental.pallas import tpu as pltpu
from jax.sharding import PartitionSpec as P

BAND = 48
PROBE = 256
HALF = 128
TILE = 512
SLOTS = 6
F32 = jnp.float32
BF16 = jnp.bfloat16
VMEM_LIMIT = 48 * 1024 * 1024


def split_table(mat):
    hi = mat.astype(BF16)
    lo = (mat - hi.astype(np.float64)).astype(BF16)
    return hi, lo


def left_table(mat):
    hi, lo = split_table(mat)
    return np.concatenate([hi, lo, hi], axis=1)


def right_table(mat):
    hi, lo = split_table(mat)
    return np.concatenate([hi, lo, hi], axis=0)


def make_tables():
    index = np.arange(PROBE)
    offset = (index[:, None] - index[None, :]).astype(np.float64)
    prop = np.where(np.abs(offset) <= BAND, np.exp(1j * np.pi * offset**2 / (2 * BAND)), 0)
    prop = prop / math.sqrt(2 * BAND + 1)
    half = np.arange(HALF)
    four = np.exp(-2j * np.pi * ((half[:, None] * half[None, :]) % HALF) / HALF) / math.sqrt(PROBE)
    twist = np.exp(-2j * np.pi * half / PROBE)

    def from_left(mat):
        return np.block([[mat.real, -mat.imag], [mat.imag, mat.real]])

    def from_right(mat):
        return from_left(mat).T

    near = np.arange(PROBE) < HALF
    edge = (np.arange(PROBE) + HALF // 2) // HALF == 1
    cross = np.where(near[:, None] != near[None, :], prop, 0)
    assert not cross[~edge].any() and not cross[:, ~edge].any()

    def pair(table, embed, mat):
        other = np.zeros((HALF, HALF), complex)
        for a in range(HALF):
            for b in range(HALF):
                to, of = (a + HALF, b) if a < HALF // 2 else (a, b + HALF)
                if (b >= HALF // 2) == (a < HALF // 2):
                    other[a, b] = mat[to, of]
        return np.stack([table(embed(mat[:HALF, :HALF])), table(embed(other))])

    order = np.concatenate([np.arange(0, PROBE, 2), np.arange(1, PROBE, 2)])
    perm = np.zeros((PROBE, PROBE))
    perm[np.arange(PROBE), order] = 1
    return {
        "prop_l": pair(left_table, from_left, prop),
        "prop_r": pair(right_table, from_right, prop),
        "back_l": pair(left_table, from_left, prop.conj()),
        "back_r": pair(right_table, from_right, prop.conj()),
        "four_l": left_table(from_left(four)),
        "four_r": right_table(from_right(four)),
        "ruof_l": left_table(from_left(four.conj())),
        "ruof_r": right_table(from_right(four.conj())),
        "tw_row": np.stack(
            [
                np.broadcast_to(twist.real[:, None], (HALF, PROBE)),
                np.broadcast_to(twist.imag[:, None], (HALF, PROBE)),
            ]
        ).astype(np.float32),
        "tw_col": np.stack(
            [
                np.broadcast_to(twist.real[None, :], (8, HALF)),
                np.broadcast_to(twist.imag[None, :], (8, HALF)),
            ]
        ).astype(np.float32),
        "perm_l": np.concatenate([perm] * 3, axis=1).astype(BF16),
        "perm_r": np.concatenate([perm.T] * 3, axis=0).astype(BF16),
    }


def parted(x):
    hi = x.astype(BF16)
    return hi, (x - hi.astype(F32)).astype(BF16)


def lmul(table, x):
    hi, lo = parted(x)
    return jnp.dot(table, jnp.concatenate([hi, hi, lo], axis=0), preferred_element_type=F32)


def rmul(x, table):
    hi, lo = parted(x)
    return jnp.dot(jnp.concatenate([hi, hi, lo], axis=1), table, preferred_element_type=F32)


def exact_parts(x):
    hi = x.astype(BF16)
    rest = x - hi.astype(F32)
    mid = rest.astype(BF16)
    return hi, mid, (rest - mid.astype(F32)).astype(BF16)


def prop_left(re, im, table):
    h, q = HALF, HALF // 2
    x = jnp.concatenate(
        [jnp.concatenate([re[:h], im[:h]], axis=0), jnp.concatenate([re[h:], im[h:]], axis=0)], axis=1
    )
    y = lmul(table[0], x)
    v = lmul(table[1], jnp.concatenate([re[h : h + q], re[q:h], im[h : h + q], im[q:h]], axis=0))
    n = PROBE
    re = [y[:q, :n], y[q:h, :n] + v[q:h], y[:q, n:] + v[:q], y[q:h, n:]]
    im = [y[h : h + q, :n], y[h + q :, :n] + v[h + q :], y[h : h + q, n:] + v[h : h + q], y[h + q :, n:]]
    return jnp.concatenate(re, axis=0), jnp.concatenate(im, axis=0)


def prop_right(re, im, table):
    h, n = HALF, PROBE
    low = lax.broadcasted_iota(jnp.int32, (1, h), 1) < h // 2
    x = jnp.concatenate(
        [jnp.concatenate([re[:, :h], im[:, :h]], axis=1), jnp.concatenate([re[:, h:], im[:, h:]], axis=1)], axis=0
    )
    y = rmul(x, table[0])
    u = [jnp.where(low, z[:, h:], z[:, :h]) for z in (re, im)]
    v = rmul(jnp.concatenate(u, axis=1), table[1])
    out = []
    for at in (slice(0, h), slice(h, n)):
        out.append(
            jnp.concatenate(
                [y[:n, at] + jnp.where(low, 0.0, v[:, at]), y[n:, at] + jnp.where(low, v[:, at], 0.0)], axis=1
            )
        )
    return out


def place_of(scalars, slot):
    row = scalars[2 * slot]
    col = scalars[2 * slot + 1]
    row_base = pl.multiple_of(row // 8 * 8, 8)
    col_base = pl.multiple_of(col // 128 * 128, 128)
    return row_base, row - row_base, col_base, col - col_base


def window_of(field, part, place):
    row_base, row_off, col_base, col_off = place
    x = field[part, pl.ds(row_base, PROBE + 8), pl.ds(col_base, PROBE + 128)]
    x = pltpu.roll(x, (PROBE + 128 - col_off) % (PROBE + 128), 1)[:, :PROBE]
    return pltpu.roll(x, (PROBE + 8 - row_off) % (PROBE + 8), 0)[:PROBE]


def add_window(field, part, place, x):
    row_base, row_off, col_base, col_off = place
    x = jnp.concatenate([x, jnp.zeros((8, PROBE), F32)], axis=0)
    x = pltpu.roll(x, row_off, 0)
    x = jnp.concatenate([x, jnp.zeros((PROBE + 8, 128), F32)], axis=1)
    x = pltpu.roll(x, col_off, 1)
    at = (part, pl.ds(row_base, PROBE + 8), pl.ds(col_base, PROBE + 128))
    field[at] = field[at] + x


def fetch_field(layer, core, obj, right, low, diag, side, field, sems, meanwhile=None):
    t = TILE
    copies = [
        pltpu.make_async_copy(obj.at[layer], field.at[:, :t, :t], sems.at[0]),
        pltpu.make_async_copy(right, field.at[:, :t, t:], sems.at[1]),
        pltpu.make_async_copy(low, field.at[:, t:, :t], sems.at[2]),
    ]
    for copy in copies:
        copy.start()
    if meanwhile is not None:
        meanwhile()

    @pl.when(core == 0)
    def _():
        copy = pltpu.make_async_copy(side, field.at[:, t:, t:], sems.at[3])
        copy.start()
        copy.wait()

    @pl.when(core != 0)
    def _():
        copy = pltpu.make_async_copy(diag, field.at[:, t:, t:], sems.at[3])
        copy.start()
        copy.wait()

    for copy in copies:
        copy.wait()


def store_field(field, main, right, low_a, low_b, corner, sems):
    n, t = PROBE, TILE
    copies = [
        pltpu.make_async_copy(field.at[:, :t, t:], right, sems.at[0]),
        pltpu.make_async_copy(field.at[:, t:, n:t], low_b, sems.at[1]),
        pltpu.make_async_copy(field.at[:, t:, :n], low_a, sems.at[2]),
        pltpu.make_async_copy(field.at[:, t:, t:], corner, sems.at[3]),
        pltpu.make_async_copy(field.at[:, :t, :t], main, sems.at[4]),
    ]
    for copy in copies:
        copy.start()
    for copy in copies:
        copy.wait()


def amp_kernel(amp, perm_l, perm_r, out):
    hi, mid, lo = exact_parts(amp[0])
    y = jnp.dot(perm_l[...], jnp.concatenate([hi, mid, lo], axis=0), preferred_element_type=F32)
    hi, mid, lo = exact_parts(y)
    out[0] = jnp.dot(jnp.concatenate([hi, mid, lo], axis=1), perm_r[...], preferred_element_type=F32)


def out_kernel(
    scalars, obj, right, low, diag, side, mine, across, mine_other, across_other, table_l, table_r,
    psi, win, probe_rows, field, sems, probe_sem,
):
    slot = pl.program_id(0)
    probe = probe_rows.reshape(2, 2, PROBE, PROBE)

    @pl.when(slot == 0)
    def _():
        core, y_hi, z = scalars[13], scalars[14], scalars[15]
        copies = [
            pltpu.make_async_copy(src.at[k], probe_rows.at[:, :, z ^ k, y, c], probe_sem)
            for src, y, c in (
                (mine, y_hi, core),
                (across, 1 - y_hi, core),
                (mine_other, y_hi, 1 - core),
                (across_other, 1 - y_hi, 1 - core),
            )
            for k in range(4)
        ]
        for copy in copies:
            copy.start()
        fetch_field(0, core, obj, right, low, diag, side, field, sems)
        for copy in copies:
            copy.wait()

    @pl.when(slot < scalars[12])
    def _():
        place = place_of(scalars, slot)
        w_re = window_of(field, 0, place)
        w_im = window_of(field, 1, place)
        win[0, 0] = w_re
        win[0, 1] = w_im
        x = []
        for m in (0, 1):
            re = probe[m, 0] * w_re - probe[m, 1] * w_im
            im = probe[m, 0] * w_im + probe[m, 1] * w_re
            x.append(prop_left(re, im, table_l))
        for m in (0, 1):
            re, im = prop_right(*x[m], table_r)
            psi[0, m, 0] = re
            psi[0, m, 1] = im


def far_kernel(
    scalars, obj, right, low, diag, side, psi, amp, four_l, four_r, ruof_l, ruof_r, tw_row, tw_col,
    g_psi, g_main, g_right, g_low_a, g_low_b, g_corner, field, grad, win, gwin, sems,
):
    slot = pl.program_id(0)
    h, n = HALF, PROBE
    used = scalars[12]

    def load_window(at):
        place = place_of(scalars, at)
        win[0] = window_of(field, 0, place)
        win[1] = window_of(field, 1, place)

    def flush(at):
        place = place_of(scalars, at)
        add_window(grad, 0, place, gwin[0])
        add_window(grad, 1, place, gwin[1])

    @pl.when(slot == 0)
    def _():
        def clear():
            grad[...] = jnp.zeros_like(grad)
            gwin[...] = jnp.zeros_like(gwin)

        fetch_field(1, scalars[13], obj, right, low, diag, side, field, sems, clear)
        load_window(0)

    @pl.when(slot < used)
    def _():
        w_re, w_im = win[0], win[1]
        tr, ti = tw_row[0], tw_row[1]
        cr, ci = tw_col[0, 0:1], tw_col[1, 0:1]
        chi = {}

        def left(m, odd):
            if m not in chi:
                p_re, p_im = psi[0, m, 0], psi[0, m, 1]
                chi[m] = (p_re * w_re - p_im * w_im, p_re * w_im + p_im * w_re)
            re, im = chi[m]
            if odd:
                d_re, d_im = re[:h] - re[h:], im[:h] - im[h:]
                x = [d_re * tr - d_im * ti, d_re * ti + d_im * tr]
            else:
                x = [re[:h] + re[h:], im[:h] + im[h:]]
            return lmul(four_l[...], jnp.concatenate(x, axis=0))

        def across(y):
            re, im = y[:h], y[h:]
            d_re, d_im = re[:, :h] - re[:, h:], im[:, :h] - im[:, h:]
            even = jnp.concatenate([re[:, :h] + re[:, h:], im[:, :h] + im[:, h:]], axis=1)
            odd = jnp.concatenate([d_re * cr - d_im * ci, d_re * ci + d_im * cr], axis=1)
            return rmul(jnp.concatenate([even, odd], axis=0), four_r[...])

        def slope_of(z0, z1, rows):
            sq = z0 * z0 + z1 * z1
            total = sq[:, :h] + sq[:, h:] + 1.0
            both = jnp.concatenate([amp[0, rows, :h], amp[0, rows, h:]], axis=0)
            slope = 2.0 - 2.0 * both * lax.rsqrt(total)
            return jnp.concatenate([slope, slope], axis=1)

        def back_across(z):
            y = rmul(z, ruof_r[...])
            q_re = y[h:, :h] * cr + y[h:, h:] * ci
            q_im = y[h:, h:] * cr - y[h:, :h] * ci
            re = jnp.concatenate([y[:h, :h] + q_re, y[:h, :h] - q_re], axis=1)
            im = jnp.concatenate([y[:h, h:] + q_im, y[:h, h:] - q_im], axis=1)
            return jnp.concatenate([re, im], axis=0)

        def finish(m, y_even, y_odd):
            q_re = y_odd[:h] * tr + y_odd[h:] * ti
            q_im = y_odd[h:] * tr - y_odd[:h] * ti
            re = jnp.concatenate([y_even[:h] + q_re, y_even[:h] - q_re], axis=0)
            im = jnp.concatenate([y_even[h:] + q_im, y_even[h:] - q_im], axis=0)
            g_psi[0, m, 0] = w_re * re + w_im * im
            g_psi[0, m, 1] = w_re * im - w_im * re
            p_re, p_im = psi[0, m, 0], psi[0, m, 1]
            return p_re * re + p_im * im, p_re * im - p_im * re

        back = ruof_l[...]
        l0e = left(0, 0)
        l1e = left(1, 0)
        l0o = left(0, 1)
        z0e = across(l0e)
        l1o = left(1, 1)
        z1e = across(l1e)
        slope_e = slope_of(z0e, z1e, slice(0, h))
        z0o = across(l0o)
        b0e = back_across(z0e * slope_e)
        z1o = across(l1o)
        flush(jnp.maximum(slot - 1, 0))
        slope_o = slope_of(z0o, z1o, slice(h, n))
        load_window(jnp.minimum(slot + 1, SLOTS - 1))
        b1e = back_across(z1e * slope_e)
        a0e = lmul(back, b0e)
        b0o = back_across(z0o * slope_o)
        a1e = lmul(back, b1e)
        b1o = back_across(z1o * slope_o)
        a0o = lmul(back, b0o)
        a1o = lmul(back, b1o)
        u_re, u_im = finish(0, a0e, a0o)
        v_re, v_im = finish(1, a1e, a1o)
        gwin[0] = u_re + v_re
        gwin[1] = u_im + v_im

    @pl.when(slot == pl.num_programs(0) - 1)
    def _():
        flush(used - 1)
        store_field(grad, g_main, g_right, g_low_a, g_low_b, g_corner, sems)


def home_kernel(
    scalars, win, g_psi, probe, table_l, table_r,
    g_probe, g_main, g_right, g_low_a, g_low_b, g_corner, grad, sems,
):
    slot = pl.program_id(0)

    @pl.when(slot == 0)
    def _():
        grad[...] = jnp.zeros_like(grad)
        g_probe[...] = jnp.zeros_like(g_probe)

    @pl.when(slot < scalars[12])
    def _():
        place = place_of(scalars, slot)
        x = [prop_left(g_psi[0, m, 0], g_psi[0, m, 1], table_l) for m in (0, 1)]
        w_re, w_im = win[0, 0], win[0, 1]
        gw_re = gw_im = None
        for m in (0, 1):
            re, im = prop_right(*x[m], table_r)
            p_re, p_im = probe[m, 0], probe[m, 1]
            a_re = p_re * re + p_im * im
            a_im = p_re * im - p_im * re
            gw_re = a_re if m == 0 else gw_re + a_re
            gw_im = a_im if m == 0 else gw_im + a_im
            g_probe[m, 0] += w_re * re + w_im * im
            g_probe[m, 1] += w_re * im - w_im * re
        add_window(grad, 0, place, gw_re)
        add_window(grad, 1, place, gw_im)

    @pl.when(slot == pl.num_programs(0) - 1)
    def _():
        store_field(grad, g_main, g_right, g_low_a, g_low_b, g_corner, sems)


def join_kernel(main, right, low_a, low_b, diag, *rest):
    out = rest[-1]
    n, h = PROBE, HALF
    i = pl.program_id(0)

    @pl.when(i < 2)
    def _():
        out[0, :, :, :n] = main[:, :, :n] + right[...] + low_a[...] + diag[...]
        out[0, :, :, n:] = main[:, :, n:] + low_b[...]

    @pl.when(i >= 2)
    def _():
        out[0, :, :, :n] = main[:, :, :n] + right[...]
        out[0, :, :, n:] = main[:, :, n:]


def whole(shape):
    return pl.BlockSpec(shape, lambda j, s: (0,) * len(shape))


def held():
    return pl.BlockSpec(memory_space=pltpu.VMEM)


def any_spec():
    return pl.BlockSpec(memory_space=pl.ANY)


def of_slot(shape):
    return pl.BlockSpec(
        (1,) + shape, lambda j, s: (jnp.minimum(j, s[12] - 1),) + (0,) * len(shape)
    )


def cost(flops, data):
    return pl.CostEstimate(flops=int(flops), bytes_accessed=int(data), transcendentals=0)


def params(limit=VMEM_LIMIT):
    return pltpu.CompilerParams(vmem_limit_bytes=limit)


FIELD_PARTS = [(2, TILE, TILE), (2, TILE, PROBE), (2, PROBE, PROBE), (2, PROBE, PROBE), (2, PROBE, PROBE)]


def sds(shape):
    return jax.ShapeDtypeStruct(shape, F32)


def permute_amplitudes(amp, tables):
    n = PROBE
    return pl.pallas_call(
        amp_kernel,
        grid=(SLOTS,),
        in_specs=[
            pl.BlockSpec((1, n, n), lambda j: (j, 0, 0)),
            pl.BlockSpec((n, 3 * n), lambda j: (0, 0)),
            pl.BlockSpec((3 * n, n), lambda j: (0, 0)),
        ],
        out_specs=pl.BlockSpec((1, n, n), lambda j: (j, 0, 0)),
        out_shape=sds((SLOTS, n, n)),
        compiler_params=params(60 * 1024 * 1024),
        cost_estimate=cost(1.2e9, 4e6),
        name="order_amplitudes",
    )(amp, tables["perm_l"], tables["perm_r"])


def run_out(scalars, obj, halo, probe, tables):
    n = PROBE
    return pl.pallas_call(
        out_kernel,
        grid_spec=pltpu.PrefetchScalarGridSpec(
            num_scalar_prefetch=1,
            grid=(SLOTS,),
            in_specs=[any_spec()] * 9 + [held()] * 2,
            out_specs=[of_slot((2, 2, n, n)), of_slot((2, n, n)), whole((2, 2, 4, 2, 2, 16, n))],
            scratch_shapes=[
                pltpu.VMEM((2, 3 * n, 3 * n), F32),
                pltpu.SemaphoreType.DMA((5,)),
                pltpu.SemaphoreType.DMA,
            ],
        ),
        out_shape=[sds((SLOTS, 2, 2, n, n)), sds((SLOTS, 2, n, n)), sds((2, 2, 4, 2, 2, 16, n))],
        compiler_params=params(60 * 1024 * 1024),
        cost_estimate=cost(6e10, 2e7),
        name="propagate_out",
    )(scalars, obj, *halo, *probe, tables["prop_l"], tables["prop_r"])


def run_far(scalars, obj, halo, psi, amp, tables):
    n = PROBE
    return pl.pallas_call(
        far_kernel,
        grid_spec=pltpu.PrefetchScalarGridSpec(
            num_scalar_prefetch=1,
            grid=(SLOTS,),
            in_specs=[any_spec()] * 5
            + [of_slot((2, 2, n, n)), of_slot((n, n))]
            + [held()] * 6,
            out_specs=[of_slot((2, 2, n, n))] + [any_spec()] * 5,
            scratch_shapes=[
                pltpu.VMEM((2, 3 * n, 3 * n), F32),
                pltpu.VMEM((2, 3 * n, 3 * n), F32),
                pltpu.VMEM((2, n, n), F32),
                pltpu.VMEM((2, n, n), F32),
                pltpu.SemaphoreType.DMA((5,)),
            ],
        ),
        out_shape=[sds((SLOTS, 2, 2, n, n))] + [sds(s) for s in FIELD_PARTS],
        compiler_params=params(),
        cost_estimate=cost(6e10, 2e7),
        name="far_field",
    )(
        scalars, obj, *halo, psi, amp,
        tables["four_l"], tables["four_r"], tables["ruof_l"], tables["ruof_r"],
        tables["tw_row"], tables["tw_col"],
    )


def run_home(scalars, win, g_psi, probe, tables):
    n = PROBE
    return pl.pallas_call(
        home_kernel,
        grid_spec=pltpu.PrefetchScalarGridSpec(
            num_scalar_prefetch=1,
            grid=(SLOTS,),
            in_specs=[
                of_slot((2, n, n)),
                of_slot((2, 2, n, n)),
                held(),
                held(),
                held(),
            ],
            out_specs=[whole((2, 2, n, n))] + [any_spec()] * 5,
            scratch_shapes=[pltpu.VMEM((2, 3 * n, 3 * n), F32), pltpu.SemaphoreType.DMA((5,))],
        ),
        out_shape=[sds((2, 2, n, n))] + [sds(s) for s in FIELD_PARTS],
        compiler_params=params(),
        cost_estimate=cost(6e10, 2e7),
        name="propagate_home",
    )(scalars, win, g_psi, probe, tables["back_l"], tables["back_r"])


def run_join(layer, main, arrived, into):
    n, h = PROBE, HALF
    top = lambda i: (0, jnp.minimum(i, 1), 0)
    extra = [] if into is None else [into]
    return pl.pallas_call(
        join_kernel,
        grid=(4,),
        in_specs=[
            pl.BlockSpec((2, h, TILE), lambda i: (0, i, 0)),
            pl.BlockSpec((2, h, n), lambda i: (0, i, 0)),
            pl.BlockSpec((2, h, n), top),
            pl.BlockSpec((2, h, n), top),
            pl.BlockSpec((2, h, n), top),
        ]
        + [pl.BlockSpec(memory_space=pl.ANY)] * len(extra),
        out_specs=pl.BlockSpec((1, 2, h, TILE), lambda i: (layer, 0, i, 0)),
        out_shape=sds((2, 2, TILE, TILE)),
        input_output_aliases={} if into is None else {5: 0},
        compiler_params=params(),
        cost_estimate=cost(1e6, 6e6),
        name="join_gradients",
    )(main, *arrived, *extra)


def solution(mesh):
    n_gx, n_gy = mesh.shape["gx"], mesh.shape["gy"]
    axes = tuple(mesh.axis_names)
    tables = make_tables()

    def number(gx, gy):
        return gx * n_gy + gy if axes == ("gx", "gy") else gy * n_gx + gx

    def send(x, target):
        pairs = []
        for gx in range(n_gx):
            for gy in range(n_gy):
                to = target(gx, gy)
                if to is not None and 0 <= to[0] < n_gx and 0 <= to[1] < n_gy:
                    pairs.append((number(gx, gy), number(*to)))
        return lax.ppermute(x, axes, pairs)

    def flip(gx_bits, gy_bits):
        return lambda gx, gy: (gx ^ gx_bits, gy ^ gy_bits)

    def pieces(obj, layer):
        n = PROBE
        return obj[layer, :, :n, :n], obj[layer, :, :, :n], obj[layer, :, :n]

    def bring(corner, edge, low):
        right = send(edge, lambda gx, gy: (gx - 1, gy))
        low = send(low, lambda gx, gy: (gx, gy - 1))
        diag = send(corner, lambda gx, gy: (gx - 1, gy - 1) if gx % 2 == 0 else None)
        return right, low, diag

    def bring_side(low):
        return send(low[:, :, :PROBE], lambda gx, gy: (gx - 1, gy) if gx % 2 == 1 else None)

    def take_back(right, low_a, low_b, corner):
        side = send(corner, lambda gx, gy: (gx + 1, gy) if gx % 2 == 0 else None)
        right = send(right, lambda gx, gy: (gx + 1, gy))
        low_b = send(low_b, lambda gx, gy: (gx, gy + 1))
        diag = send(corner, lambda gx, gy: (gx + 1, gy + 1) if gx % 2 == 1 else None)
        low_a = send(low_a + side, lambda gx, gy: (gx, gy + 1))
        return right, low_a, low_b, diag

    def gather_probe(probe):
        return jnp.stack([probe] + [send(probe, flip(4 * k, 0)) for k in (1, 2, 3)])

    def reduce_chip(grad):
        gx = lax.axis_index("gx")
        core, z = gx % 2, gx // 4
        rows = PROBE // n_gx
        parts = jnp.transpose(grad.reshape(2, 2, 4, 2, 2, rows, PROBE), (4, 2, 3, 0, 1, 5, 6))
        keep = jnp.where(core == 0, parts[0], parts[1])
        give = jnp.where(core == 0, parts[1], parts[0])
        return keep + send(give, flip(1, 0))

    def halved(part, bit, there):
        keep = jnp.where(bit == 0, part[0], part[1])
        give = jnp.where(bit == 0, part[1], part[0])
        return keep + send(give, there)

    def halved(part, bit, there):
        keep = jnp.where(bit == 0, part[0], part[1])
        give = jnp.where(bit == 0, part[1], part[0])
        return keep + send(give, there)

    def reduce_z(part):
        z = lax.axis_index("gx") // 4
        part = halved(part.reshape(2, 2, *part.shape[1:]), z // 2, flip(8, 0))
        return halved(part, z % 2, flip(4, 0))

    def reduce_xy(part):
        for bit in (2, 4):
            part = part + send(part, flip(0, bit))
        part = halved(part, lax.axis_index("gx") // 2 % 2, flip(2, 1))
        return part + send(part, flip(0, 1))

    def on_device(obj, probe, positions, counts, amplitudes):
        gx = lax.axis_index("gx").astype(jnp.int32)
        scalars = jnp.concatenate(
            [positions.reshape(2 * SLOTS), counts.reshape(1), jnp.stack([gx & 1, gx >> 1 & 1, gx >> 2])]
        )
        pieces_0, mine = lax.optimization_barrier((pieces(obj, 0), gather_probe(probe)))
        halo_0 = bring(*pieces_0)
        across = send(mine, flip(2, 1))
        probe_parts = [mine, across, send(mine, flip(1, 0)), send(across, flip(1, 0))]
        obj_late, diag = lax.optimization_barrier((obj, halo_0[2]))
        halo_0 = (*halo_0[:2], diag)
        amp = permute_amplitudes(amplitudes[0, 0], tables)
        pieces_1, halo_0, amp, probe_parts = lax.optimization_barrier((pieces(obj_late, 1), halo_0, amp, probe_parts))
        halo_1 = bring(*pieces_1)
        psi, win, probe_rows = run_out(scalars, obj, (*halo_0, bring_side(halo_0[1])), probe_parts, tables)
        low, psi = lax.optimization_barrier((halo_1[1], psi))
        halo_1 = (halo_1[0], low, halo_1[2], bring_side(low))
        probe_full = probe_rows.reshape(2, 2, PROBE, PROBE)
        g_psi, main_1, *edges_1 = run_far(scalars, obj, halo_1, psi, amp, tables)
        back_1 = take_back(*edges_1)
        used = counts[0, 0] > 0

        def home(operands):
            g_probe, *fields = run_home(*operands, tables)
            return reduce_chip(g_probe), *fields

        def idle(operands):
            return tuple(jnp.zeros(x.shape, x.dtype) for x in jax.eval_shape(home, operands))

        part, main_0, *edges_0 = lax.cond(used, home, idle, (scalars, win, g_psi, probe_full))
        edges_0, part, back_1 = lax.optimization_barrier((edges_0, part, back_1))
        back_0 = take_back(*edges_0)

        def rest(operands):
            part, main, back = operands
            part, grad = lax.optimization_barrier((reduce_z(part), run_join(1, main, back, None)))
            return reduce_xy(part), grad

        def nothing(operands):
            return tuple(jnp.zeros(x.shape, x.dtype) for x in jax.eval_shape(rest, operands))

        probe_grad, grad = lax.cond(used, rest, nothing, (part, main_1, back_1))
        grad = run_join(0, main_0, back_0, grad)
        return grad, probe_grad

    return jax.shard_map(
        on_device,
        mesh=mesh,
        in_specs=(
            P(None, None, "gy", "gx"),
            P(None, None, "gx", None),
            P("gy", "gx", None, None),
            P("gy", "gx"),
            P("gy", "gx", None, None, None),
        ),
        out_specs=(P(None, None, "gy", "gx"), P(None, None, "gx", None)),
        check_vma=False,
    )
```

```python
import functools
import math

import jax
import jax.numpy as jnp
import numpy as np
from jax import lax
from jax.experimental import pallas as pl
from jax.experimental.pallas import tpu as pltpu
from jax.sharding import PartitionSpec as P

BAND = 48
PROBE = 256
HALF = 128
TILE = 512
SLOTS = 6
F32 = jnp.float32
BF16 = jnp.bfloat16
VMEM_LIMIT = 48 * 1024 * 1024


def split_table(mat):
    hi = mat.astype(BF16)
    lo = (mat - hi.astype(np.float64)).astype(BF16)
    return hi, lo


def left_table(mat):
    hi, lo = split_table(mat)
    return np.concatenate([hi, lo, hi], axis=1)


def right_table(mat):
    hi, lo = split_table(mat)
    return np.concatenate([hi, lo, hi], axis=0)


def make_tables():
    index = np.arange(PROBE)
    offset = (index[:, None] - index[None, :]).astype(np.float64)
    prop = np.where(np.abs(offset) <= BAND, np.exp(1j * np.pi * offset**2 / (2 * BAND)), 0)
    prop = prop / math.sqrt(2 * BAND + 1)
    half = np.arange(HALF)
    four = np.exp(-2j * np.pi * ((half[:, None] * half[None, :]) % HALF) / HALF) / math.sqrt(PROBE)
    twist = np.exp(-2j * np.pi * half / PROBE)

    def from_left(mat):
        return np.block([[mat.real, -mat.imag], [mat.imag, mat.real]])

    def from_right(mat):
        return from_left(mat).T

    near = np.arange(PROBE) < HALF
    edge = (np.arange(PROBE) + HALF // 2) // HALF == 1
    cross = np.where(near[:, None] != near[None, :], prop, 0)
    assert not cross[~edge].any() and not cross[:, ~edge].any()

    def pair(table, embed, mat):
        other = np.zeros((HALF, HALF), complex)
        for a in range(HALF):
            for b in range(HALF):
                to, of = (a + HALF, b) if a < HALF // 2 else (a, b + HALF)
                if (b >= HALF // 2) == (a < HALF // 2):
                    other[a, b] = mat[to, of]
        return np.stack([table(embed(mat[:HALF, :HALF])), table(embed(other))])

    order = np.concatenate([np.arange(0, PROBE, 2), np.arange(1, PROBE, 2)])
    perm = np.zeros((PROBE, PROBE))
    perm[np.arange(PROBE), order] = 1
    return {
        "prop_l": pair(left_table, from_left, prop),
        "prop_r": pair(right_table, from_right, prop),
        "back_l": pair(left_table, from_left, prop.conj()),
        "back_r": pair(right_table, from_right, prop.conj()),
        "four_l": left_table(from_left(four)),
        "four_r": right_table(from_right(four)),
        "ruof_l": left_table(from_left(four.conj())),
        "ruof_r": right_table(from_right(four.conj())),
        "tw_row": np.stack(
            [
                np.broadcast_to(twist.real[:, None], (HALF, PROBE)),
                np.broadcast_to(twist.imag[:, None], (HALF, PROBE)),
            ]
        ).astype(np.float32),
        "tw_col": np.stack(
            [
                np.broadcast_to(twist.real[None, :], (8, HALF)),
                np.broadcast_to(twist.imag[None, :], (8, HALF)),
            ]
        ).astype(np.float32),
        "perm_l": np.concatenate([perm] * 3, axis=1).astype(BF16),
        "perm_r": np.concatenate([perm.T] * 3, axis=0).astype(BF16),
    }


def parted(x):
    hi = x.astype(BF16)
    return hi, (x - hi.astype(F32)).astype(BF16)


def lmul(table, x):
    hi, lo = parted(x)
    return jnp.dot(table, jnp.concatenate([hi, hi, lo], axis=0), preferred_element_type=F32)


def rmul(x, table):
    hi, lo = parted(x)
    return jnp.dot(jnp.concatenate([hi, hi, lo], axis=1), table, preferred_element_type=F32)


def exact_parts(x):
    hi = x.astype(BF16)
    rest = x - hi.astype(F32)
    mid = rest.astype(BF16)
    return hi, mid, (rest - mid.astype(F32)).astype(BF16)


def prop_left(re, im, table):
    h, q = HALF, HALF // 2
    x = jnp.concatenate(
        [jnp.concatenate([re[:h], im[:h]], axis=0), jnp.concatenate([re[h:], im[h:]], axis=0)], axis=1
    )
    y = lmul(table[0], x)
    v = lmul(table[1], jnp.concatenate([re[h : h + q], re[q:h], im[h : h + q], im[q:h]], axis=0))
    n = PROBE
    re = [y[:q, :n], y[q:h, :n] + v[q:h], y[:q, n:] + v[:q], y[q:h, n:]]
    im = [y[h : h + q, :n], y[h + q :, :n] + v[h + q :], y[h : h + q, n:] + v[h : h + q], y[h + q :, n:]]
    return jnp.concatenate(re, axis=0), jnp.concatenate(im, axis=0)


def prop_right(re, im, table):
    h, n = HALF, PROBE
    low = lax.broadcasted_iota(jnp.int32, (1, h), 1) < h // 2
    x = jnp.concatenate(
        [jnp.concatenate([re[:, :h], im[:, :h]], axis=1), jnp.concatenate([re[:, h:], im[:, h:]], axis=1)], axis=0
    )
    y = rmul(x, table[0])
    u = [jnp.where(low, z[:, h:], z[:, :h]) for z in (re, im)]
    v = rmul(jnp.concatenate(u, axis=1), table[1])
    out = []
    for at in (slice(0, h), slice(h, n)):
        out.append(
            jnp.concatenate(
                [y[:n, at] + jnp.where(low, 0.0, v[:, at]), y[n:, at] + jnp.where(low, v[:, at], 0.0)], axis=1
            )
        )
    return out


def place_of(scalars, slot):
    row = scalars[2 * slot]
    col = scalars[2 * slot + 1]
    row_base = pl.multiple_of(row // 8 * 8, 8)
    col_base = pl.multiple_of(col // 128 * 128, 128)
    return row_base, row - row_base, col_base, col - col_base


def window_of(field, part, place):
    row_base, row_off, col_base, col_off = place
    x = field[part, pl.ds(row_base, PROBE + 8), pl.ds(col_base, PROBE + 128)]
    x = pltpu.roll(x, (PROBE + 128 - col_off) % (PROBE + 128), 1)[:, :PROBE]
    return pltpu.roll(x, (PROBE + 8 - row_off) % (PROBE + 8), 0)[:PROBE]


def add_window(field, part, place, x):
    row_base, row_off, col_base, col_off = place
    x = jnp.concatenate([x, jnp.zeros((8, PROBE), F32)], axis=0)
    x = pltpu.roll(x, row_off, 0)
    x = jnp.concatenate([x, jnp.zeros((PROBE + 8, 128), F32)], axis=1)
    x = pltpu.roll(x, col_off, 1)
    at = (part, pl.ds(row_base, PROBE + 8), pl.ds(col_base, PROBE + 128))
    field[at] = field[at] + x


def fetch_field(layer, core, obj, right, low_a, low_b, diag, side, field, sems, meanwhile=None):
    n, t = PROBE, TILE
    copies = [
        pltpu.make_async_copy(obj.at[layer], field.at[:, :t, :t], sems.at[0]),
        pltpu.make_async_copy(right, field.at[:, :t, t:], sems.at[1]),
        pltpu.make_async_copy(low_a, field.at[:, t:, :n], sems.at[2]),
        pltpu.make_async_copy(low_b, field.at[:, t:, n:t], sems.at[3]),
    ]
    for copy in copies:
        copy.start()
    if meanwhile is not None:
        meanwhile()

    @pl.when(core == 0)
    def _():
        copy = pltpu.make_async_copy(side, field.at[:, t:, t:], sems.at[4])
        copy.start()
        copy.wait()

    @pl.when(core != 0)
    def _():
        copy = pltpu.make_async_copy(diag, field.at[:, t:, t:], sems.at[4])
        copy.start()
        copy.wait()

    for copy in copies:
        copy.wait()


def store_field(field, main, right, low_a, low_b, corner, sems):
    n, t = PROBE, TILE
    copies = [
        pltpu.make_async_copy(field.at[:, :t, t:], right, sems.at[0]),
        pltpu.make_async_copy(field.at[:, t:, n:t], low_b, sems.at[1]),
        pltpu.make_async_copy(field.at[:, t:, :n], low_a, sems.at[2]),
        pltpu.make_async_copy(field.at[:, t:, t:], corner, sems.at[3]),
        pltpu.make_async_copy(field.at[:, :t, :t], main, sems.at[4]),
    ]
    for copy in copies:
        copy.start()
    for copy in copies:
        copy.wait()


def amp_kernel(amp, perm_l, perm_r, out):
    hi, mid, lo = exact_parts(amp[0])
    y = jnp.dot(perm_l[...], jnp.concatenate([hi, mid, lo], axis=0), preferred_element_type=F32)
    hi, mid, lo = exact_parts(y)
    out[0] = jnp.dot(jnp.concatenate([hi, mid, lo], axis=1), perm_r[...], preferred_element_type=F32)


def out_kernel(
    scalars, obj, right, low_a, low_b, diag, side, mine, across, mine_other, across_other, table_l, table_r,
    psi, win, probe_rows, field, sems, probe_sem,
):
    slot = pl.program_id(0)
    probe = probe_rows.reshape(2, 2, PROBE, PROBE)

    @pl.when(slot == 0)
    def _():
        core, y_hi, z = scalars[13], scalars[14], scalars[15]
        copies = [
            pltpu.make_async_copy(src.at[k], probe_rows.at[:, :, z ^ k, y, c], probe_sem)
            for src, y, c in (
                (mine, y_hi, core),
                (across, 1 - y_hi, core),
                (mine_other, y_hi, 1 - core),
                (across_other, 1 - y_hi, 1 - core),
            )
            for k in range(4)
        ]
        for copy in copies:
            copy.start()
        fetch_field(0, core, obj, right, low_a, low_b, diag, side, field, sems)
        for copy in copies:
            copy.wait()

    @pl.when(slot < scalars[12])
    def _():
        place = place_of(scalars, slot)
        w_re = window_of(field, 0, place)
        w_im = window_of(field, 1, place)
        win[0, 0] = w_re
        win[0, 1] = w_im
        x = []
        for m in (0, 1):
            re = probe[m, 0] * w_re - probe[m, 1] * w_im
            im = probe[m, 0] * w_im + probe[m, 1] * w_re
            x.append(prop_left(re, im, table_l))
        for m in (0, 1):
            re, im = prop_right(*x[m], table_r)
            psi[0, m, 0] = re
            psi[0, m, 1] = im


def far_kernel(
    scalars, obj, right, low_a, low_b, diag, side, psi, amp, four_l, four_r, ruof_l, ruof_r, tw_row, tw_col,
    g_psi, g_main, g_right, g_low_a, g_low_b, g_corner, field, grad, win, gwin, sems,
):
    slot = pl.program_id(0)
    h, n = HALF, PROBE
    used = scalars[12]

    def load_window(at):
        place = place_of(scalars, at)
        win[0] = window_of(field, 0, place)
        win[1] = window_of(field, 1, place)

    def flush(at):
        place = place_of(scalars, at)
        add_window(grad, 0, place, gwin[0])
        add_window(grad, 1, place, gwin[1])

    @pl.when(slot == 0)
    def _():
        def clear():
            grad[...] = jnp.zeros_like(grad)
            gwin[...] = jnp.zeros_like(gwin)

        fetch_field(1, scalars[13], obj, right, low_a, low_b, diag, side, field, sems, clear)
        load_window(0)

    @pl.when(slot < used)
    def _():
        w_re, w_im = win[0], win[1]
        tr, ti = tw_row[0], tw_row[1]
        cr, ci = tw_col[0, 0:1], tw_col[1, 0:1]
        chi = {}

        def left(m, odd):
            if m not in chi:
                p_re, p_im = psi[0, m, 0], psi[0, m, 1]
                chi[m] = (p_re * w_re - p_im * w_im, p_re * w_im + p_im * w_re)
            re, im = chi[m]
            if odd:
                d_re, d_im = re[:h] - re[h:], im[:h] - im[h:]
                x = [d_re * tr - d_im * ti, d_re * ti + d_im * tr]
            else:
                x = [re[:h] + re[h:], im[:h] + im[h:]]
            return lmul(four_l[...], jnp.concatenate(x, axis=0))

        def across(y):
            re, im = y[:h], y[h:]
            d_re, d_im = re[:, :h] - re[:, h:], im[:, :h] - im[:, h:]
            even = jnp.concatenate([re[:, :h] + re[:, h:], im[:, :h] + im[:, h:]], axis=1)
            odd = jnp.concatenate([d_re * cr - d_im * ci, d_re * ci + d_im * cr], axis=1)
            return rmul(jnp.concatenate([even, odd], axis=0), four_r[...])

        def slope_of(z0, z1, rows):
            sq = z0 * z0 + z1 * z1
            total = sq[:, :h] + sq[:, h:] + 1.0
            both = jnp.concatenate([amp[0, rows, :h], amp[0, rows, h:]], axis=0)
            slope = 2.0 - 2.0 * both * lax.rsqrt(total)
            return jnp.concatenate([slope, slope], axis=1)

        def back_across(z):
            y = rmul(z, ruof_r[...])
            q_re = y[h:, :h] * cr + y[h:, h:] * ci
            q_im = y[h:, h:] * cr - y[h:, :h] * ci
            re = jnp.concatenate([y[:h, :h] + q_re, y[:h, :h] - q_re], axis=1)
            im = jnp.concatenate([y[:h, h:] + q_im, y[:h, h:] - q_im], axis=1)
            return jnp.concatenate([re, im], axis=0)

        def finish(m, y_even, y_odd):
            q_re = y_odd[:h] * tr + y_odd[h:] * ti
            q_im = y_odd[h:] * tr - y_odd[:h] * ti
            re = jnp.concatenate([y_even[:h] + q_re, y_even[:h] - q_re], axis=0)
            im = jnp.concatenate([y_even[h:] + q_im, y_even[h:] - q_im], axis=0)
            g_psi[0, m, 0] = w_re * re + w_im * im
            g_psi[0, m, 1] = w_re * im - w_im * re
            p_re, p_im = psi[0, m, 0], psi[0, m, 1]
            return p_re * re + p_im * im, p_re * im - p_im * re

        back = ruof_l[...]
        l0e = left(0, 0)
        l1e = left(1, 0)
        l0o = left(0, 1)
        z0e = across(l0e)
        l1o = left(1, 1)
        z1e = across(l1e)
        slope_e = slope_of(z0e, z1e, slice(0, h))
        z0o = across(l0o)
        b0e = back_across(z0e * slope_e)
        z1o = across(l1o)
        flush(jnp.maximum(slot - 1, 0))
        slope_o = slope_of(z0o, z1o, slice(h, n))
        load_window(jnp.minimum(slot + 1, SLOTS - 1))
        b1e = back_across(z1e * slope_e)
        a0e = lmul(back, b0e)
        b0o = back_across(z0o * slope_o)
        a1e = lmul(back, b1e)
        b1o = back_across(z1o * slope_o)
        a0o = lmul(back, b0o)
        a1o = lmul(back, b1o)
        u_re, u_im = finish(0, a0e, a0o)
        v_re, v_im = finish(1, a1e, a1o)
        gwin[0] = u_re + v_re
        gwin[1] = u_im + v_im

    @pl.when(slot == pl.num_programs(0) - 1)
    def _():
        flush(used - 1)
        store_field(grad, g_main, g_right, g_low_a, g_low_b, g_corner, sems)


def home_kernel(
    scalars, win, g_psi, probe, table_l, table_r,
    g_probe, g_main, g_right, g_low_a, g_low_b, g_corner, grad, sems,
):
    slot = pl.program_id(0)

    @pl.when(slot == 0)
    def _():
        grad[...] = jnp.zeros_like(grad)
        g_probe[...] = jnp.zeros_like(g_probe)

    @pl.when(slot < scalars[12])
    def _():
        place = place_of(scalars, slot)
        x = [prop_left(g_psi[0, m, 0], g_psi[0, m, 1], table_l) for m in (0, 1)]
        w_re, w_im = win[0, 0], win[0, 1]
        gw_re = gw_im = None
        for m in (0, 1):
            re, im = prop_right(*x[m], table_r)
            p_re, p_im = probe[m, 0], probe[m, 1]
            a_re = p_re * re + p_im * im
            a_im = p_re * im - p_im * re
            gw_re = a_re if m == 0 else gw_re + a_re
            gw_im = a_im if m == 0 else gw_im + a_im
            g_probe[m, 0] += w_re * re + w_im * im
            g_probe[m, 1] += w_re * im - w_im * re
        add_window(grad, 0, place, gw_re)
        add_window(grad, 1, place, gw_im)

    @pl.when(slot == pl.num_programs(0) - 1)
    def _():
        store_field(grad, g_main, g_right, g_low_a, g_low_b, g_corner, sems)


def join_kernel(main, right, low_a, low_b, diag, *rest):
    out = rest[-1]
    n = PROBE
    i = pl.program_id(0)

    @pl.when(i < 4)
    def _():
        out[0, :, :, :n] = main[:, :, :n] + right[...] + low_a[...] + diag[...]
        out[0, :, :, n:] = main[:, :, n:] + low_b[...]

    @pl.when(i >= 4)
    def _():
        out[0, :, :, :n] = main[:, :, :n] + right[...]
        out[0, :, :, n:] = main[:, :, n:]


def cut_kernel(obj, corner, edge, low, sems):
    n = PROBE
    copies = [
        pltpu.make_async_copy(obj.at[0, :, :n, :n], corner, sems.at[0]),
        pltpu.make_async_copy(obj.at[0, :, :, :n], edge, sems.at[1]),
        pltpu.make_async_copy(obj.at[0, :, :n, n:], low, sems.at[2]),
    ]
    for copy in copies:
        copy.start()
    for copy in copies:
        copy.wait()


def whole(shape):
    return pl.BlockSpec(shape, lambda j, s: (0,) * len(shape))


def held():
    return pl.BlockSpec(memory_space=pltpu.VMEM)


def any_spec():
    return pl.BlockSpec(memory_space=pl.ANY)


def of_slot(shape):
    return pl.BlockSpec(
        (1,) + shape, lambda j, s: (jnp.minimum(j, s[12] - 1),) + (0,) * len(shape)
    )


def cost(flops, data):
    return pl.CostEstimate(flops=int(flops), bytes_accessed=int(data), transcendentals=0)


def params():
    return pltpu.CompilerParams(vmem_limit_bytes=VMEM_LIMIT)


FIELD_PARTS = [(2, TILE, TILE), (2, TILE, PROBE), (2, PROBE, PROBE), (2, PROBE, PROBE), (2, PROBE, PROBE)]


def sds(shape):
    return jax.ShapeDtypeStruct(shape, F32)


def cut_first(obj):
    n = PROBE
    return pl.pallas_call(
        cut_kernel,
        in_specs=[pl.BlockSpec(memory_space=pl.ANY)],
        out_specs=[pl.BlockSpec(memory_space=pl.ANY)] * 3,
        out_shape=[sds((2, n, n)), sds((2, TILE, n)), sds((2, n, n))],
        scratch_shapes=[pltpu.SemaphoreType.DMA((3,))],
        compiler_params=params(),
        cost_estimate=cost(1e6, 4e6),
        name="cut_pieces",
    )(obj)


def permute_amplitudes(amp, tables):
    n = PROBE
    return pl.pallas_call(
        amp_kernel,
        grid=(SLOTS,),
        in_specs=[
            pl.BlockSpec((1, n, n), lambda j: (j, 0, 0)),
            pl.BlockSpec((n, 3 * n), lambda j: (0, 0)),
            pl.BlockSpec((3 * n, n), lambda j: (0, 0)),
        ],
        out_specs=pl.BlockSpec((1, n, n), lambda j: (j, 0, 0)),
        out_shape=sds((SLOTS, n, n)),
        compiler_params=params(),
        cost_estimate=cost(1.2e9, 4e6),
        name="order_amplitudes",
    )(amp, tables["perm_l"], tables["perm_r"])


def run_out(scalars, obj, halo, probe, tables):
    n = PROBE
    return pl.pallas_call(
        out_kernel,
        grid_spec=pltpu.PrefetchScalarGridSpec(
            num_scalar_prefetch=1,
            grid=(SLOTS,),
            in_specs=[any_spec()] * 10 + [held()] * 2,
            out_specs=[of_slot((2, 2, n, n)), of_slot((2, n, n)), whole((2, 2, 4, 2, 2, 16, n))],
            scratch_shapes=[
                pltpu.VMEM((2, 3 * n, 3 * n), F32),
                pltpu.SemaphoreType.DMA((5,)),
                pltpu.SemaphoreType.DMA,
            ],
        ),
        out_shape=[sds((SLOTS, 2, 2, n, n)), sds((SLOTS, 2, n, n)), sds((2, 2, 4, 2, 2, 16, n))],
        compiler_params=params(),
        cost_estimate=cost(6e10, 2e7),
        name="propagate_out",
    )(scalars, obj, *halo, *probe, tables["prop_l"], tables["prop_r"])


def run_far(scalars, obj, halo, psi, amp, tables):
    n = PROBE
    return pl.pallas_call(
        far_kernel,
        grid_spec=pltpu.PrefetchScalarGridSpec(
            num_scalar_prefetch=1,
            grid=(SLOTS,),
            in_specs=[any_spec()] * 6
            + [of_slot((2, 2, n, n)), of_slot((n, n))]
            + [held()] * 6,
            out_specs=[of_slot((2, 2, n, n))] + [any_spec()] * 5,
            scratch_shapes=[
                pltpu.VMEM((2, 3 * n, 3 * n), F32),
                pltpu.VMEM((2, 3 * n, 3 * n), F32),
                pltpu.VMEM((2, n, n), F32),
                pltpu.VMEM((2, n, n), F32),
                pltpu.SemaphoreType.DMA((5,)),
            ],
        ),
        out_shape=[sds((SLOTS, 2, 2, n, n))] + [sds(s) for s in FIELD_PARTS],
        compiler_params=params(),
        cost_estimate=cost(6e10, 2e7),
        name="far_field",
    )(
        scalars, obj, *halo, psi, amp,
        tables["four_l"], tables["four_r"], tables["ruof_l"], tables["ruof_r"],
        tables["tw_row"], tables["tw_col"],
    )


def run_home(scalars, win, g_psi, probe, tables):
    n = PROBE
    return pl.pallas_call(
        home_kernel,
        grid_spec=pltpu.PrefetchScalarGridSpec(
            num_scalar_prefetch=1,
            grid=(SLOTS,),
            in_specs=[
                of_slot((2, n, n)),
                of_slot((2, 2, n, n)),
                held(),
                held(),
                held(),
            ],
            out_specs=[whole((2, 2, n, n))] + [any_spec()] * 5,
            scratch_shapes=[pltpu.VMEM((2, 3 * n, 3 * n), F32), pltpu.SemaphoreType.DMA((5,))],
        ),
        out_shape=[sds((2, 2, n, n))] + [sds(s) for s in FIELD_PARTS],
        compiler_params=params(),
        cost_estimate=cost(6e10, 2e7),
        name="propagate_home",
    )(scalars, win, g_psi, probe, tables["back_l"], tables["back_r"])


def run_join(layer, main, arrived, into):
    n, h = PROBE, HALF // 2
    top = lambda i: (0, jnp.minimum(i, 3), 0)
    extra = [] if into is None else [into]
    return pl.pallas_call(
        join_kernel,
        grid=(8,),
        in_specs=[
            pl.BlockSpec((2, h, TILE), lambda i: (0, i, 0)),
            pl.BlockSpec((2, h, n), lambda i: (0, i, 0)),
            pl.BlockSpec((2, h, n), top),
            pl.BlockSpec((2, h, n), top),
            pl.BlockSpec((2, h, n), top),
        ]
        + [pl.BlockSpec(memory_space=pl.ANY)] * len(extra),
        out_specs=pl.BlockSpec((1, 2, h, TILE), lambda i: (layer, 0, i, 0)),
        out_shape=sds((2, 2, TILE, TILE)),
        input_output_aliases={} if into is None else {5: 0},
        compiler_params=params(),
        cost_estimate=cost(1e6, 6e6),
        name="join_gradients",
    )(main, *arrived, *extra)


def solution(mesh):
    n_gx, n_gy = mesh.shape["gx"], mesh.shape["gy"]
    axes = tuple(mesh.axis_names)
    tables = make_tables()

    def number(gx, gy):
        return gx * n_gy + gy if axes == ("gx", "gy") else gy * n_gx + gx

    def send(x, target):
        pairs = []
        for gx in range(n_gx):
            for gy in range(n_gy):
                to = target(gx, gy)
                if to is not None and 0 <= to[0] < n_gx and 0 <= to[1] < n_gy:
                    pairs.append((number(gx, gy), number(*to)))
        return lax.ppermute(x, axes, pairs)

    def flip(gx_bits, gy_bits):
        return lambda gx, gy: (gx ^ gx_bits, gy ^ gy_bits)

    def pieces(obj, layer):
        n = PROBE
        return obj[layer, :, :n, :n], obj[layer, :, :, :n], obj[layer, :, :n, n:]

    def bring(corner, edge, low):
        low_a = send(corner, lambda gx, gy: (gx, gy - 1))
        right = send(edge, lambda gx, gy: (gx - 1, gy))
        low_b = send(low, lambda gx, gy: (gx, gy - 1))
        diag = send(corner, lambda gx, gy: (gx - 1, gy - 1) if gx % 2 == 0 else None)
        return right, low_a, low_b, diag

    def bring_side(low_a):
        return send(low_a, lambda gx, gy: (gx - 1, gy) if gx % 2 == 1 else None)

    def take_back(right, low_a, low_b, corner):
        side = send(corner, lambda gx, gy: (gx + 1, gy) if gx % 2 == 0 else None)
        right = send(right, lambda gx, gy: (gx + 1, gy))
        low_b = send(low_b, lambda gx, gy: (gx, gy + 1))
        diag = send(corner, lambda gx, gy: (gx + 1, gy + 1) if gx % 2 == 1 else None)
        low_a = send(low_a + side, lambda gx, gy: (gx, gy + 1))
        return right, low_a, low_b, diag

    def gather_probe(probe):
        return jnp.stack([probe] + [send(probe, flip(4 * k, 0)) for k in (1, 2, 3)])

    def reduce_chip(grad):
        gx = lax.axis_index("gx")
        core, z = gx % 2, gx // 4
        rows = PROBE // n_gx
        parts = jnp.transpose(grad.reshape(2, 2, 4, 2, 2, rows, PROBE), (4, 2, 3, 0, 1, 5, 6))
        keep = jnp.where(core == 0, parts[0], parts[1])
        give = jnp.where(core == 0, parts[1], parts[0])
        return keep + send(give, flip(1, 0))

    def halved(part, bit, there):
        keep = jnp.where(bit == 0, part[0], part[1])
        give = jnp.where(bit == 0, part[1], part[0])
        return keep + send(give, there)

    def halved(part, bit, there):
        keep = jnp.where(bit == 0, part[0], part[1])
        give = jnp.where(bit == 0, part[1], part[0])
        return keep + send(give, there)

    def reduce_z(part):
        z = lax.axis_index("gx") // 4
        part = halved(part.reshape(2, 2, *part.shape[1:]), z // 2, flip(8, 0))
        return halved(part, z % 2, flip(4, 0))

    def reduce_xy(part):
        for bit in (2, 4):
            part = part + send(part, flip(0, bit))
        part = halved(part, lax.axis_index("gx") // 2 % 2, flip(2, 1))
        return part + send(part, flip(0, 1))

    def on_device(obj, probe, positions, counts, amplitudes):
        gx = lax.axis_index("gx").astype(jnp.int32)
        scalars = jnp.concatenate(
            [positions.reshape(2 * SLOTS), counts.reshape(1), jnp.stack([gx & 1, gx >> 1 & 1, gx >> 2])]
        )
        pieces_0, mine = lax.optimization_barrier((cut_first(obj), gather_probe(probe)))
        halo_0 = bring(*pieces_0)
        across = send(mine, flip(2, 1))
        probe_parts = [mine, across, send(mine, flip(1, 0)), send(across, flip(1, 0))]
        obj_late, low_a = lax.optimization_barrier((obj, halo_0[1]))
        halo_0 = (halo_0[0], low_a, *halo_0[2:], bring_side(low_a))
        amp = permute_amplitudes(amplitudes[0, 0], tables)
        pieces_1, halo_0, amp, probe_parts = lax.optimization_barrier((pieces(obj_late, 1), halo_0, amp, probe_parts))
        right, low_a, *others = bring(*pieces_1)
        psi, win, probe_rows = run_out(scalars, obj, halo_0, probe_parts, tables)
        low_a, psi = lax.optimization_barrier((low_a, psi))
        halo_1 = (right, low_a, *others, bring_side(low_a))
        probe_full = probe_rows.reshape(2, 2, PROBE, PROBE)
        g_psi, main_1, *edges_1 = run_far(scalars, obj, halo_1, psi, amp, tables)
        back_1 = take_back(*edges_1)
        used = counts[0, 0] > 0

        def home(operands):
            g_probe, *fields = run_home(*operands, tables)
            return reduce_chip(g_probe), *fields

        def idle(operands):
            return tuple(jnp.zeros(x.shape, x.dtype) for x in jax.eval_shape(home, operands))

        part, main_0, *edges_0 = lax.cond(used, home, idle, (scalars, win, g_psi, probe_full))
        edges_0, part, back_1 = lax.optimization_barrier((edges_0, part, back_1))
        back_0 = take_back(*edges_0)

        def rest(operands):
            part, main, back = operands
            part, grad = lax.optimization_barrier((reduce_z(part), run_join(1, main, back, None)))
            return reduce_xy(part), grad

        def nothing(operands):
            return tuple(jnp.zeros(x.shape, x.dtype) for x in jax.eval_shape(rest, operands))

        probe_grad, grad = lax.cond(used, rest, nothing, (part, main_1, back_1))
        grad = run_join(0, main_0, back_0, grad)
        return grad, probe_grad

    return jax.shard_map(
        on_device,
        mesh=mesh,
        in_specs=(
            P(None, None, "gy", "gx"),
            P(None, None, "gx", None),
            P("gy", "gx", None, None),
            P("gy", "gx"),
            P("gy", "gx", None, None, None),
        ),
        out_specs=(P(None, None, "gy", "gx"), P(None, None, "gx", None)),
        check_vma=False,
    )
```

```python
import functools
import math

import jax
import jax.numpy as jnp
import numpy as np
from jax import lax
from jax.experimental import pallas as pl
from jax.experimental.pallas import tpu as pltpu
from jax.sharding import PartitionSpec as P

BAND = 48
PROBE = 256
HALF = 128
TILE = 512
SLOTS = 6
F32 = jnp.float32
BF16 = jnp.bfloat16
VMEM_LIMIT = 48 * 1024 * 1024


def split_table(mat):
    hi = mat.astype(BF16)
    lo = (mat - hi.astype(np.float64)).astype(BF16)
    return hi, lo


def left_table(mat):
    hi, lo = split_table(mat)
    return np.concatenate([hi, lo, hi], axis=1)


def right_table(mat):
    hi, lo = split_table(mat)
    return np.concatenate([hi, lo, hi], axis=0)


def make_tables():
    index = np.arange(PROBE)
    offset = (index[:, None] - index[None, :]).astype(np.float64)
    prop = np.where(np.abs(offset) <= BAND, np.exp(1j * np.pi * offset**2 / (2 * BAND)), 0)
    prop = prop / math.sqrt(2 * BAND + 1)
    half = np.arange(HALF)
    four = np.exp(-2j * np.pi * ((half[:, None] * half[None, :]) % HALF) / HALF) / math.sqrt(PROBE)
    twist = np.exp(-2j * np.pi * half / PROBE)

    def from_left(mat):
        return np.block([[mat.real, -mat.imag], [mat.imag, mat.real]])

    def from_right(mat):
        return from_left(mat).T

    near = np.arange(PROBE) < HALF
    edge = (np.arange(PROBE) + HALF // 2) // HALF == 1
    cross = np.where(near[:, None] != near[None, :], prop, 0)
    assert not cross[~edge].any() and not cross[:, ~edge].any()

    def pair(table, embed, mat):
        other = np.zeros((HALF, HALF), complex)
        for a in range(HALF):
            for b in range(HALF):
                to, of = (a + HALF, b) if a < HALF // 2 else (a, b + HALF)
                if (b >= HALF // 2) == (a < HALF // 2):
                    other[a, b] = mat[to, of]
        return np.stack([table(embed(mat[:HALF, :HALF])), table(embed(other))])

    order = np.concatenate([np.arange(0, PROBE, 2), np.arange(1, PROBE, 2)])
    perm = np.zeros((PROBE, PROBE))
    perm[np.arange(PROBE), order] = 1
    return {
        "prop_l": pair(left_table, from_left, prop),
        "prop_r": pair(right_table, from_right, prop),
        "back_l": pair(left_table, from_left, prop.conj()),
        "back_r": pair(right_table, from_right, prop.conj()),
        "four_l": left_table(from_left(four)),
        "four_r": right_table(from_right(four)),
        "ruof_l": left_table(from_left(four.conj())),
        "ruof_r": right_table(from_right(four.conj())),
        "tw_row": np.stack(
            [
                np.broadcast_to(twist.real[:, None], (HALF, PROBE)),
                np.broadcast_to(twist.imag[:, None], (HALF, PROBE)),
            ]
        ).astype(np.float32),
        "tw_col": np.stack(
            [
                np.broadcast_to(twist.real[None, :], (8, HALF)),
                np.broadcast_to(twist.imag[None, :], (8, HALF)),
            ]
        ).astype(np.float32),
        "perm_l": np.concatenate([perm] * 3, axis=1).astype(BF16),
        "perm_r": np.concatenate([perm.T] * 3, axis=0).astype(BF16),
    }


def parted(x):
    hi = x.astype(BF16)
    return hi, (x - hi.astype(F32)).astype(BF16)


def lmul(table, x):
    hi, lo = parted(x)
    return jnp.dot(table, jnp.concatenate([hi, hi, lo], axis=0), preferred_element_type=F32)


def rmul(x, table):
    hi, lo = parted(x)
    return jnp.dot(jnp.concatenate([hi, hi, lo], axis=1), table, preferred_element_type=F32)


def exact_parts(x):
    hi = x.astype(BF16)
    rest = x - hi.astype(F32)
    mid = rest.astype(BF16)
    return hi, mid, (rest - mid.astype(F32)).astype(BF16)


def prop_left(re, im, table):
    h, q = HALF, HALF // 2
    x = jnp.concatenate(
        [jnp.concatenate([re[:h], im[:h]], axis=0), jnp.concatenate([re[h:], im[h:]], axis=0)], axis=1
    )
    y = lmul(table[0], x)
    v = lmul(table[1], jnp.concatenate([re[h : h + q], re[q:h], im[h : h + q], im[q:h]], axis=0))
    n = PROBE
    re = [y[:q, :n], y[q:h, :n] + v[q:h], y[:q, n:] + v[:q], y[q:h, n:]]
    im = [y[h : h + q, :n], y[h + q :, :n] + v[h + q :], y[h : h + q, n:] + v[h : h + q], y[h + q :, n:]]
    return jnp.concatenate(re, axis=0), jnp.concatenate(im, axis=0)


def prop_right(re, im, table):
    h, n = HALF, PROBE
    low = lax.broadcasted_iota(jnp.int32, (1, h), 1) < h // 2
    x = jnp.concatenate(
        [jnp.concatenate([re[:, :h], im[:, :h]], axis=1), jnp.concatenate([re[:, h:], im[:, h:]], axis=1)], axis=0
    )
    y = rmul(x, table[0])
    u = [jnp.where(low, z[:, h:], z[:, :h]) for z in (re, im)]
    v = rmul(jnp.concatenate(u, axis=1), table[1])
    out = []
    for at in (slice(0, h), slice(h, n)):
        out.append(
            jnp.concatenate(
                [y[:n, at] + jnp.where(low, 0.0, v[:, at]), y[n:, at] + jnp.where(low, v[:, at], 0.0)], axis=1
            )
        )
    return out


def place_of(scalars, slot):
    row = scalars[2 * slot]
    col = scalars[2 * slot + 1]
    row_base = pl.multiple_of(row // 8 * 8, 8)
    col_base = pl.multiple_of(col // 128 * 128, 128)
    return row_base, row - row_base, col_base, col - col_base


def window_of(field, part, place):
    row_base, row_off, col_base, col_off = place
    x = field[part, pl.ds(row_base, PROBE + 8), pl.ds(col_base, PROBE + 128)]
    x = pltpu.roll(x, (PROBE + 128 - col_off) % (PROBE + 128), 1)[:, :PROBE]
    return pltpu.roll(x, (PROBE + 8 - row_off) % (PROBE + 8), 0)[:PROBE]


def add_window(field, part, place, x):
    row_base, row_off, col_base, col_off = place
    x = jnp.concatenate([x, jnp.zeros((8, PROBE), F32)], axis=0)
    x = pltpu.roll(x, row_off, 0)
    x = jnp.concatenate([x, jnp.zeros((PROBE + 8, 128), F32)], axis=1)
    x = pltpu.roll(x, col_off, 1)
    at = (part, pl.ds(row_base, PROBE + 8), pl.ds(col_base, PROBE + 128))
    field[at] = field[at] + x


def fetch_field(layer, core, obj, right, low_a, low_b, diag, side, field, sems, meanwhile=None):
    n, t = PROBE, TILE
    copies = [
        pltpu.make_async_copy(obj.at[layer], field.at[:, :t, :t], sems.at[0]),
        pltpu.make_async_copy(right, field.at[:, :t, t:], sems.at[1]),
        pltpu.make_async_copy(low_a, field.at[:, t:, :n], sems.at[2]),
        pltpu.make_async_copy(low_b, field.at[:, t:, n:t], sems.at[3]),
    ]
    for copy in copies:
        copy.start()
    if meanwhile is not None:
        meanwhile()

    @pl.when(core == 0)
    def _():
        copy = pltpu.make_async_copy(side, field.at[:, t:, t:], sems.at[4])
        copy.start()
        copy.wait()

    @pl.when(core != 0)
    def _():
        copy = pltpu.make_async_copy(diag, field.at[:, t:, t:], sems.at[4])
        copy.start()
        copy.wait()

    for copy in copies:
        copy.wait()


def store_field(field, main, right, low_a, low_b, corner, sems):
    n, t = PROBE, TILE
    copies = [
        pltpu.make_async_copy(field.at[:, :t, t:], right, sems.at[0]),
        pltpu.make_async_copy(field.at[:, t:, n:t], low_b, sems.at[1]),
        pltpu.make_async_copy(field.at[:, t:, :n], low_a, sems.at[2]),
        pltpu.make_async_copy(field.at[:, t:, t:], corner, sems.at[3]),
        pltpu.make_async_copy(field.at[:, :t, :t], main, sems.at[4]),
    ]
    for copy in copies:
        copy.start()
    for copy in copies:
        copy.wait()


def amp_kernel(amp, perm_l, perm_r, out):
    hi, mid, lo = exact_parts(amp[0])
    y = jnp.dot(perm_l[...], jnp.concatenate([hi, mid, lo], axis=0), preferred_element_type=F32)
    hi, mid, lo = exact_parts(y)
    out[0] = jnp.dot(jnp.concatenate([hi, mid, lo], axis=1), perm_r[...], preferred_element_type=F32)


def out_kernel(
    scalars, obj, right, low_a, low_b, diag, side, mine, across, mine_other, across_other, table_l, table_r,
    psi, win, probe_rows, field, sems, probe_sem,
):
    slot = pl.program_id(0)
    probe = probe_rows.reshape(2, 2, PROBE, PROBE)

    @pl.when(slot == 0)
    def _():
        core, y_hi, z = scalars[13], scalars[14], scalars[15]
        copies = [
            pltpu.make_async_copy(src.at[k], probe_rows.at[:, :, z ^ k, y, c], probe_sem)
            for src, y, c in (
                (mine, y_hi, core),
                (across, 1 - y_hi, core),
                (mine_other, y_hi, 1 - core),
                (across_other, 1 - y_hi, 1 - core),
            )
            for k in range(4)
        ]
        for copy in copies:
            copy.start()
        fetch_field(0, core, obj, right, low_a, low_b, diag, side, field, sems)
        for copy in copies:
            copy.wait()

    @pl.when(slot < scalars[12])
    def _():
        place = place_of(scalars, slot)
        w_re = window_of(field, 0, place)
        w_im = window_of(field, 1, place)
        win[0, 0] = w_re
        win[0, 1] = w_im
        x = []
        for m in (0, 1):
            re = probe[m, 0] * w_re - probe[m, 1] * w_im
            im = probe[m, 0] * w_im + probe[m, 1] * w_re
            x.append(prop_left(re, im, table_l))
        for m in (0, 1):
            re, im = prop_right(*x[m], table_r)
            psi[0, m, 0] = re
            psi[0, m, 1] = im


def far_kernel(
    scalars, obj, right, low_a, low_b, diag, side, psi, amp, four_l, four_r, ruof_l, ruof_r, tw_row, tw_col,
    g_psi, g_main, g_right, g_low_a, g_low_b, g_corner, field, grad, win, gwin, sems,
):
    slot = pl.program_id(0)
    h, n = HALF, PROBE
    used = scalars[12]

    def load_window(at):
        place = place_of(scalars, at)
        win[0] = window_of(field, 0, place)
        win[1] = window_of(field, 1, place)

    def flush(at):
        place = place_of(scalars, at)
        add_window(grad, 0, place, gwin[0])
        add_window(grad, 1, place, gwin[1])

    @pl.when(slot == 0)
    def _():
        def clear():
            grad[...] = jnp.zeros_like(grad)
            gwin[...] = jnp.zeros_like(gwin)

        fetch_field(1, scalars[13], obj, right, low_a, low_b, diag, side, field, sems, clear)
        load_window(0)

    @pl.when(slot < used)
    def _():
        w_re, w_im = win[0], win[1]
        tr, ti = tw_row[0], tw_row[1]
        cr, ci = tw_col[0, 0:1], tw_col[1, 0:1]
        chi = {}

        def left(m, odd):
            if m not in chi:
                p_re, p_im = psi[0, m, 0], psi[0, m, 1]
                chi[m] = (p_re * w_re - p_im * w_im, p_re * w_im + p_im * w_re)
            re, im = chi[m]
            if odd:
                d_re, d_im = re[:h] - re[h:], im[:h] - im[h:]
                x = [d_re * tr - d_im * ti, d_re * ti + d_im * tr]
            else:
                x = [re[:h] + re[h:], im[:h] + im[h:]]
            return lmul(four_l[...], jnp.concatenate(x, axis=0))

        def across(y):
            re, im = y[:h], y[h:]
            d_re, d_im = re[:, :h] - re[:, h:], im[:, :h] - im[:, h:]
            even = jnp.concatenate([re[:, :h] + re[:, h:], im[:, :h] + im[:, h:]], axis=1)
            odd = jnp.concatenate([d_re * cr - d_im * ci, d_re * ci + d_im * cr], axis=1)
            return rmul(jnp.concatenate([even, odd], axis=0), four_r[...])

        def slope_of(z0, z1, rows):
            sq = z0 * z0 + z1 * z1
            total = sq[:, :h] + sq[:, h:] + 1.0
            both = jnp.concatenate([amp[0, rows, :h], amp[0, rows, h:]], axis=0)
            slope = 2.0 - 2.0 * both * lax.rsqrt(total)
            return jnp.concatenate([slope, slope], axis=1)

        def back_across(z):
            y = rmul(z, ruof_r[...])
            q_re = y[h:, :h] * cr + y[h:, h:] * ci
            q_im = y[h:, h:] * cr - y[h:, :h] * ci
            re = jnp.concatenate([y[:h, :h] + q_re, y[:h, :h] - q_re], axis=1)
            im = jnp.concatenate([y[:h, h:] + q_im, y[:h, h:] - q_im], axis=1)
            return jnp.concatenate([re, im], axis=0)

        def finish(m, y_even, y_odd):
            q_re = y_odd[:h] * tr + y_odd[h:] * ti
            q_im = y_odd[h:] * tr - y_odd[:h] * ti
            re = jnp.concatenate([y_even[:h] + q_re, y_even[:h] - q_re], axis=0)
            im = jnp.concatenate([y_even[h:] + q_im, y_even[h:] - q_im], axis=0)
            g_psi[0, m, 0] = w_re * re + w_im * im
            g_psi[0, m, 1] = w_re * im - w_im * re
            p_re, p_im = psi[0, m, 0], psi[0, m, 1]
            return p_re * re + p_im * im, p_re * im - p_im * re

        back = ruof_l[...]
        l0e = left(0, 0)
        l1e = left(1, 0)
        l0o = left(0, 1)
        z0e = across(l0e)
        l1o = left(1, 1)
        z1e = across(l1e)
        slope_e = slope_of(z0e, z1e, slice(0, h))
        z0o = across(l0o)
        b0e = back_across(z0e * slope_e)
        z1o = across(l1o)
        flush(jnp.maximum(slot - 1, 0))
        slope_o = slope_of(z0o, z1o, slice(h, n))
        load_window(jnp.minimum(slot + 1, SLOTS - 1))
        b1e = back_across(z1e * slope_e)
        a0e = lmul(back, b0e)
        b0o = back_across(z0o * slope_o)
        a1e = lmul(back, b1e)
        b1o = back_across(z1o * slope_o)
        a0o = lmul(back, b0o)
        a1o = lmul(back, b1o)
        u_re, u_im = finish(0, a0e, a0o)
        v_re, v_im = finish(1, a1e, a1o)
        gwin[0] = u_re + v_re
        gwin[1] = u_im + v_im

    @pl.when(slot == pl.num_programs(0) - 1)
    def _():
        flush(used - 1)
        store_field(grad, g_main, g_right, g_low_a, g_low_b, g_corner, sems)


def home_kernel(
    scalars, win, g_psi, probe, table_l, table_r,
    g_probe, g_main, g_right, g_low_a, g_low_b, g_corner, grad, sems,
):
    slot = pl.program_id(0)

    @pl.when(slot == 0)
    def _():
        grad[...] = jnp.zeros_like(grad)
        g_probe[...] = jnp.zeros_like(g_probe)

    @pl.when(slot < scalars[12])
    def _():
        place = place_of(scalars, slot)
        x = [prop_left(g_psi[0, m, 0], g_psi[0, m, 1], table_l) for m in (0, 1)]
        w_re, w_im = win[0, 0], win[0, 1]
        gw_re = gw_im = None
        for m in (0, 1):
            re, im = prop_right(*x[m], table_r)
            p_re, p_im = probe[m, 0], probe[m, 1]
            a_re = p_re * re + p_im * im
            a_im = p_re * im - p_im * re
            gw_re = a_re if m == 0 else gw_re + a_re
            gw_im = a_im if m == 0 else gw_im + a_im
            g_probe[m, 0] += w_re * re + w_im * im
            g_probe[m, 1] += w_re * im - w_im * re
        add_window(grad, 0, place, gw_re)
        add_window(grad, 1, place, gw_im)

    @pl.when(slot == pl.num_programs(0) - 1)
    def _():
        store_field(grad, g_main, g_right, g_low_a, g_low_b, g_corner, sems)


def join_kernel(main, right, low_a, low_b, diag, *rest):
    out = rest[-1]
    n = PROBE
    i = pl.program_id(0)

    @pl.when(i < 1)
    def _():
        out[0, :, :, :n] = main[:, :, :n] + right[...] + low_a[...] + diag[...]
        out[0, :, :, n:] = main[:, :, n:] + low_b[...]

    @pl.when(i >= 1)
    def _():
        out[0, :, :, :n] = main[:, :, :n] + right[...]
        out[0, :, :, n:] = main[:, :, n:]


def whole(shape):
    return pl.BlockSpec(shape, lambda j, s: (0,) * len(shape))


def held():
    return pl.BlockSpec(memory_space=pltpu.VMEM)


def any_spec():
    return pl.BlockSpec(memory_space=pl.ANY)


def of_slot(shape):
    return pl.BlockSpec(
        (1,) + shape, lambda j, s: (jnp.minimum(j, s[12] - 1),) + (0,) * len(shape)
    )


def cost(flops, data):
    return pl.CostEstimate(flops=int(flops), bytes_accessed=int(data), transcendentals=0)


def params():
    return pltpu.CompilerParams(vmem_limit_bytes=VMEM_LIMIT)


FIELD_PARTS = [(2, TILE, TILE), (2, TILE, PROBE), (2, PROBE, PROBE), (2, PROBE, PROBE), (2, PROBE, PROBE)]


def sds(shape):
    return jax.ShapeDtypeStruct(shape, F32)


def permute_amplitudes(amp, tables):
    n = PROBE
    return pl.pallas_call(
        amp_kernel,
        grid=(SLOTS,),
        in_specs=[
            pl.BlockSpec((1, n, n), lambda j: (j, 0, 0)),
            pl.BlockSpec((n, 3 * n), lambda j: (0, 0)),
            pl.BlockSpec((3 * n, n), lambda j: (0, 0)),
        ],
        out_specs=pl.BlockSpec((1, n, n), lambda j: (j, 0, 0)),
        out_shape=sds((SLOTS, n, n)),
        compiler_params=params(),
        cost_estimate=cost(1.2e9, 4e6),
        name="order_amplitudes",
    )(amp, tables["perm_l"], tables["perm_r"])


def run_out(scalars, obj, halo, probe, tables):
    n = PROBE
    return pl.pallas_call(
        out_kernel,
        grid_spec=pltpu.PrefetchScalarGridSpec(
            num_scalar_prefetch=1,
            grid=(SLOTS,),
            in_specs=[any_spec()] * 10 + [held()] * 2,
            out_specs=[of_slot((2, 2, n, n)), of_slot((2, n, n)), whole((2, 2, 4, 2, 2, 16, n))],
            scratch_shapes=[
                pltpu.VMEM((2, 3 * n, 3 * n), F32),
                pltpu.SemaphoreType.DMA((5,)),
                pltpu.SemaphoreType.DMA,
            ],
        ),
        out_shape=[sds((SLOTS, 2, 2, n, n)), sds((SLOTS, 2, n, n)), sds((2, 2, 4, 2, 2, 16, n))],
        compiler_params=params(),
        cost_estimate=cost(6e10, 2e7),
        name="propagate_out",
    )(scalars, obj, *halo, *probe, tables["prop_l"], tables["prop_r"])


def run_far(scalars, obj, halo, psi, amp, tables):
    n = PROBE
    return pl.pallas_call(
        far_kernel,
        grid_spec=pltpu.PrefetchScalarGridSpec(
            num_scalar_prefetch=1,
            grid=(SLOTS,),
            in_specs=[any_spec()] * 6
            + [of_slot((2, 2, n, n)), of_slot((n, n))]
            + [held()] * 6,
            out_specs=[of_slot((2, 2, n, n))] + [any_spec()] * 5,
            scratch_shapes=[
                pltpu.VMEM((2, 3 * n, 3 * n), F32),
                pltpu.VMEM((2, 3 * n, 3 * n), F32),
                pltpu.VMEM((2, n, n), F32),
                pltpu.VMEM((2, n, n), F32),
                pltpu.SemaphoreType.DMA((5,)),
            ],
        ),
        out_shape=[sds((SLOTS, 2, 2, n, n))] + [sds(s) for s in FIELD_PARTS],
        compiler_params=params(),
        cost_estimate=cost(6e10, 2e7),
        name="far_field",
    )(
        scalars, obj, *halo, psi, amp,
        tables["four_l"], tables["four_r"], tables["ruof_l"], tables["ruof_r"],
        tables["tw_row"], tables["tw_col"],
    )


def run_home(scalars, win, g_psi, probe, tables):
    n = PROBE
    return pl.pallas_call(
        home_kernel,
        grid_spec=pltpu.PrefetchScalarGridSpec(
            num_scalar_prefetch=1,
            grid=(SLOTS,),
            in_specs=[
                of_slot((2, n, n)),
                of_slot((2, 2, n, n)),
                held(),
                held(),
                held(),
            ],
            out_specs=[whole((2, 2, n, n))] + [any_spec()] * 5,
            scratch_shapes=[pltpu.VMEM((2, 3 * n, 3 * n), F32), pltpu.SemaphoreType.DMA((5,))],
        ),
        out_shape=[sds((2, 2, n, n))] + [sds(s) for s in FIELD_PARTS],
        compiler_params=params(),
        cost_estimate=cost(6e10, 2e7),
        name="propagate_home",
    )(scalars, win, g_psi, probe, tables["back_l"], tables["back_r"])


def run_join(layer, main, arrived, into):
    n, h = PROBE, PROBE
    top = lambda i: (0, 0, 0)
    extra = [] if into is None else [into]
    return pl.pallas_call(
        join_kernel,
        grid=(2,),
        in_specs=[
            pl.BlockSpec((2, h, TILE), lambda i: (0, i, 0)),
            pl.BlockSpec((2, h, n), lambda i: (0, i, 0)),
            pl.BlockSpec((2, h, n), top),
            pl.BlockSpec((2, h, n), top),
            pl.BlockSpec((2, h, n), top),
        ]
        + [pl.BlockSpec(memory_space=pl.ANY)] * len(extra),
        out_specs=pl.BlockSpec((1, 2, h, TILE), lambda i: (layer, 0, i, 0)),
        out_shape=sds((2, 2, TILE, TILE)),
        input_output_aliases={} if into is None else {5: 0},
        compiler_params=params(),
        cost_estimate=cost(1e6, 6e6),
        name="join_gradients",
    )(main, *arrived, *extra)


def solution(mesh):
    n_gx, n_gy = mesh.shape["gx"], mesh.shape["gy"]
    axes = tuple(mesh.axis_names)
    tables = make_tables()

    def number(gx, gy):
        return gx * n_gy + gy if axes == ("gx", "gy") else gy * n_gx + gx

    def send(x, target):
        pairs = []
        for gx in range(n_gx):
            for gy in range(n_gy):
                to = target(gx, gy)
                if to is not None and 0 <= to[0] < n_gx and 0 <= to[1] < n_gy:
                    pairs.append((number(gx, gy), number(*to)))
        return lax.ppermute(x, axes, pairs)

    def flip(gx_bits, gy_bits):
        return lambda gx, gy: (gx ^ gx_bits, gy ^ gy_bits)

    def pieces(obj, layer):
        n = PROBE
        return obj[layer, :, :n, :n], obj[layer, :, :, :n], obj[layer, :, :n, n:]

    def bring(corner, edge, low):
        low_a = send(corner, lambda gx, gy: (gx, gy - 1))
        right = send(edge, lambda gx, gy: (gx - 1, gy))
        low_b = send(low, lambda gx, gy: (gx, gy - 1))
        diag = send(corner, lambda gx, gy: (gx - 1, gy - 1) if gx % 2 == 0 else None)
        return right, low_a, low_b, diag

    def bring_side(low_a):
        return send(low_a, lambda gx, gy: (gx - 1, gy) if gx % 2 == 1 else None)

    def take_back(right, low_a, low_b, corner):
        side = send(corner, lambda gx, gy: (gx + 1, gy) if gx % 2 == 0 else None)
        right = send(right, lambda gx, gy: (gx + 1, gy))
        low_b = send(low_b, lambda gx, gy: (gx, gy + 1))
        diag = send(corner, lambda gx, gy: (gx + 1, gy + 1) if gx % 2 == 1 else None)
        low_a = send(low_a + side, lambda gx, gy: (gx, gy + 1))
        return right, low_a, low_b, diag

    def gather_probe(probe):
        return jnp.stack([probe] + [send(probe, flip(4 * k, 0)) for k in (1, 2, 3)])

    def reduce_chip(grad):
        gx = lax.axis_index("gx")
        core, z = gx % 2, gx // 4
        rows = PROBE // n_gx
        parts = jnp.transpose(grad.reshape(2, 2, 4, 2, 2, rows, PROBE), (4, 2, 3, 0, 1, 5, 6))
        keep = jnp.where(core == 0, parts[0], parts[1])
        give = jnp.where(core == 0, parts[1], parts[0])
        return keep + send(give, flip(1, 0))

    def halved(part, bit, there):
        keep = jnp.where(bit == 0, part[0], part[1])
        give = jnp.where(bit == 0, part[1], part[0])
        return keep + send(give, there)

    def halved(part, bit, there):
        keep = jnp.where(bit == 0, part[0], part[1])
        give = jnp.where(bit == 0, part[1], part[0])
        return keep + send(give, there)

    def reduce_z(part):
        z = lax.axis_index("gx") // 4
        part = halved(part.reshape(2, 2, *part.shape[1:]), z // 2, flip(8, 0))
        return halved(part, z % 2, flip(4, 0))

    def reduce_xy(part):
        for bit in (2, 4):
            part = part + send(part, flip(0, bit))
        part = halved(part, lax.axis_index("gx") // 2 % 2, flip(2, 1))
        return part + send(part, flip(0, 1))

    def on_device(obj, probe, positions, counts, amplitudes):
        gx = lax.axis_index("gx").astype(jnp.int32)
        scalars = jnp.concatenate(
            [positions.reshape(2 * SLOTS), counts.reshape(1), jnp.stack([gx & 1, gx >> 1 & 1, gx >> 2])]
        )
        pieces_0, mine = lax.optimization_barrier((pieces(obj, 0), gather_probe(probe)))
        halo_0 = bring(*pieces_0)
        across = send(mine, flip(2, 1))
        probe_parts = [mine, across, send(mine, flip(1, 0)), send(across, flip(1, 0))]
        obj_late, low_a = lax.optimization_barrier((obj, halo_0[1]))
        halo_0 = (halo_0[0], low_a, *halo_0[2:], bring_side(low_a))
        amp = permute_amplitudes(amplitudes[0, 0], tables)
        pieces_1, halo_0, amp, probe_parts = lax.optimization_barrier((pieces(obj_late, 1), halo_0, amp, probe_parts))
        right, low_a, *others = bring(*pieces_1)
        psi, win, probe_rows = run_out(scalars, obj, halo_0, probe_parts, tables)
        low_a, psi = lax.optimization_barrier((low_a, psi))
        halo_1 = (right, low_a, *others, bring_side(low_a))
        probe_full = probe_rows.reshape(2, 2, PROBE, PROBE)
        g_psi, main_1, *edges_1 = run_far(scalars, obj, halo_1, psi, amp, tables)
        back_1 = take_back(*edges_1)
        used = counts[0, 0] > 0

        def home(operands):
            g_probe, *fields = run_home(*operands, tables)
            return reduce_chip(g_probe), *fields

        def idle(operands):
            return tuple(jnp.zeros(x.shape, x.dtype) for x in jax.eval_shape(home, operands))

        part, main_0, *edges_0 = lax.cond(used, home, idle, (scalars, win, g_psi, probe_full))
        edges_0, part, back_1 = lax.optimization_barrier((edges_0, part, back_1))
        back_0 = take_back(*edges_0)

        def rest(operands):
            part, main, back = operands
            part, grad = lax.optimization_barrier((reduce_z(part), run_join(1, main, back, None)))
            return reduce_xy(part), grad

        def nothing(operands):
            return tuple(jnp.zeros(x.shape, x.dtype) for x in jax.eval_shape(rest, operands))

        probe_grad, grad = lax.cond(used, rest, nothing, (part, main_1, back_1))
        grad = run_join(0, main_0, back_0, grad)
        return grad, probe_grad

    return jax.shard_map(
        on_device,
        mesh=mesh,
        in_specs=(
            P(None, None, "gy", "gx"),
            P(None, None, "gx", None),
            P("gy", "gx", None, None),
            P("gy", "gx"),
            P("gy", "gx", None, None, None),
        ),
        out_specs=(P(None, None, "gy", "gx"), P(None, None, "gx", None)),
        check_vma=False,
    )
```
